256 devices in a mesh: gx: 32 (over y, z), gy: 8 (over x, core).
Axes of the slice: x: 4, y: 4, z: 8, core: 2. Of those that a mesh axis runs over, the one named last changes fastest.
Arguments:
- right_side: float32 [512, 256, 128], P('gx', 'gy'), may hold values from -160 to 160
- beta: float32 [512, 256, 128], P('gx', 'gy'), may hold values from 1 to 10
- shift: float32 [512, 256, 128], P('gx', 'gy'), may hold values from 0.5 to 4
Outputs:
- corrected: float32 [512, 256, 128], P('gx', 'gy')
- middle: float32 [256, 128, 64], P('gx', 'gy')
The draws below stay inside these ranges and needn't reach their ends.
All inputs are finite; a program needn't handle non-finite values.
Results may differ from the reference program's by a relative error of at most 0.00002.
Values sent between devices are 32-bit elements; how exact they have to be, the bound alone decides.
No kernel may reach another device: no remote copies, remote signals or barrier semaphores. Data moves between devices by JAX's collectives and lax.ppermute only.
A program may use at most 128 MiB of HBM per device.

```python
import math
import jax
import jax.numpy as jnp

CZ = 128
SWEEPS = 4
NX = 512
NY = 256


def block_levels(key, shape, cuts, least, top_value):
    def one(axis_at, shards_of):
        steps = jax.random.uniform(jax.random.fold_in(jax.random.fold_in(key, 6), axis_at), (shards_of,), jnp.float32, least / len(cuts), top_value / len(cuts))
        return jnp.repeat(jnp.exp(steps), shape[axis_at] // shards_of).reshape((-1,) + (1,) * (len(shape) - axis_at - 1))

    gain = one(*cuts[0])
    for cut in cuts[1:]:
        gain = gain * one(*cut)
    return gain


def scatter_about(stream_key, extent, scale, reach, split=(), kind=jnp.bfloat16):
    entries = scale * jax.random.normal(stream_key, extent, jnp.float32)
    if split:
        entries = entries * block_levels(stream_key, extent, split, -0.22, 0.18)
    return jnp.clip(entries, -reach, reach).astype(kind)


def setup_inputs(seed: int = 0) -> dict:
    streams_of = jax.random.split(jax.random.key(seed), 4)
    right_side = scatter_about(streams_of[0], (NX, NY, CZ), 20.0, 160.0, ((0, 32), (1, 8)), jnp.float32)
    beta = jnp.clip(jnp.exp(math.log(10.0) - 2.3025851 * jax.random.uniform(streams_of[1], (NX, NY, CZ), jnp.float32) ** block_levels(streams_of[1], (NX, NY, CZ), ((0, 32), (1, 8)), -0.2, 0.2)), 1.0, 10.0)
    shift = jnp.clip(jnp.exp(math.log(4.0) - 2.0794415 * jax.random.uniform(streams_of[2], (NX, NY, CZ), jnp.float32) ** block_levels(streams_of[2], (NX, NY, CZ), ((0, 32), (1, 8)), -0.2, 0.2)), 0.5, 4.0)
    return {"right_side": right_side, "beta": beta, "shift": shift}


def restrict(field):
    nx, ny, nz = field.shape
    return field.reshape(nx // 2, 2, ny // 2, 2, nz // 2, 2).mean(axis=(1, 3, 5))


def prolong(field):
    return jnp.repeat(jnp.repeat(jnp.repeat(field, 2, 0), 2, 1), 2, 2)


def neighbours(padded):
    return [padded[2:, 1:-1, 1:-1], padded[:-2, 1:-1, 1:-1], padded[1:-1, 2:, 1:-1],
            padded[1:-1, :-2, 1:-1], padded[1:-1, 1:-1, 2:], padded[1:-1, 1:-1, :-2]]


def make_level(beta_l, shift_l, scale):
    weights = [0.5 * (beta_l + other) for other in neighbours(jnp.pad(beta_l, 1))]
    total = weights[0] + weights[1] + weights[2] + weights[3] + weights[4] + weights[5]
    inv_diag = 1.0 / (shift_l + scale * total)

    def apply_op(field):
        others = neighbours(jnp.pad(field, 1))
        acc = weights[0] * (field - others[0])
        for index in range(1, 6):
            acc = acc + weights[index] * (field - others[index])
        return shift_l * field + scale * acc
    return apply_op, inv_diag


def chebyshev(rhs, apply_op, inv_diag):
    theta, delta = 1.15, 0.85
    sigma = theta / delta
    rho_old = 1.0 / sigma
    step_dir = rhs * inv_diag / theta
    field = step_dir
    for sweep in range(SWEEPS - 1):
        resid = rhs - apply_op(field)
        rho_new = 1.0 / (2.0 * sigma - rho_old)
        step_dir = rho_new * rho_old * step_dir + (2.0 * rho_new / delta) * resid * inv_diag
        field = field + step_dir
        rho_old = rho_new
    return field


def reference(right_side, beta, shift):
    apply_fine, inv_fine = make_level(beta, shift, 1.0)
    x_fine = chebyshev(right_side, apply_fine, inv_fine)
    rhs_mid = restrict(right_side - apply_fine(x_fine))
    beta_mid, shift_mid = restrict(beta), restrict(shift)
    apply_mid, inv_mid = make_level(beta_mid, shift_mid, 0.25)
    x_mid = chebyshev(rhs_mid, apply_mid, inv_mid)
    rhs_low = restrict(rhs_mid - apply_mid(x_mid))
    apply_low, inv_low = make_level(restrict(beta_mid), restrict(shift_mid), 0.0625)
    x_low = chebyshev(rhs_low, apply_low, inv_low)
    middle = x_mid + prolong(x_low)
    corrected = x_fine + prolong(middle)
    return corrected, middle
```

```python
import functools

import jax
import jax.numpy as jnp
from jax import lax
from jax.experimental import pallas as pl
from jax.experimental.pallas import tpu as pltpu
from jax.sharding import PartitionSpec as P

SWEEPS = 4
THETA, DELTA = 1.15, 0.85
SIGMA = THETA / DELTA
F32 = jnp.float32


def coefficients():
    rho, out = 1.0 / SIGMA, []
    for _ in range(SWEEPS - 1):
        new = 1.0 / (2.0 * SIGMA - rho)
        out.append((new * rho, 2.0 * new / DELTA))
        rho = new
    return out


def lanes(rows):
    return lax.broadcasted_iota(jnp.int32, (rows, 128), 1)


def roll(value, shift):
    return pltpu.roll(value, shift % 128, 1)


def build(depth, planes, rows, rep, scale, beta, rhs, shift, work):
    wx, wy, wym, wz, wzm, diag, inv, rhs_n, start = work
    lane = lanes(rows)
    first, last = lane < rep, lane >= 128 - rep
    half = 0.5 * scale
    dom = pl.ds(8, rows)
    prev, cur = beta[0, dom, :], beta[1, dom, :]
    wx_prev = half * (prev + cur)
    for i in range(planes):
        nxt = beta[i + 2, dom, :]
        wx_next = half * (cur + nxt)
        w_up = half * (cur + beta[i + 1, pl.ds(9, rows), :])
        w_down = half * (cur + beta[i + 1, pl.ds(7, rows), :])
        w_right = half * (cur + jnp.where(last, 0.0, roll(cur, -rep)))
        w_left = half * (cur + jnp.where(first, 0.0, roll(cur, rep)))
        d = shift(i) + (wx_prev + wx_next + w_up + w_down + w_right + w_left)
        iv = jnp.where(cur > 0.0, 1.0 / d, 0.0)
        c = rhs(i) * iv
        wx[i] = wx_next
        wy[i] = w_up
        wym[i] = w_down
        wz[i] = jnp.where(last, 0.0, w_right)
        wzm[i] = jnp.where(first, 0.0, w_left)
        diag[i] = d
        inv[i] = iv
        rhs_n[i] = c
        start[i, dom, :] = c * (1.0 / THETA)
        cur, wx_prev = nxt, wx_next


def scaled_residual(src, lo, hi, rows, rep, work, emit):
    wx, wy, wym, wz, wzm, _, inv, rhs_n, _ = work
    dom = pl.ds(8, rows)
    prev, cur, wx_prev = src[lo - 1, dom, :], src[lo, dom, :], wx[lo - 1]
    for i in range(lo, hi):
        nxt, wx_next = src[i + 1, dom, :], wx[i]
        t = wx_next * nxt + wx_prev * prev
        t = t + wy[i] * src[i, pl.ds(9, rows), :] + wym[i] * src[i, pl.ds(7, rows), :]
        t = t + wz[i] * roll(cur, -rep) + wzm[i] * roll(cur, rep)
        emit(i, cur, rhs_n[i] + inv[i] * t - cur)
        prev, cur, wx_prev = cur, nxt, wx_next


def smooth(planes, rows, rep, work, other, step):
    src, dst = work[8], other
    for k, (a, g) in enumerate(coefficients()):

        def emit(i, cur, e, a=a, g=g, k=k, dst=dst):
            before = cur if k == 0 else step[i]
            d = a * before + g * e
            if k < SWEEPS - 2:
                step[i] = d
            dst[i, pl.ds(8, rows), :] = cur + d

        scaled_residual(src, k + 1, planes - k - 1, rows, rep, work, emit)
        src, dst = dst, src
    return src


def flags():
    ix, iy = lax.axis_index("gx"), lax.axis_index("gy")
    nx, ny = lax.axis_size("gx"), lax.axis_size("gy")
    one = lambda c: jnp.where(c, 1.0, 0.0).astype(F32)
    near = (one(ix > 0), one(ix < nx - 1))
    far = (one(ix > 1), one(ix < nx - 2))
    return near, far, (one(iy > 0), one(iy < ny - 1))


def pack_fine_y(b, beta, shift, left, right, first, last):
    for x in range(-4, 20):
        if x < 0:
            pb, ps = left[x + 4], left[x + 13]
        elif x < 16:
            pb, ps = b[x], shift[x]
        else:
            pb, ps = right[x - 16], right[x - 7]
        first[x + 4, 0:4, :] = pb[0:4]
        first[x + 4, 4:8, :] = ps[0:4]
        last[x + 4, 0:4, :] = pb[28:32]
        last[x + 4, 4:8, :] = ps[28:32]
    for x in range(-5, 21):
        p = left[x + 9] if x < 0 else beta[x] if x < 16 else right[x - 12]
        first[x + 29, 0:5, :] = p[0:5]
        first[x + 29, 5:8, :] = p[0:3]
        last[x + 29, 0:5, :] = p[27:32]
        last[x + 29, 5:8, :] = p[0:3]


def fine_kernel(
    b, beta, shift, left, right, down, up, x_out, packed,
    be, bb, ss, wx, wy, wym, wz, wzm, diag, inv, rhs_n, xa, xb, step, pair,
):
    near, _, sides = flags()
    for x in range(-5, 21):
        if x < 0:
            own, f = left[x + 9] * near[0], near[0]
        elif x < 16:
            own, f = beta[x], None
        else:
            own, f = right[x - 12] * near[1], near[1]
        lo, hi = down[x + 29, 0:5, :] * sides[0], up[x + 29, 0:5, :] * sides[1]
        if f is not None:
            lo, hi = lo * f, hi * f
        be[x + 5, 12:44, :] = own
        be[x + 5, 7:12, :] = lo
        be[x + 5, 44:49, :] = hi
    for x in range(-4, 20):
        if x < 0:
            pb, ps = left[x + 4], left[x + 13]
        elif x < 16:
            pb, ps = b[x], shift[x]
        else:
            pb, ps = right[x - 16], right[x - 7]
        for dst, own, at in ((bb, pb, 0), (ss, ps, 4)):
            dst[x + 4, 4:36, :] = own
            dst[x + 4, 0:4, :] = down[x + 4, at:at + 4, :]
            dst[x + 4, 36:40, :] = up[x + 4, at:at + 4, :]
    work = (wx, wy, wym, wz, wzm, diag, inv, rhs_n, xa)
    build(4, 24, 40, 1, 1.0, be, lambda i: bb[i], lambda i: ss[i], work)
    x = smooth(24, 40, 1, work, xb, step)

    even = lanes(8) % 2 == 0

    def pack(field, m, plane, start):
        e = pair[plane, pl.ds(start, 8, 4), :] + pair[plane, pl.ds(start + 1, 8, 4), :]
        o = pair[plane, pl.ds(start + 2, 8, 4), :] + pair[plane, pl.ds(start + 3, 8, 4), :]
        packed[field, m] = jnp.where(even, e + roll(e, -1), o + roll(o, 1)) * 0.125

    for m in range(8):
        pair[m, 0:32, :] = beta[2 * m] + beta[2 * m + 1]
        pair[m + 8, 0:32, :] = shift[2 * m] + shift[2 * m + 1]
    for m in range(8):
        pack(1, m, m, 0)
        pack(2, m, m + 8, 0)
    held = {}

    def emit(i, cur, e):
        r = e * diag[i]
        if i % 2 == 0:
            held[0] = r
        else:
            pair[16 + (i - 4) // 2] = held[0] + r

    scaled_residual(x, 4, 20, 40, 1, work, emit)
    for m in range(8):
        pack(0, m, m + 16, 4)
    for i in range(16):
        x_out[i] = x[i + 4, pl.ds(12, 32), :]


def mid_plane(field, x, own, left, right, left2, right2):
    at = (0, 2, 5)[field]
    if x < -8:
        return left2[at + x + (10, 11, 10)[field]]
    if x < 0:
        return left[field, x + 8]
    if x < 8:
        return own[field, x]
    if x < 16:
        return right[field, x - 8]
    return right2[at + x - 16]


def pack_mid_y(own, left, right, left2, right2, first, last):
    for x in range(-11, 19):
        for field, at, count in ((0, 0, 5), (2, 5, 5), (1, 10, 6)):
            if field != 1 and not -10 <= x < 18:
                first[x + 11, at:at + count, :] = jnp.zeros((count, 128), F32)
                last[x + 11, at:at + count, :] = jnp.zeros((count, 128), F32)
                continue
            p = mid_plane(field, x, own, left, right, left2, right2)
            first[x + 11, at:at + count, :] = p[0:count]
            last[x + 11, at:at + count, :] = p[8 - count:8]


def coarse_kernel(
    x_fine, own, left, right, left2, right2, down, up, out, mid_out,
    be, bb, ss, wx, wy, wym, wz, wzm, diag, inv, rhs_n, xa, xb, step, pair,
    be2, ss2, wx2, wy2, wym2, wz2, wzm2, diag2, inv2, rhs_n2, xa2, xb2, step2,
    rep_mid, rep_fine, mids,
):
    near, far, sides = flags()

    def spread(dst, plane, start, packed):
        n = packed.shape[0]
        even = lanes(n) % 2 == 0
        dst[plane, pl.ds(start, n, 2), :] = jnp.where(even, packed, roll(packed, 1))
        dst[plane, pl.ds(start + 1, n, 2), :] = jnp.where(even, roll(packed, -1), packed)

    for x in range(-11, 19):
        f = near[0] if -8 <= x < 0 else far[0] if x < -8 else None
        f = near[1] if 8 <= x < 16 else far[1] if x >= 16 else f
        p = mid_plane(1, x, own, left, right, left2, right2)
        lo, hi = down[x + 11, 10:16, :] * sides[0], up[x + 11, 10:16, :] * sides[1]
        if f is not None:
            p, lo, hi = p * f, lo * f, hi * f
        spread(be, x + 11, 20, p)
        spread(be, x + 11, 8, lo)
        spread(be, x + 11, 36, hi)
    for x in range(-10, 18):
        for dst, field, at in ((bb, 0, 0), (ss, 2, 5)):
            spread(dst, x + 10, 12, mid_plane(field, x, own, left, right, left2, right2))
            spread(dst, x + 10, 2, down[x + 11, at:at + 5, :])
            spread(dst, x + 10, 28, up[x + 11, at:at + 5, :])
    work = (wx, wy, wym, wz, wzm, diag, inv, rhs_n, xa)
    build(10, 28, 40, 2, 0.25, be, lambda i: bb[i], lambda i: ss[i], work)
    x1 = smooth(28, 40, 2, work, xb, step)

    low_pair = lanes(16) % 4 < 2

    def down_sample(src, plane, start):
        s = src[plane, pl.ds(start, 16, 2), :] + src[plane, pl.ds(start + 1, 16, 2), :]
        return (s + jnp.where(low_pair, roll(s, -2), roll(s, 2))) * 0.125

    for m in range(12):
        pair[m] = be[2 * m + 3, pl.ds(8, 40), :] + be[2 * m + 4, pl.ds(8, 40), :]
    for m in range(12):
        be2[m, 8:24, :] = down_sample(pair, m, 4)
    for m in range(10):
        pair[12 + m] = ss[2 * m + 4] + ss[2 * m + 5]
    for m in range(10):
        ss2[m] = down_sample(pair, 12 + m, 4)
    held = {}

    def emit(i, cur, e):
        r = e * diag[i]
        if i % 2 == 0:
            held[0] = r
        else:
            pair[22 + (i - 4) // 2] = held[0] + r

    scaled_residual(x1, 4, 24, 40, 2, work, emit)
    work2 = (wx2, wy2, wym2, wz2, wzm2, diag2, inv2, rhs_n2, xa2)
    build(3, 10, 16, 4, 0.0625, be2, lambda i: down_sample(pair, 22 + i, 4), lambda i: ss2[i], work2)
    x2 = smooth(10, 16, 4, work2, xb2, step2)

    for m in range(4):
        low = x2[m + 3, pl.ds(12, 8), :]
        rep_mid[m, pl.ds(0, 8, 2), :] = low
        rep_mid[m, pl.ds(1, 8, 2), :] = low
    for m in range(8):
        mid = x1[m + 10, pl.ds(20, 16), :] + rep_mid[m // 2]
        mids[pl.ds(16 * m, 16), :] = mid
        rep_fine[m, pl.ds(0, 16, 2), :] = mid
        rep_fine[m, pl.ds(1, 16, 2), :] = mid
    for i in range(16):
        out[i] = x_fine[i] + rep_fine[i // 2]
    row = lax.broadcasted_iota(jnp.int32, (128, 64), 0)
    col = lax.broadcasted_iota(jnp.int32, (128, 64), 1)
    pick = jnp.where(row == 2 * col, 1.0, 0.0).astype(F32)
    compact = jnp.dot(mids[...], pick, precision=lax.Precision.HIGHEST, preferred_element_type=F32)
    for m in range(8):
        mid_out[m] = compact[16 * m:16 * m + 16]


def vmem(*shape):
    return pltpu.VMEM(shape, F32)


def call(kernel, ins, outs, scratch=(), limit=24 * 2**20):
    spec = pl.BlockSpec(memory_space=pltpu.VMEM)
    return pl.pallas_call(
        kernel,
        out_shape=[jax.ShapeDtypeStruct(s, F32) for s in outs],
        in_specs=[spec] * len(ins),
        out_specs=[spec] * len(outs),
        scratch_shapes=list(scratch),
        compiler_params=pltpu.CompilerParams(vmem_limit_bytes=limit),
    )(*ins)


def ring(value, axis, by):
    n = lax.axis_size(axis)
    return lax.ppermute(value, axis, [(i, (i + by) % n) for i in range(n)])


def work_scratch(planes, rows):
    full = [vmem(planes, rows, 128) for _ in range(8)]
    tall = [vmem(planes, rows + 16, 128) for _ in range(2)]
    return full + tall + [vmem(planes, rows, 128)]


def local(b, beta, shift):
    to_right = jnp.concatenate([b[12:], beta[11:], shift[12:]], axis=0)
    to_left = jnp.concatenate([b[:4], beta[:5], shift[:4]], axis=0)
    left, right = ring(to_right, "gx", 1), ring(to_left, "gx", -1)
    first, last = call(pack_fine_y, (b, beta, shift, left, right), [(50, 8, 128)] * 2)
    down, up = ring(last, "gy", 1), ring(first, "gy", -1)
    x_fine, packed = call(
        fine_kernel,
        (b, beta, shift, left, right, down, up),
        [(16, 32, 128), (3, 8, 8, 128)],
        [vmem(26, 56, 128), vmem(24, 40, 128), vmem(24, 40, 128)] + work_scratch(24, 40) + [vmem(24, 40, 128)],
    )
    tail = jnp.concatenate([packed[0, 6:], packed[1, 5:], packed[2, 6:]], axis=0)
    head = jnp.concatenate([packed[0, :2], packed[1, :3], packed[2, :2]], axis=0)
    left, right = ring(packed, "gx", 1), ring(packed, "gx", -1)
    left2, right2 = ring(tail, "gx", 2), ring(head, "gx", -2)
    around = (packed, left, right, left2, right2)
    first, last = call(pack_mid_y, around, [(30, 16, 128)] * 2)
    down, up = ring(last, "gy", 1), ring(first, "gy", -1)
    return tuple(call(
        coarse_kernel,
        (x_fine, *around, down, up),
        [(16, 32, 128), (8, 16, 64)],
        [vmem(30, 56, 128), vmem(28, 40, 128), vmem(28, 40, 128)] + work_scratch(28, 40) + [vmem(32, 40, 128)]
        + [vmem(12, 32, 128), vmem(10, 16, 128)] + work_scratch(10, 16)
        + [vmem(4, 16, 128), vmem(8, 32, 128), vmem(128, 128)],
    ))


def solution(mesh):
    placed = P("gx", "gy", None)
    return jax.shard_map(
        local, mesh=mesh, in_specs=(placed,) * 3, out_specs=(placed, placed), check_vma=False
    )
```

```python
import jax
import jax.numpy as jnp
from jax import lax
from jax.experimental import pallas as pl
from jax.experimental.pallas import tpu as pltpu
from jax.sharding import PartitionSpec as P

SWEEPS = 4
THETA, DELTA = 1.15, 0.85
SIGMA = THETA / DELTA
F32 = jnp.float32


def coefficients():
    rho, out = 1.0 / SIGMA, []
    for _ in range(SWEEPS - 1):
        new = 1.0 / (2.0 * SIGMA - rho)
        out.append((new * rho, 2.0 * new / DELTA))
        rho = new
    return out


def lanes(rows):
    return lax.broadcasted_iota(jnp.int32, (rows, 128), 1)


def roll(value, shift):
    return pltpu.roll(value, shift % 128, 1)


class Level:
    def __init__(self, depth, own_planes, rows, own_rows, rep):
        self.depth, self.own, self.rep = depth, own_planes, rep
        self.planes = own_planes + 2 * depth
        self.rows, self.first_row, self.own_rows = rows, (rows - own_rows) // 2, own_rows

    def span(self, plane, reach):
        x = plane - self.depth
        far = max(0, -x, x - self.own + 1)
        side = max(0, reach - far)
        lo = max(0, self.first_row - side) // 8 * 8
        hi = min(self.rows, -(-(self.first_row + self.own_rows + side) // 8) * 8)
        return lo, hi - lo


def build(level, scale, beta, rhs, shift, work):
    wx, wy, wym, wz, wzm, diag, inv, rhs_n, start = work
    rep, half, last_span = level.rep, 0.5 * scale, None
    for i in range(level.planes):
        lo, n = level.span(i, level.depth)
        if (lo, n) != last_span:
            prev, cur = beta[i, pl.ds(8 + lo, n), :], beta[i + 1, pl.ds(8 + lo, n), :]
            wx_prev = half * (prev + cur)
            if i:
                wx[i - 1, pl.ds(lo, n), :] = wx_prev
            lane = lanes(n)
            first, last = lane < rep, lane >= 128 - rep
            last_span = (lo, n)
        at = pl.ds(lo, n)
        nxt = beta[i + 2, pl.ds(8 + lo, n), :]
        wx_next = half * (cur + nxt)
        w_up = half * (cur + beta[i + 1, pl.ds(9 + lo, n), :])
        w_down = half * (cur + beta[i + 1, pl.ds(7 + lo, n), :])
        w_right = half * (cur + jnp.where(last, 0.0, roll(cur, -rep)))
        w_left = half * (cur + jnp.where(first, 0.0, roll(cur, rep)))
        d = shift(i, at) + (wx_prev + wx_next + w_up + w_down + w_right + w_left)
        iv = jnp.where(cur > 0.0, 1.0 / d, 0.0)
        c = rhs(i, at) * iv
        wx[i, at, :] = wx_next
        wy[i, at, :] = w_up
        wym[i, at, :] = w_down
        wz[i, at, :] = jnp.where(last, 0.0, w_right)
        wzm[i, at, :] = jnp.where(first, 0.0, w_left)
        diag[i, at, :] = d
        inv[i, at, :] = iv
        rhs_n[i, at, :] = c
        start[i, pl.ds(8 + lo, n), :] = c * (1.0 / THETA)
        cur, wx_prev = nxt, wx_next


def scaled_residual(level, src, cut, reach, work, emit):
    wx, wy, wym, wz, wzm, _, inv, rhs_n, _ = work
    rep, last_span = level.rep, None
    for i in range(cut, level.planes - cut):
        lo, n = level.span(i, reach)
        at, dom = pl.ds(lo, n), pl.ds(8 + lo, n)
        if (lo, n) != last_span:
            prev, cur, wx_prev = src[i - 1, dom, :], src[i, dom, :], wx[i - 1, at, :]
            last_span = (lo, n)
        nxt, wx_next = src[i + 1, dom, :], wx[i, at, :]
        t = wx_next * nxt + wx_prev * prev
        t = t + wy[i, at, :] * src[i, pl.ds(9 + lo, n), :] + wym[i, at, :] * src[i, pl.ds(7 + lo, n), :]
        t = t + wz[i, at, :] * roll(cur, -rep) + wzm[i, at, :] * roll(cur, rep)
        emit(i, lo, n, cur, rhs_n[i, at, :] + inv[i, at, :] * t - cur)
        prev, cur, wx_prev = cur, nxt, wx_next


def smooth(level, work, other, step):
    src, dst = work[8], other
    for k, (a, g) in enumerate(coefficients()):

        def emit(i, lo, n, cur, e, a=a, g=g, k=k, dst=dst):
            before = cur if k == 0 else step[i, pl.ds(lo, n), :]
            d = a * before + g * e
            if k < SWEEPS - 2:
                step[i, pl.ds(lo, n), :] = d
            dst[i, pl.ds(8 + lo, n), :] = cur + d

        scaled_residual(level, src, k + 1, level.depth - k - 1, work, emit)
        src, dst = dst, src
    return src


FINE = Level(4, 16, 40, 32, 1)
MID = Level(10, 8, 40, 16, 2)
LOW = Level(3, 4, 16, 8, 4)


def y_rows(level, order, cells):
    table, at = {}, 0
    for field, x, per in order:
        far = max(0, -x, x - level.own + 1)
        count = -(-max(0, level.depth + (field == 1) - far) // per)
        if count:
            table[field, x] = (at, count)
            at += count
    return table, -(-at // 8) * 8


def y_order(level, per):
    own = [(f, x, per) for x in range(level.own) for f in (0, 2)] + [(1, x, per) for x in range(level.own)]
    sides = [x for x in range(-level.depth, level.own + level.depth) if not 0 <= x < level.own]
    return own + [(f, x, per) for f in (0, 2, 1) for x in sides]


FINE_ROWS, FINE_SIZE = y_rows(FINE, y_order(FINE, 1), 1)
MID_ROWS, MID_SIZE = y_rows(MID, y_order(MID, 2), 2)


def flag(condition):
    return jnp.where(condition, 1.0, 0.0).astype(F32)


def x_flags():
    i, n = lax.axis_index("gx"), lax.axis_size("gx")
    return {-2: flag(i > 1), -1: flag(i > 0), 1: flag(i < n - 1), 2: flag(i < n - 2)}


def y_flags():
    j, n = lax.axis_index("gy"), lax.axis_size("gy")
    return flag(j > 0), flag(j < n - 1)


def upward(axis, by):
    return lax.rem(lax.axis_index(axis), 2 * by) >= by


def swaps(first, second, axis, by):
    axes = ("gx", "gy")
    size = [lax.axis_size(name) for name in axes]
    dim = axes.index(axis)
    orders = []
    for sign in (1, -1):
        pairs = []
        for i in range(size[0]):
            for j in range(size[1]):
                to = [i, j]
                to[dim] += sign * by if to[dim] % (2 * by) >= by else -sign * by
                if not 0 <= to[dim] < size[dim]:
                    to = [i, j]
                    to[1 - dim] ^= 1
                pairs.append((i * size[1] + j, to[0] * size[1] + to[1]))
        orders.append(pairs)
    return lax.ppermute(first, axes, orders[0]), lax.ppermute(second, axes, orders[1])


COUNTS = (4, 5, 4)
STARTS = (0, 4, 9)


def pack_fine_x(fields):
    ends = [f[:n] for f, n in zip(fields, COUNTS)] + [f[16 - n:] for f, n in zip(fields, COUNTS)]
    first, last = jnp.concatenate(ends[:3], axis=0), jnp.concatenate(ends[3:], axis=0)
    first, last = lax.optimization_barrier((first, last))
    up = upward("gx", 1)
    return jnp.where(up, last, first), jnp.where(up, first, last)


def fine_plane(field, x, own, in_a, in_b, up):
    if 0 <= x < 16:
        return own[field][x]
    i = STARTS[field] + (x + COUNTS[field] if x < 0 else x - 16)
    return jnp.where(up, in_b[i], in_a[i]) if x < 0 else jnp.where(up, in_a[i], in_b[i])


def pack_y(table, height, plane, out_a, out_b):
    up = upward("gy", 1)
    for (field, x), (at, count) in table.items():
        p = plane(field, x)
        first, last = p[0:count], p[height - count:height]
        out_a[pl.ds(at, count), :] = jnp.where(up, last, first)
        out_b[pl.ds(at, count), :] = jnp.where(up, first, last)


def pack_fine_y(b, beta, shift, in_a, in_b, out_a, out_b):
    up = upward("gx", 1)
    pack_y(FINE_ROWS, 32, lambda f, x: fine_plane(f, x, (b, beta, shift), in_a, in_b, up), out_a, out_b)


def y_sides(table, field, x, in_a, in_b, up):
    at, count = table[field, x]
    a, b = in_a[pl.ds(at, count), :], in_b[pl.ds(at, count), :]
    return jnp.where(up, b, a), jnp.where(up, a, b), count


def fine_kernel(
    b, beta, shift, xa_in, xb_in, ya_in, yb_in, x_out, packed, far_a, far_b,
    be, bb, ss, wx, wy, wym, wz, wzm, diag, inv, rhs_n, xa, xb, step, pair,
):
    near, (low, high) = x_flags(), y_flags()
    up_x, up_y = upward("gx", 1), upward("gy", 1)
    for field, dst, first in ((1, be, 12), (0, bb, 4), (2, ss, 4)):
        reach = COUNTS[field]
        for x in range(-reach, 16 + reach):
            p = fine_plane(field, x, (b, beta, shift), xa_in, xb_in, up_x)
            f = None if field != 1 or 0 <= x < 16 else near[-1] if x < 0 else near[1]
            dst[x + reach, pl.ds(first, 32), :] = p if f is None else p * f
            if (field, x) in FINE_ROWS:
                lo, hi, n = y_sides(FINE_ROWS, field, x, ya_in, yb_in, up_y)
                if field == 1:
                    lo, hi = (lo * low, hi * high) if f is None else (lo * (low * f), hi * (high * f))
                dst[x + reach, pl.ds(first - n, n), :] = lo
                dst[x + reach, pl.ds(first + 32, n), :] = hi
    work = (wx, wy, wym, wz, wzm, diag, inv, rhs_n, xa)
    build(FINE, 1.0, be, lambda i, at: bb[i, at, :], lambda i, at: ss[i, at, :], work)
    x = smooth(FINE, work, xb, step)

    even = lanes(8) % 2 == 0

    def pack(field, m, plane, start):
        e = pair[plane, pl.ds(start, 8, 4), :] + pair[plane, pl.ds(start + 1, 8, 4), :]
        o = pair[plane, pl.ds(start + 2, 8, 4), :] + pair[plane, pl.ds(start + 3, 8, 4), :]
        packed[field, m] = jnp.where(even, e + roll(e, -1), o + roll(o, 1)) * 0.125

    for m in range(8):
        pair[m, 0:32, :] = beta[2 * m] + beta[2 * m + 1]
        pair[m + 8, 0:32, :] = shift[2 * m] + shift[2 * m + 1]
    for m in range(8):
        pack(1, m, m, 0)
        pack(2, m, m + 8, 0)
    held = {}

    def emit(i, lo, n, cur, e):
        r = e * diag[i]
        if i % 2 == 0:
            held[0] = r
        else:
            pair[16 + (i - 4) // 2] = held[0] + r

    scaled_residual(FINE, x, 4, 0, work, emit)
    for m in range(8):
        pack(0, m, m + 16, 4)
    up2 = upward("gx", 2)
    for field, n in enumerate(FAR):
        for i in range(n):
            first, last = packed[field, i], packed[field, 8 - n + i]
            far_a[FAR_AT[field] + i] = jnp.where(up2, last, first)
            far_b[FAR_AT[field] + i] = jnp.where(up2, first, last)
    for i in range(16):
        x_out[i] = x[i + 4, pl.ds(12, 32), :]


FAR = (2, 3, 2)
FAR_AT = (0, 2, 5)


def mid_plane(field, x, own, near_a, near_b, far_a, far_b, up, up2):
    if 0 <= x < 8:
        return own[field, x]
    if -8 <= x < 16:
        a, b = near_a[field, x % 8], near_b[field, x % 8]
    else:
        i = FAR_AT[field] + (x + 8 + FAR[field] if x < 0 else x - 16)
        a, b, up = far_a[i], far_b[i], up2
    return jnp.where(up, b, a) if x < 0 else jnp.where(up, a, b)


def pack_mid_y(own, near_a, near_b, far_a, far_b, out_a, out_b):
    up, up2 = upward("gx", 1), upward("gx", 2)
    pack_y(MID_ROWS, 8, lambda f, x: mid_plane(f, x, own, near_a, near_b, far_a, far_b, up, up2), out_a, out_b)


def coarse_kernel(
    x_fine, own, near_a, near_b, far_a, far_b, ya_in, yb_in, out, mid_out,
    be, bb, ss, wx, wy, wym, wz, wzm, diag, inv, rhs_n, xa, xb, step, pair,
    be2, ss2, wx2, wy2, wym2, wz2, wzm2, diag2, inv2, rhs_n2, xa2, xb2, step2,
    rep_mid, rep_fine, mids,
):
    near, (low, high) = x_flags(), y_flags()
    up, up2, up_y = upward("gx", 1), upward("gx", 2), upward("gy", 1)

    def spread(dst, plane, start, packed):
        n = packed.shape[0]
        even = lanes(n) % 2 == 0
        dst[plane, pl.ds(start, n, 2), :] = jnp.where(even, packed, roll(packed, 1))
        dst[plane, pl.ds(start + 1, n, 2), :] = jnp.where(even, roll(packed, -1), packed)

    for field, dst, first in ((1, be, 20), (0, bb, 12), (2, ss, 12)):
        reach = 11 if field == 1 else 10
        for x in range(-reach, 8 + reach):
            p = mid_plane(field, x, own, near_a, near_b, far_a, far_b, up, up2)
            f = None
            if field == 1 and not 0 <= x < 8:
                f = near[-2 if x < -8 else -1 if x < 0 else 1 if x < 16 else 2]
                p = p * f
            spread(dst, x + reach, first, p)
            if (field, x) in MID_ROWS:
                lo, hi, n = y_sides(MID_ROWS, field, x, ya_in, yb_in, up_y)
                if field == 1:
                    lo, hi = (lo * low, hi * high) if f is None else (lo * (low * f), hi * (high * f))
                spread(dst, x + reach, first - 2 * n, lo)
                spread(dst, x + reach, first + 16, hi)
    work = (wx, wy, wym, wz, wzm, diag, inv, rhs_n, xa)
    build(MID, 0.25, be, lambda i, at: bb[i, at, :], lambda i, at: ss[i, at, :], work)
    x1 = smooth(MID, work, xb, step)

    low_pair = lanes(16) % 4 < 2

    def down_sample(plane):
        s = pair[plane, pl.ds(4, 16, 2), :] + pair[plane, pl.ds(5, 16, 2), :]
        return (s + jnp.where(low_pair, roll(s, -2), roll(s, 2))) * 0.125

    for m in range(12):
        pair[m] = be[2 * m + 3, pl.ds(8, 40), :] + be[2 * m + 4, pl.ds(8, 40), :]
    for m in range(10):
        pair[12 + m] = ss[2 * m + 4] + ss[2 * m + 5]
    for m in range(12):
        be2[m, 8:24, :] = down_sample(m)
    for m in range(10):
        ss2[m] = down_sample(12 + m)
    held = {}

    def emit(i, lo, n, cur, e):
        r = e * diag[i, pl.ds(lo, n), :]
        if i % 2 == 0:
            held[0] = lo, n, r
        else:
            lo0, n0, r0 = held[0]
            at, end = max(lo, lo0), min(lo + n, lo0 + n0)
            total = r0[at - lo0:end - lo0] + r[at - lo:end - lo]
            pair[22 + (i - 4) // 2, pl.ds(at, end - at), :] = total

    scaled_residual(MID, x1, 4, 6, work, emit)
    work2 = (wx2, wy2, wym2, wz2, wzm2, diag2, inv2, rhs_n2, xa2)
    build(LOW, 0.0625, be2, lambda i, at: down_sample(22 + i), lambda i, at: ss2[i, at, :], work2)
    x2 = smooth(LOW, work2, xb2, step2)

    for m in range(4):
        low_x = x2[m + 3, pl.ds(12, 8), :]
        rep_mid[m, pl.ds(0, 8, 2), :] = low_x
        rep_mid[m, pl.ds(1, 8, 2), :] = low_x
    for m in range(8):
        mid = x1[m + 10, pl.ds(20, 16), :] + rep_mid[m // 2]
        mids[pl.ds(16 * m, 16), :] = mid
        rep_fine[m, pl.ds(0, 16, 2), :] = mid
        rep_fine[m, pl.ds(1, 16, 2), :] = mid
    for i in range(16):
        out[i] = x_fine[i] + rep_fine[i // 2]
    row = lax.broadcasted_iota(jnp.int32, (128, 64), 0)
    col = lax.broadcasted_iota(jnp.int32, (128, 64), 1)
    pick = jnp.where(row == 2 * col, 1.0, 0.0).astype(F32)
    compact = jnp.dot(mids[...], pick, precision=lax.Precision.HIGHEST, preferred_element_type=F32)
    for m in range(8):
        mid_out[m] = compact[16 * m:16 * m + 16]


def vmem(*shape):
    return pltpu.VMEM(shape, F32)


def call(kernel, ins, outs, scratch=(), limit=24 * 2**20, space=pltpu.VMEM):
    return pl.pallas_call(
        kernel,
        out_shape=[jax.ShapeDtypeStruct(s, F32) for s in outs],
        in_specs=[pl.BlockSpec(memory_space=space)] * len(ins),
        out_specs=[pl.BlockSpec(memory_space=pltpu.VMEM)] * len(outs),
        scratch_shapes=list(scratch),
        compiler_params=pltpu.CompilerParams(vmem_limit_bytes=limit),
    )(*ins)


def work_scratch(level):
    planes, rows = level.planes, level.rows
    flat = [vmem(planes, rows, 128) for _ in range(8)]
    return flat + [vmem(planes, rows + 16, 128) for _ in range(2)] + [vmem(planes, rows, 128)]


def level_scratch(level):
    planes, rows = level.planes, level.rows
    return [vmem(planes + 2, rows + 16, 128)] + [vmem(planes, rows, 128)] * 2 + work_scratch(level)


def local(b, beta, shift):
    a, c = pack_fine_x((b, beta, shift))
    xs = swaps(a, c, "gx", 1)
    a, c = call(pack_fine_y, (b, beta, shift, *xs), [(FINE_SIZE, 128)] * 2)
    ys = swaps(a, c, "gy", 1)
    x_fine, packed, a, c = call(
        fine_kernel,
        (b, beta, shift, *xs, *ys),
        [(16, 32, 128), (3, 8, 8, 128), (7, 8, 128), (7, 8, 128)],
        level_scratch(FINE) + [vmem(24, 40, 128)],
    )
    around = (packed, *swaps(packed, packed, "gx", 1), *swaps(a, c, "gx", 2))
    a, c = call(pack_mid_y, around, [(MID_SIZE, 128)] * 2)
    ys = swaps(a, c, "gy", 1)
    low = [vmem(LOW.planes + 2, 32, 128), vmem(LOW.planes, 16, 128)] + work_scratch(LOW)
    return tuple(call(
        coarse_kernel,
        (x_fine, *around, *ys),
        [(16, 32, 128), (8, 16, 64)],
        level_scratch(MID) + [vmem(32, 40, 128)] + low + [vmem(4, 16, 128), vmem(8, 32, 128), vmem(128, 128)],
    ))


def solution(mesh):
    placed = P("gx", "gy", None)
    return jax.shard_map(
        local, mesh=mesh, in_specs=(placed,) * 3, out_specs=(placed, placed), check_vma=False
    )
```

```python
import jax
import jax.numpy as jnp
from jax import lax
from jax.experimental import pallas as pl
from jax.experimental.pallas import tpu as pltpu
from jax.sharding import PartitionSpec as P

SWEEPS = 4
THETA, DELTA = 1.15, 0.85
SIGMA = THETA / DELTA
F32 = jnp.float32


def coefficients():
    rho, out = 1.0 / SIGMA, []
    for _ in range(SWEEPS - 1):
        new = 1.0 / (2.0 * SIGMA - rho)
        out.append((new * rho, 2.0 * new / DELTA))
        rho = new
    return out


def lanes(rows):
    return lax.broadcasted_iota(jnp.int32, (rows, 128), 1)


def roll(value, shift):
    return pltpu.roll(value, shift % 128, 1)


class Level:
    def __init__(self, depth, own_planes, rows, own_rows, rep, folded):
        self.depth, self.own, self.rep, self.folded = depth, own_planes, rep, folded
        self.planes = depth + own_planes // 2 if folded else own_planes + 2 * depth
        self.rows, self.first_row, self.own_rows = rows, (rows - own_rows) // 2, own_rows

    def cut(self, k):
        return k, self.planes - (0 if self.folded else k)

    def span(self, plane, reach):
        x = plane - self.depth
        far = max(0, -x) if self.folded else max(0, -x, x - self.own + 1)
        side = max(0, reach - far)
        lo = max(0, self.first_row - side) // 8 * 8
        hi = min(self.rows, -(-(self.first_row + self.own_rows + side) // 8) * 8)
        return lo, hi - lo

    def put(self, dst, i, at, value):
        dst[i, at, :] = value
        if self.folded and i == self.planes - 1:
            dst[i + 1, at, :] = swap_lanes(value)


def swap_lanes(value):
    return jnp.where(lanes(value.shape[0]) % 2 == 0, roll(value, -1), roll(value, 1))


def build(level, scale, beta, rhs, shift, work):
    wx, wy, wym, wz, wzm, diag, inv, rhs_n, start = work
    rep, half, last_span = level.rep, 0.5 * scale, None
    for i in range(level.planes):
        lo, n = level.span(i, level.depth)
        if (lo, n) != last_span:
            prev, cur = beta[i, pl.ds(8 + lo, n), :], beta[i + 1, pl.ds(8 + lo, n), :]
            wx_prev = half * (prev + cur)
            if i:
                wx[i - 1, pl.ds(lo, n), :] = wx_prev
            lane = lanes(n)
            first, last = lane < rep, lane >= 128 - rep
            last_span = (lo, n)
        at = pl.ds(lo, n)
        nxt = beta[i + 2, pl.ds(8 + lo, n), :]
        wx_next = half * (cur + nxt)
        w_up = half * (cur + beta[i + 1, pl.ds(9 + lo, n), :])
        w_down = half * (cur + beta[i + 1, pl.ds(7 + lo, n), :])
        w_right = half * (cur + jnp.where(last, 0.0, roll(cur, -rep)))
        w_left = half * (cur + jnp.where(first, 0.0, roll(cur, rep)))
        d = shift(i, at) + (wx_prev + wx_next + w_up + w_down + w_right + w_left)
        iv = jnp.where(cur > 0.0, 1.0 / d, 0.0)
        c = rhs(i, at) * iv
        wx[i, at, :] = wx_next
        wy[i, at, :] = w_up
        wym[i, at, :] = w_down
        wz[i, at, :] = jnp.where(last, 0.0, w_right)
        wzm[i, at, :] = jnp.where(first, 0.0, w_left)
        diag[i, at, :] = d
        inv[i, at, :] = iv
        rhs_n[i, at, :] = c
        level.put(start, i, pl.ds(8 + lo, n), c * (1.0 / THETA))
        cur, wx_prev = nxt, wx_next


def scaled_residual(level, src, cut, reach, work, emit):
    wx, wy, wym, wz, wzm, _, inv, rhs_n, _ = work
    rep, last_span = level.rep, None
    for i in range(*level.cut(cut)):
        lo, n = level.span(i, reach)
        at, dom = pl.ds(lo, n), pl.ds(8 + lo, n)
        if (lo, n) != last_span:
            prev, cur, wx_prev = src[i - 1, dom, :], src[i, dom, :], wx[i - 1, at, :]
            last_span = (lo, n)
        nxt, wx_next = src[i + 1, dom, :], wx[i, at, :]
        t = wx_next * nxt + wx_prev * prev
        t = t + wy[i, at, :] * src[i, pl.ds(9 + lo, n), :] + wym[i, at, :] * src[i, pl.ds(7 + lo, n), :]
        t = t + wz[i, at, :] * roll(cur, -rep) + wzm[i, at, :] * roll(cur, rep)
        emit(i, lo, n, cur, rhs_n[i, at, :] + inv[i, at, :] * t - cur)
        prev, cur, wx_prev = cur, nxt, wx_next


def smooth(level, work, other, step):
    src, dst = work[8], other
    for k, (a, g) in enumerate(coefficients()):

        def emit(i, lo, n, cur, e, a=a, g=g, k=k, dst=dst):
            before = cur if k == 0 else step[i, pl.ds(lo, n), :]
            d = a * before + g * e
            if k < SWEEPS - 2:
                step[i, pl.ds(lo, n), :] = d
            level.put(dst, i, pl.ds(8 + lo, n), cur + d)

        scaled_residual(level, src, k + 1, level.depth - k - 1, work, emit)
        src, dst = dst, src
    return src


FINE = Level(4, 16, 40, 32, 1, False)
MID = Level(10, 8, 40, 16, 2, True)
LOW = Level(3, 4, 16, 8, 4, True)


def y_rows(level, order, cells):
    table, at = {}, 0
    for field, x, per in order:
        far = max(0, -x, x - level.own + 1)
        count = -(-max(0, level.depth + (field == 1) - far) // per)
        if count:
            table[field, x] = (at, count)
            at += count
    return table, -(-at // 8) * 8


def y_order(level, per):
    own = [(f, x, per) for x in range(level.own) for f in (0, 2)] + [(1, x, per) for x in range(level.own)]
    sides = [x for x in range(-level.depth, level.own + level.depth) if not 0 <= x < level.own]
    return own + [(f, x, per) for f in (0, 2, 1) for x in sides]


FINE_ROWS, FINE_SIZE = y_rows(FINE, y_order(FINE, 1), 1)
MID_ROWS, MID_SIZE = y_rows(MID, y_order(MID, 2), 2)


def flag(condition):
    return jnp.where(condition, 1.0, 0.0).astype(F32)


def x_flags():
    i, n = lax.axis_index("gx"), lax.axis_size("gx")
    return {-2: flag(i > 1), -1: flag(i > 0), 1: flag(i < n - 1), 2: flag(i < n - 2)}


def y_flags():
    j, n = lax.axis_index("gy"), lax.axis_size("gy")
    return flag(j > 0), flag(j < n - 1)


def upward(axis, by):
    return lax.rem(lax.axis_index(axis), 2 * by) >= by


def swaps(first, second, axis, by):
    axes = ("gx", "gy")
    size = [lax.axis_size(name) for name in axes]
    dim = axes.index(axis)
    orders = []
    for sign in (1, -1):
        pairs = []
        for i in range(size[0]):
            for j in range(size[1]):
                to = [i, j]
                to[dim] += sign * by if to[dim] % (2 * by) >= by else -sign * by
                if not 0 <= to[dim] < size[dim]:
                    to = [i, j]
                    to[1 - dim] ^= 1
                pairs.append((i * size[1] + j, to[0] * size[1] + to[1]))
        orders.append(pairs)
    return lax.ppermute(first, axes, orders[0]), lax.ppermute(second, axes, orders[1])


COUNTS = (4, 5, 4)
STARTS = (0, 4, 9)


def pack_fine_x(fields):
    ends = [f[:n] for f, n in zip(fields, COUNTS)] + [f[16 - n:] for f, n in zip(fields, COUNTS)]
    first, last = jnp.concatenate(ends[:3], axis=0), jnp.concatenate(ends[3:], axis=0)
    first, last = lax.optimization_barrier((first, last))
    up = upward("gx", 1)
    return jnp.where(up, last, first), jnp.where(up, first, last)


def fine_plane(field, x, own, in_a, in_b, up):
    if 0 <= x < 16:
        return own[field][x]
    i = STARTS[field] + (x + COUNTS[field] if x < 0 else x - 16)
    return jnp.where(up, in_b[i], in_a[i]) if x < 0 else jnp.where(up, in_a[i], in_b[i])


def pack_y(table, height, plane, out_a, out_b):
    up = upward("gy", 1)
    for (field, x), (at, count) in table.items():
        p = plane(field, x)
        first, last = p[0:count], p[height - count:height]
        out_a[pl.ds(at, count), :] = jnp.where(up, last, first)
        out_b[pl.ds(at, count), :] = jnp.where(up, first, last)


def pack_fine_y(b, beta, shift, in_a, in_b, out_a, out_b):
    up = upward("gx", 1)
    pack_y(FINE_ROWS, 32, lambda f, x: fine_plane(f, x, (b, beta, shift), in_a, in_b, up), out_a, out_b)


def y_sides(table, field, x, in_a, in_b, up):
    at, count = table[field, x]
    a, b = in_a[pl.ds(at, count), :], in_b[pl.ds(at, count), :]
    return jnp.where(up, b, a), jnp.where(up, a, b), count


def fine_kernel(
    b, beta, shift, xa_in, xb_in, ya_in, yb_in, x_out, packed, far_a, far_b,
    be, bb, ss, wx, wy, wym, wz, wzm, diag, inv, rhs_n, xa, xb, step, pair,
):
    near, (low, high) = x_flags(), y_flags()
    up_x, up_y = upward("gx", 1), upward("gy", 1)
    for field, dst, first in ((1, be, 12), (0, bb, 4), (2, ss, 4)):
        reach = COUNTS[field]
        for x in range(-reach, 16 + reach):
            p = fine_plane(field, x, (b, beta, shift), xa_in, xb_in, up_x)
            f = None if field != 1 or 0 <= x < 16 else near[-1] if x < 0 else near[1]
            dst[x + reach, pl.ds(first, 32), :] = p if f is None else p * f
            if (field, x) in FINE_ROWS:
                lo, hi, n = y_sides(FINE_ROWS, field, x, ya_in, yb_in, up_y)
                if field == 1:
                    lo, hi = (lo * low, hi * high) if f is None else (lo * (low * f), hi * (high * f))
                dst[x + reach, pl.ds(first - n, n), :] = lo
                dst[x + reach, pl.ds(first + 32, n), :] = hi
    work = (wx, wy, wym, wz, wzm, diag, inv, rhs_n, xa)
    build(FINE, 1.0, be, lambda i, at: bb[i, at, :], lambda i, at: ss[i, at, :], work)
    x = smooth(FINE, work, xb, step)

    even = lanes(8) % 2 == 0

    def pack(field, m, plane, start):
        e = pair[plane, pl.ds(start, 8, 4), :] + pair[plane, pl.ds(start + 1, 8, 4), :]
        o = pair[plane, pl.ds(start + 2, 8, 4), :] + pair[plane, pl.ds(start + 3, 8, 4), :]
        packed[field, m] = jnp.where(even, e + roll(e, -1), o + roll(o, 1)) * 0.125

    for m in range(8):
        pair[m, 0:32, :] = beta[2 * m] + beta[2 * m + 1]
        pair[m + 8, 0:32, :] = shift[2 * m] + shift[2 * m + 1]
    for m in range(8):
        pack(1, m, m, 0)
        pack(2, m, m + 8, 0)
    held = {}

    def emit(i, lo, n, cur, e):
        r = e * diag[i]
        if i % 2 == 0:
            held[0] = r
        else:
            pair[16 + (i - 4) // 2] = held[0] + r

    scaled_residual(FINE, x, 4, 0, work, emit)
    for m in range(8):
        pack(0, m, m + 16, 4)
    up2 = upward("gx", 2)
    for field, n in enumerate(FAR):
        for i in range(n):
            first, last = packed[field, i], packed[field, 8 - n + i]
            far_a[FAR_AT[field] + i] = jnp.where(up2, last, first)
            far_b[FAR_AT[field] + i] = jnp.where(up2, first, last)
    for i in range(16):
        x_out[i] = x[i + 4, pl.ds(12, 32), :]


FAR = (2, 3, 2)
FAR_AT = (0, 2, 5)


def mid_plane(field, x, own, near_a, near_b, far_a, far_b, up, up2):
    if 0 <= x < 8:
        return own[field, x]
    if -8 <= x < 16:
        a, b = near_a[field, x % 8], near_b[field, x % 8]
    else:
        i = FAR_AT[field] + (x + 8 + FAR[field] if x < 0 else x - 16)
        a, b, up = far_a[i], far_b[i], up2
    return jnp.where(up, b, a) if x < 0 else jnp.where(up, a, b)


def pack_mid_y(own, near_a, near_b, far_a, far_b, out_a, out_b):
    up, up2 = upward("gx", 1), upward("gx", 2)
    pack_y(MID_ROWS, 8, lambda f, x: mid_plane(f, x, own, near_a, near_b, far_a, far_b, up, up2), out_a, out_b)


def coarse_kernel(
    x_fine, own, near_a, near_b, far_a, far_b, ya_in, yb_in, out, mid_out,
    be, bb, ss, wx, wy, wym, wz, wzm, diag, inv, rhs_n, xa, xb, step, pair,
    be2, ss2, wx2, wy2, wym2, wz2, wzm2, diag2, inv2, rhs_n2, xa2, xb2, step2,
    rep_mid, rep_fine, mids,
):
    near, (low, high) = x_flags(), y_flags()
    up, up2, up_y = upward("gx", 1), upward("gx", 2), upward("gy", 1)

    def spread(dst, plane, start, a, b):
        n = a.shape[0]
        even = lanes(n) % 2 == 0
        dst[plane, pl.ds(start, n, 2), :] = jnp.where(even, a, roll(b, 1))
        dst[plane, pl.ds(start + 1, n, 2), :] = jnp.where(even, roll(a, -1), b)

    def gather(field, x):
        parts = [mid_plane(field, x, own, near_a, near_b, far_a, far_b, up, up2), None, None]
        if (field, x) in MID_ROWS:
            parts[1:] = y_sides(MID_ROWS, field, x, ya_in, yb_in, up_y)[:2]
        if field != 1:
            return parts
        f = 1.0 if 0 <= x < 8 else near[-2 if x < -8 else -1 if x < 0 else 1 if x < 16 else 2]
        return [p if p is None else p * s for p, s in zip(parts, (f, low * f, high * f))]

    for field, dst, first in ((1, be, 20), (0, bb, 12), (2, ss, 12)):
        reach = 11 if field == 1 else 10
        for i in range(reach + 4):
            a, b = gather(field, i - reach), gather(field, 7 + reach - i)
            spread(dst, i, first, a[0], b[0])
            if a[1] is not None:
                spread(dst, i, first - 2 * a[1].shape[0], a[1], b[1])
                spread(dst, i, first + 16, a[2], b[2])
    be[15, pl.ds(8, 40), :] = swap_lanes(be[14, pl.ds(8, 40), :])
    work = (wx, wy, wym, wz, wzm, diag, inv, rhs_n, xa)
    build(MID, 0.25, be, lambda i, at: bb[i, at, :], lambda i, at: ss[i, at, :], work)
    x1 = smooth(MID, work, xb, step)

    low_pair = lanes(16) % 4 < 2

    def down_sample(plane):
        s = pair[plane, pl.ds(4, 16, 2), :] + pair[plane, pl.ds(5, 16, 2), :]
        return (s + jnp.where(low_pair, roll(s, -2), roll(s, 2))) * 0.125

    for m in range(6):
        pair[m] = be[2 * m + 3, pl.ds(8, 40), :] + be[2 * m + 4, pl.ds(8, 40), :]
    for m in range(5):
        pair[6 + m] = ss[2 * m + 4] + ss[2 * m + 5]
    for m in range(6):
        be2[m, 8:24, :] = down_sample(m)
    be2[6, 8:24, :] = swap_lanes(be2[5, 8:24, :])
    for m in range(5):
        ss2[m] = down_sample(6 + m)
    held = {}

    def emit(i, lo, n, cur, e):
        r = e * diag[i, pl.ds(lo, n), :]
        if i % 2 == 0:
            held[0] = lo, n, r
        else:
            lo0, n0, r0 = held[0]
            at, end = max(lo, lo0), min(lo + n, lo0 + n0)
            total = r0[at - lo0:end - lo0] + r[at - lo:end - lo]
            pair[11 + (i - 4) // 2, pl.ds(at, end - at), :] = total

    scaled_residual(MID, x1, 4, 6, work, emit)
    work2 = (wx2, wy2, wym2, wz2, wzm2, diag2, inv2, rhs_n2, xa2)
    build(LOW, 0.0625, be2, lambda i, at: down_sample(11 + i), lambda i, at: ss2[i, at, :], work2)
    x2 = smooth(LOW, work2, xb2, step2)

    for m in range(2):
        low_x = x2[m + 3, pl.ds(12, 8), :]
        rep_mid[m, pl.ds(0, 8, 2), :] = low_x
        rep_mid[m, pl.ds(1, 8, 2), :] = low_x
    even = lanes(16) % 2 == 0
    for m in range(4):
        both = x1[m + 10, pl.ds(20, 16), :] + rep_mid[m // 2]
        for x, mid in (
            (m, jnp.where(even, both, roll(both, 1))),
            (7 - m, jnp.where(even, roll(both, -1), both)),
        ):
            mids[pl.ds(16 * x, 16), :] = mid
            rep_fine[x, pl.ds(0, 16, 2), :] = mid
            rep_fine[x, pl.ds(1, 16, 2), :] = mid
    for i in range(16):
        out[i] = x_fine[i] + rep_fine[i // 2]
    row = lax.broadcasted_iota(jnp.int32, (128, 64), 0)
    col = lax.broadcasted_iota(jnp.int32, (128, 64), 1)
    pick = jnp.where(row == 2 * col, 1.0, 0.0).astype(F32)
    compact = jnp.dot(mids[...], pick, precision=lax.Precision.HIGHEST, preferred_element_type=F32)
    for m in range(8):
        mid_out[m] = compact[16 * m:16 * m + 16]


def vmem(*shape):
    return pltpu.VMEM(shape, F32)


def call(kernel, ins, outs, scratch=(), limit=24 * 2**20, space=pltpu.VMEM):
    return pl.pallas_call(
        kernel,
        out_shape=[jax.ShapeDtypeStruct(s, F32) for s in outs],
        in_specs=[pl.BlockSpec(memory_space=space)] * len(ins),
        out_specs=[pl.BlockSpec(memory_space=pltpu.VMEM)] * len(outs),
        scratch_shapes=list(scratch),
        compiler_params=pltpu.CompilerParams(vmem_limit_bytes=limit),
    )(*ins)


def work_scratch(level):
    planes, rows = level.planes, level.rows
    flat = [vmem(planes, rows, 128) for _ in range(8)]
    return flat + [vmem(planes + 1, rows + 16, 128) for _ in range(2)] + [vmem(planes, rows, 128)]


def level_scratch(level):
    planes, rows = level.planes, level.rows
    return [vmem(planes + 2, rows + 16, 128)] + [vmem(planes, rows, 128)] * 2 + work_scratch(level)


def local(b, beta, shift):
    a, c = pack_fine_x((b, beta, shift))
    xs = swaps(a, c, "gx", 1)
    a, c = call(pack_fine_y, (b, beta, shift, *xs), [(FINE_SIZE, 128)] * 2)
    ys = swaps(a, c, "gy", 1)
    x_fine, packed, a, c = call(
        fine_kernel,
        (b, beta, shift, *xs, *ys),
        [(16, 32, 128), (3, 8, 8, 128), (7, 8, 128), (7, 8, 128)],
        level_scratch(FINE) + [vmem(24, 40, 128)],
    )
    around = (packed, *swaps(packed, packed, "gx", 1), *swaps(a, c, "gx", 2))
    a, c = call(pack_mid_y, around, [(MID_SIZE, 128)] * 2)
    ys = swaps(a, c, "gy", 1)
    low = [vmem(LOW.planes + 2, 32, 128), vmem(LOW.planes, 16, 128)] + work_scratch(LOW)
    return tuple(call(
        coarse_kernel,
        (x_fine, *around, *ys),
        [(16, 32, 128), (8, 16, 64)],
        level_scratch(MID) + [vmem(16, 40, 128)] + low + [vmem(2, 16, 128), vmem(8, 32, 128), vmem(128, 128)],
    ))


def solution(mesh):
    placed = P("gx", "gy", None)
    return jax.shard_map(
        local, mesh=mesh, in_specs=(placed,) * 3, out_specs=(placed, placed), check_vma=False
    )
```

```python
import jax
import jax.numpy as jnp
from jax import lax
from jax.experimental import pallas as pl
from jax.experimental.pallas import tpu as pltpu
from jax.sharding import PartitionSpec as P

SWEEPS = 4
THETA, DELTA = 1.15, 0.85
SIGMA = THETA / DELTA
F32 = jnp.float32


def coefficients():
    rho, out = 1.0 / SIGMA, []
    for _ in range(SWEEPS - 1):
        new = 1.0 / (2.0 * SIGMA - rho)
        out.append((new * rho, 2.0 * new / DELTA))
        rho = new
    return out


def lanes(rows):
    return lax.broadcasted_iota(jnp.int32, (rows, 128), 1)


def roll(value, shift):
    return pltpu.roll(value, shift % 128, 1)


class Level:
    def __init__(self, depth, own_planes, rows, own_rows, rep, folded=False, bases=(0,)):
        self.bases = bases
        self.depth, self.own, self.rep, self.folded = depth, own_planes, rep, folded
        self.planes = depth + own_planes // 2 if folded else own_planes + 2 * depth
        self.rows, self.first_row, self.own_rows = rows, (rows - own_rows) // 2, own_rows

    def cut(self, k):
        return k, self.planes - (0 if self.folded else k)

    def span(self, plane, reach):
        x = plane - self.depth
        far = max(0, -x) if self.folded else max(0, -x, x - self.own + 1)
        side = max(0, reach - far)
        lo = max(0, self.first_row - side) // 8 * 8
        hi = min(self.rows, -(-(self.first_row + self.own_rows + side) // 8) * 8)
        return lo, hi - lo

    def put(self, dst, i, at, value):
        dst[i, at, :] = value
        if self.folded and i == self.planes - 1:
            dst[i + 1, at, :] = swap_lanes(value)


def swap_lanes(value):
    return jnp.where(lanes(value.shape[0]) % 2 == 0, roll(value, -1), roll(value, 1))


def build(level, scale, beta, rhs, shift, work):
    wx, wy, wym, wz, wzm, diag, inv, rhs_n, start = work
    rep, half, last_span = level.rep, 0.5 * scale, None
    for base, i in [(base, i) for base in level.bases for i in range(level.planes)]:
        lo, n = level.span(i, level.depth)
        lo += base
        if (lo, n) != last_span:
            prev, cur = beta[i, pl.ds(8 + lo, n), :], beta[i + 1, pl.ds(8 + lo, n), :]
            wx_prev = half * (prev + cur)
            if i:
                wx[i - 1, pl.ds(lo, n), :] = wx_prev
            lane = lanes(n)
            first, last = lane < rep, lane >= 128 - rep
            last_span = (lo, n)
        at = pl.ds(lo, n)
        nxt = beta[i + 2, pl.ds(8 + lo, n), :]
        wx_next = half * (cur + nxt)
        w_up = half * (cur + beta[i + 1, pl.ds(9 + lo, n), :])
        w_down = half * (cur + beta[i + 1, pl.ds(7 + lo, n), :])
        w_right = half * (cur + jnp.where(last, 0.0, roll(cur, -rep)))
        w_left = half * (cur + jnp.where(first, 0.0, roll(cur, rep)))
        d = shift(i, at) + (wx_prev + wx_next + w_up + w_down + w_right + w_left)
        iv = jnp.where(cur > 0.0, 1.0 / d, 0.0)
        c = rhs(i, at) * iv
        wx[i, at, :] = wx_next
        wy[i, at, :] = w_up
        wym[i, at, :] = w_down
        wz[i, at, :] = jnp.where(last, 0.0, w_right)
        wzm[i, at, :] = jnp.where(first, 0.0, w_left)
        diag[i, at, :] = d
        inv[i, at, :] = iv
        rhs_n[i, at, :] = c
        level.put(start, i, pl.ds(8 + lo, n), c * (1.0 / THETA))
        cur, wx_prev = nxt, wx_next


def scaled_residual(level, src, cut, reach, work, emit):
    wx, wy, wym, wz, wzm, _, inv, rhs_n, _ = work
    rep, last_span = level.rep, None
    for base, i in [(base, i) for base in level.bases for i in range(*level.cut(cut))]:
        lo, n = level.span(i, reach)
        lo += base
        at, dom = pl.ds(lo, n), pl.ds(8 + lo, n)
        if (lo, n) != last_span:
            prev, cur, wx_prev = src[i - 1, dom, :], src[i, dom, :], wx[i - 1, at, :]
            last_span = (lo, n)
        nxt, wx_next = src[i + 1, dom, :], wx[i, at, :]
        t = wx_next * nxt + wx_prev * prev
        t = t + wy[i, at, :] * src[i, pl.ds(9 + lo, n), :] + wym[i, at, :] * src[i, pl.ds(7 + lo, n), :]
        t = t + wz[i, at, :] * roll(cur, -rep) + wzm[i, at, :] * roll(cur, rep)
        emit(i, lo, n, cur, rhs_n[i, at, :] + inv[i, at, :] * t - cur)
        prev, cur, wx_prev = cur, nxt, wx_next


def smooth(level, work, other, step):
    src, dst = work[8], other
    for k, (a, g) in enumerate(coefficients()):

        def emit(i, lo, n, cur, e, a=a, g=g, k=k, dst=dst):
            before = cur if k == 0 else step[i, pl.ds(lo, n), :]
            d = a * before + g * e
            if k < SWEEPS - 2:
                step[i, pl.ds(lo, n), :] = d
            level.put(dst, i, pl.ds(8 + lo, n), cur + d)

        scaled_residual(level, src, k + 1, level.depth - k - 1, work, emit)
        src, dst = dst, src
    return src


FINE = Level(4, 16, 32, 32, 1)
STRIP = Level(4, 16, 16, 16, 1, bases=(0, 24))
MID = Level(10, 8, 40, 16, 2, folded=True)
LOW = Level(3, 4, 16, 8, 4, folded=True)


def table(entries):
    rows, at = {}, 0
    for key, count in entries:
        rows[key] = (at, count)
        at += count
    return rows, -(-at // 8) * 8


FACE_Y, FACE_Y_SIZE = table([((f, x), 8) for x in range(16) for f in (0, 2)] + [((1, x), 9) for x in range(16)])

MID_Y = {0: 4, 1: 6, 2: 5}
HALO_X = [-1, -2, -3, -4, -5, 16, 17, 18, 19, 20]


def away(x):
    return -x if x < 0 else x - 15


SECOND_Y, SECOND_Y_SIZE = table(
    [((f, "mid", m), MID_Y[f]) for f in range(3) for m in range(8)]
    + [((f, "fine", x), 8 + (f == 1) - away(x)) for f in range(3) for x in HALO_X if away(x) < 5 + (f == 1)]
)


def side_rows(field, far):
    return -(-max(0, 10 + (field == 1) - far) // 2)


NEAR_X, NEAR_X_SIZE = table([((f, d), 8 + 2 * side_rows(f, d)) for f in range(3) for d in range(1, 9)])
FAR_X, FAR_X_SIZE = table([((f, d), 8 + 2 * side_rows(f, d)) for f in range(3) for d in range(9, 11 + (f == 1))])


def flag(condition):
    return jnp.where(condition, 1.0, 0.0).astype(F32)


def x_flags():
    i, n = lax.axis_index("gx"), lax.axis_size("gx")
    return {-2: flag(i > 1), -1: flag(i > 0), 1: flag(i < n - 1), 2: flag(i < n - 2)}


def y_flags():
    j, n = lax.axis_index("gy"), lax.axis_size("gy")
    return flag(j > 0), flag(j < n - 1)


def upward(axis, by):
    return lax.rem(lax.axis_index(axis), 2 * by) >= by


def swaps(first, second, axis, by):
    axes = ("gx", "gy")
    size = [lax.axis_size(name) for name in axes]
    dim = axes.index(axis)
    orders = []
    for sign in (1, -1):
        pairs = []
        for i in range(size[0]):
            for j in range(size[1]):
                to = [i, j]
                to[dim] += sign * by if to[dim] % (2 * by) >= by else -sign * by
                if not 0 <= to[dim] < size[dim]:
                    to = [i, j]
                    to[1 - dim] ^= 1
                pairs.append((i * size[1] + j, to[0] * size[1] + to[1]))
        orders.append(pairs)
    return lax.ppermute(first, axes, orders[0]), lax.ppermute(second, axes, orders[1])


COUNTS = (4, 5, 4)
STARTS = (0, 4, 9)


def pack_fine_x(fields):
    ends = [f[:n] for f, n in zip(fields, COUNTS)] + [f[16 - n:] for f, n in zip(fields, COUNTS)]
    first, last = jnp.concatenate(ends[:3], axis=0), jnp.concatenate(ends[3:], axis=0)
    first, last = lax.optimization_barrier((first, last))
    up = upward("gx", 1)
    return jnp.where(up, last, first), jnp.where(up, first, last)


def fine_plane(field, x, own, in_a, in_b, up):
    if 0 <= x < 16:
        return own[field][x]
    i = STARTS[field] + (x + COUNTS[field] if x < 0 else x - 16)
    return jnp.where(up, in_b[i], in_a[i]) if x < 0 else jnp.where(up, in_a[i], in_b[i])


def pick(ref, rows, key):
    at, count = rows[key]
    return ref[pl.ds(at, count), :]


def put_both(out_a, out_b, rows, key, up, higher, lower):
    at, count = rows[key]
    out_a[pl.ds(at, count), :] = jnp.where(up, higher, lower)
    out_b[pl.ds(at, count), :] = jnp.where(up, lower, higher)


def pack_face_y(b, beta, shift, out_a, out_b):
    up = upward("gy", 1)
    for field, src in enumerate((b, beta, shift)):
        for x in range(16):
            n = FACE_Y[field, x][1]
            put_both(out_a, out_b, FACE_Y, (field, x), up, src[x, pl.ds(32 - n, n), :], src[x, pl.ds(0, n), :])


def y_sides(rows, key, in_a, in_b, up):
    a, b = pick(in_a, rows, key), pick(in_b, rows, key)
    return jnp.where(up, b, a), jnp.where(up, a, b)


def pack_pairs(pair, plane, start, count):
    even = lanes(count) % 2 == 0
    e = pair[plane, pl.ds(start, count, 4), :] + pair[plane, pl.ds(start + 1, count, 4), :]
    o = pair[plane, pl.ds(start + 2, count, 4), :] + pair[plane, pl.ds(start + 3, count, 4), :]
    return jnp.where(even, e + roll(e, -1), o + roll(o, 1)) * 0.125


def pair_residual(level, src, work, pair, first):
    diag, held = work[5], {}

    def emit(i, lo, n, cur, e):
        r = e * diag[i, pl.ds(lo, n), :]
        if i % 2 == 0:
            held[0] = r
        else:
            pair[first + (i - 4) // 2, pl.ds(lo, n), :] = held[0] + r

    scaled_residual(level, src, 4, 0, work, emit)


def inner_kernel(
    b, beta, shift, xa_in, xb_in, ya_in, yb_in, x_out, packed, out_a, out_b,
    be, bb, ss, wx, wy, wym, wz, wzm, diag, inv, rhs_n, xa, xb, step, pair,
):
    near, (low, high) = x_flags(), y_flags()
    up_x, up_y = upward("gx", 1), upward("gy", 1)
    own = (b, beta, shift)
    for x in range(-5, 21):
        p = fine_plane(1, x, own, xa_in, xb_in, up_x)
        be[x + 5, 8:40, :] = p if 0 <= x < 16 else p * (near[-1] if x < 0 else near[1])
        if 0 <= x < 16:
            lo, hi = y_sides(FACE_Y, (1, x), ya_in, yb_in, up_y)
            be[x + 5, 7:8, :] = lo[8:9] * low
            be[x + 5, 40:41, :] = hi[0:1] * high
        else:
            at = SECOND_Y[1, "fine", x][1]
            put_both(out_a, out_b, SECOND_Y, (1, "fine", x), up_y, p[32 - at:32], p[0:at])
    for field, dst in ((0, bb), (2, ss)):
        for x in range(-4, 20):
            if 0 <= x < 16:
                continue
            p = fine_plane(field, x, own, xa_in, xb_in, up_x)
            dst[x + 4] = p
            at = SECOND_Y[field, "fine", x][1]
            put_both(out_a, out_b, SECOND_Y, (field, "fine", x), up_y, p[32 - at:32], p[0:at])
    work = (wx, wy, wym, wz, wzm, diag, inv, rhs_n, xa)

    def plane_of(src, halo):
        return lambda i, at: src[i - 4] if 4 <= i < 20 else halo[i]

    build(FINE, 1.0, be, plane_of(b, bb), plane_of(shift, ss), work)
    x = smooth(FINE, work, xb, step)
    for m in range(8):
        pair[m] = beta[2 * m] + beta[2 * m + 1]
        pair[m + 8] = shift[2 * m] + shift[2 * m + 1]
    pair_residual(FINE, x, work, pair, 16)
    for m in range(8):
        packed[1, m] = pack_pairs(pair, m, 0, 8)
        packed[2, m] = pack_pairs(pair, m + 8, 0, 8)
        packed[0, m] = pack_pairs(pair, m + 16, 0, 8)
    for m in range(8):
        for field, skip in ((0, 1), (1, 0), (2, 0)):
            n = MID_Y[field]
            higher = packed[field, m, pl.ds(8 - skip - n, n), :]
            lower = packed[field, m, pl.ds(skip, n), :]
            put_both(out_a, out_b, SECOND_Y, (field, "mid", m), up_y, higher, lower)
    for i in range(16):
        x_out[i] = x[i + 4, pl.ds(8, 32), :]


def edge_kernel(
    b, beta, shift, xa_in, xb_in, ya_in, yb_in, packed, ya2, yb2,
    x_out, ext, near_a, near_b, far_a, far_b,
    be, bb, ss, wx, wy, wym, wz, wzm, diag, inv, rhs_n, xa, xb, step, pair,
):
    near, (low, high) = x_flags(), y_flags()
    up_x, up_y = upward("gx", 1), upward("gy", 1)
    own = (b, beta, shift)

    def sides(field, x):
        if 0 <= x < 16:
            return y_sides(FACE_Y, (field, x), ya_in, yb_in, up_y)
        return y_sides(SECOND_Y, (field, "fine", x), ya2, yb2, up_y)

    for x in range(-5, 21):
        p = fine_plane(1, x, own, xa_in, xb_in, up_x)
        lo, hi = sides(1, x)
        n = lo.shape[0]
        f = 1.0 if 0 <= x < 16 else near[-1] if x < 0 else near[1]
        if not 0 <= x < 16:
            p = p * f
        be[x + 5, 16:25, :] = p[0:9]
        be[x + 5, 31:40, :] = p[23:32]
        be[x + 5, pl.ds(16 - n, n), :] = lo * (low * f)
        be[x + 5, pl.ds(40, n), :] = hi * (high * f)
    for field, dst in ((0, bb), (2, ss)):
        for x in range(-4, 20):
            p = fine_plane(field, x, own, xa_in, xb_in, up_x)
            lo, hi = sides(field, x)
            n = lo.shape[0]
            dst[x + 4, 8:16, :] = p[0:8]
            dst[x + 4, 24:32, :] = p[24:32]
            dst[x + 4, pl.ds(8 - n, n), :] = lo
            dst[x + 4, pl.ds(32, n), :] = hi
    work = (wx, wy, wym, wz, wzm, diag, inv, rhs_n, xa)
    build(STRIP, 1.0, be, lambda i, at: bb[i, at, :], lambda i, at: ss[i, at, :], work)
    x = smooth(STRIP, work, xb, step)
    pair_residual(STRIP, x, work, pair, 0)
    for m in range(8):
        ext[0, m, 7:13, :] = packed[0, m, 1:7, :]
        ext[0, m, 5:7, :] = pack_pairs(pair, m, 4, 2)
        ext[0, m, 13:15, :] = pack_pairs(pair, m, 28, 2)
        for field, skip, scale in ((0, 1, (None, None)), (1, 0, (low, high)), (2, 0, (None, None))):
            if field:
                ext[field, m, 6:14, :] = packed[field, m]
            n = MID_Y[field]
            lo, hi = y_sides(SECOND_Y, (field, "mid", m), ya2, yb2, up_y)
            ext[field, m, pl.ds(6 - skip - n, n), :] = lo if scale[0] is None else lo * scale[0]
            ext[field, m, pl.ds(14 + skip, n), :] = hi if scale[1] is None else hi * scale[1]
    up2 = upward("gx", 2)
    for rows, up, a, c, first in ((NEAR_X, up_x, near_a, near_b, 1), (FAR_X, up2, far_a, far_b, 9)):
        for field, d in rows:
            n = side_rows(field, d)
            at = pl.ds(6 - n, 8 + 2 * n)
            higher, lower = ext[field, 8 - d + (first - 1), at, :], ext[field, d - first, at, :]
            put_both(a, c, rows, (field, d), up, higher, lower)
    for i in range(16):
        x_out[i, 0:4, :] = x[i + 4, pl.ds(16, 4), :]
        x_out[i, 4:8, :] = x[i + 4, pl.ds(36, 4), :]


def coarse_kernel(
    x_fine, x_edge, ext, near_a, near_b, far_a, far_b, out, mid_out,
    be, bb, ss, wx, wy, wym, wz, wzm, diag, inv, rhs_n, xa, xb, step, pair,
    be2, ss2, wx2, wy2, wym2, wz2, wzm2, diag2, inv2, rhs_n2, xa2, xb2, step2,
    rep_mid, rep_fine, mids,
):
    flags = x_flags()
    up, up2 = upward("gx", 1), upward("gx", 2)

    def spread(dst, plane, start, a, b):
        n = a.shape[0]
        even = lanes(n) % 2 == 0
        dst[plane, pl.ds(start, n, 2), :] = jnp.where(even, a, roll(b, 1))
        dst[plane, pl.ds(start + 1, n, 2), :] = jnp.where(even, roll(a, -1), b)

    def gather(field, d):
        if d <= 0:
            n = side_rows(field, 0)
            at = pl.ds(6 - n, 8 + 2 * n)
            return ext[field, -d, at, :], ext[field, 7 + d, at, :]
        rows, a, c, u = (NEAR_X, near_a, near_b, up) if d <= 8 else (FAR_X, far_a, far_b, up2)
        a, c = pick(a, rows, (field, d)), pick(c, rows, (field, d))
        lower, higher = jnp.where(u, c, a), jnp.where(u, a, c)
        if field == 1:
            hop = 1 if d <= 8 else 2
            return lower * flags[-hop], higher * flags[hop]
        return lower, higher

    for field, dst, first in ((1, be, 20), (0, bb, 12), (2, ss, 12)):
        reach = 11 if field == 1 else 10
        for i in range(reach + 4):
            a, b = gather(field, reach - i)
            spread(dst, i, first - (a.shape[0] - 8), a, b)
    be[15, pl.ds(8, 40), :] = swap_lanes(be[14, pl.ds(8, 40), :])
    work = (wx, wy, wym, wz, wzm, diag, inv, rhs_n, xa)
    build(MID, 0.25, be, lambda i, at: bb[i, at, :], lambda i, at: ss[i, at, :], work)
    x1 = smooth(MID, work, xb, step)

    low_pair = lanes(16) % 4 < 2

    def down_sample(plane):
        s = pair[plane, pl.ds(4, 16, 2), :] + pair[plane, pl.ds(5, 16, 2), :]
        return (s + jnp.where(low_pair, roll(s, -2), roll(s, 2))) * 0.125

    for m in range(6):
        pair[m] = be[2 * m + 3, pl.ds(8, 40), :] + be[2 * m + 4, pl.ds(8, 40), :]
    for m in range(5):
        pair[6 + m] = ss[2 * m + 4] + ss[2 * m + 5]
    for m in range(6):
        be2[m, 8:24, :] = down_sample(m)
    be2[6, 8:24, :] = swap_lanes(be2[5, 8:24, :])
    for m in range(5):
        ss2[m] = down_sample(6 + m)
    held = {}

    def emit(i, lo, n, cur, e):
        r = e * diag[i, pl.ds(lo, n), :]
        if i % 2 == 0:
            held[0] = lo, n, r
        else:
            lo0, n0, r0 = held[0]
            at, end = max(lo, lo0), min(lo + n, lo0 + n0)
            total = r0[at - lo0:end - lo0] + r[at - lo:end - lo]
            pair[11 + (i - 4) // 2, pl.ds(at, end - at), :] = total

    scaled_residual(MID, x1, 4, 6, work, emit)
    work2 = (wx2, wy2, wym2, wz2, wzm2, diag2, inv2, rhs_n2, xa2)
    build(LOW, 0.0625, be2, lambda i, at: down_sample(11 + i), lambda i, at: ss2[i, at, :], work2)
    x2 = smooth(LOW, work2, xb2, step2)

    for m in range(2):
        low_x = x2[m + 3, pl.ds(12, 8), :]
        rep_mid[m, pl.ds(0, 8, 2), :] = low_x
        rep_mid[m, pl.ds(1, 8, 2), :] = low_x
    even = lanes(16) % 2 == 0
    for m in range(4):
        both = x1[m + 10, pl.ds(20, 16), :] + rep_mid[m // 2]
        for x, mid in (
            (m, jnp.where(even, both, roll(both, 1))),
            (7 - m, jnp.where(even, roll(both, -1), both)),
        ):
            mids[pl.ds(16 * x, 16), :] = mid
            rep_fine[x, pl.ds(0, 16, 2), :] = mid
            rep_fine[x, pl.ds(1, 16, 2), :] = mid
    for i in range(16):
        out[i, 4:28, :] = x_fine[i, 4:28, :] + rep_fine[i // 2, 4:28, :]
        out[i, 0:4, :] = x_edge[i, 0:4, :] + rep_fine[i // 2, 0:4, :]
        out[i, 28:32, :] = x_edge[i, 4:8, :] + rep_fine[i // 2, 28:32, :]
    row = lax.broadcasted_iota(jnp.int32, (128, 64), 0)
    col = lax.broadcasted_iota(jnp.int32, (128, 64), 1)
    even_lanes = jnp.where(row == 2 * col, 1.0, 0.0).astype(F32)
    compact = jnp.dot(mids[...], even_lanes, precision=lax.Precision.HIGHEST, preferred_element_type=F32)
    for m in range(8):
        mid_out[m] = compact[16 * m:16 * m + 16]


def vmem(*shape):
    return pltpu.VMEM(shape, F32)


def call(kernel, ins, outs, scratch=(), limit=24 * 2**20, space=pltpu.VMEM):
    return pl.pallas_call(
        kernel,
        out_shape=[jax.ShapeDtypeStruct(s, F32) for s in outs],
        in_specs=[pl.BlockSpec(memory_space=space)] * len(ins),
        out_specs=[pl.BlockSpec(memory_space=pltpu.VMEM)] * len(outs),
        scratch_shapes=list(scratch),
        compiler_params=pltpu.CompilerParams(vmem_limit_bytes=limit),
    )(*ins)


def work_scratch(planes, rows):
    flat = [vmem(planes, rows, 128) for _ in range(8)]
    return flat + [vmem(planes + 1, rows + 16, 128) for _ in range(2)] + [vmem(planes, rows, 128)]


def level_scratch(planes, rows):
    return [vmem(planes + 2, rows + 16, 128)] + [vmem(planes, rows, 128)] * 2 + work_scratch(planes, rows)


def local(b, beta, shift):
    fields = (b, beta, shift)
    a, c = pack_fine_x(fields)
    xs = swaps(a, c, "gx", 1)
    a, c = call(pack_face_y, fields, [(FACE_Y_SIZE, 128)] * 2)
    ys = swaps(a, c, "gy", 1)
    x_fine, packed, a, c = call(
        inner_kernel,
        (*fields, *xs, *ys),
        [(16, 32, 128), (3, 8, 8, 128)] + [(SECOND_Y_SIZE, 128)] * 2,
        level_scratch(FINE.planes, 32) + [vmem(24, 32, 128)],
    )
    second = swaps(a, c, "gy", 1)
    x_edge, ext, near_a, near_b, far_a, far_b = call(
        edge_kernel,
        (*fields, *xs, *ys, packed, *second),
        [(16, 8, 128), (3, 8, 24, 128)] + [(NEAR_X_SIZE, 128)] * 2 + [(FAR_X_SIZE, 128)] * 2,
        level_scratch(STRIP.planes, 40) + [vmem(8, 40, 128)],
    )
    around = (*swaps(near_a, near_b, "gx", 1), *swaps(far_a, far_b, "gx", 2))
    low = [vmem(LOW.planes + 2, 32, 128), vmem(LOW.planes, 16, 128)] + work_scratch(LOW.planes, 16)
    return tuple(call(
        coarse_kernel,
        (x_fine, x_edge, ext, *around),
        [(16, 32, 128), (8, 16, 64)],
        level_scratch(MID.planes, 40) + [vmem(16, 40, 128)] + low
        + [vmem(2, 16, 128), vmem(8, 32, 128), vmem(128, 128)],
    ))


def solution(mesh):
    placed = P("gx", "gy", None)
    return jax.shard_map(
        local, mesh=mesh, in_specs=(placed,) * 3, out_specs=(placed, placed), check_vma=False
    )
```

```python
import jax
import jax.numpy as jnp
from jax import lax
from jax.experimental import pallas as pl
from jax.experimental.pallas import tpu as pltpu
from jax.sharding import PartitionSpec as P

SWEEPS = 4
THETA, DELTA = 1.15, 0.85
SIGMA = THETA / DELTA
F32 = jnp.float32


def coefficients():
    rho, out = 1.0 / SIGMA, []
    for _ in range(SWEEPS - 1):
        new = 1.0 / (2.0 * SIGMA - rho)
        out.append((new * rho, 2.0 * new / DELTA))
        rho = new
    return out


def lanes(rows):
    return lax.broadcasted_iota(jnp.int32, (rows, 128), 1)


def roll(value, shift):
    return pltpu.roll(value, shift % 128, 1)


class Level:
    def __init__(self, depth, own_planes, rows, own_rows, rep, folded=False, bases=(0,)):
        self.bases = bases
        self.depth, self.own, self.rep, self.folded = depth, own_planes, rep, folded
        self.planes = depth + own_planes // 2 if folded else own_planes + 2 * depth
        self.rows, self.first_row, self.own_rows = rows, (rows - own_rows) // 2, own_rows

    def cut(self, k):
        return k, self.planes - (0 if self.folded else k)

    def span(self, plane, reach):
        x = plane - self.depth
        far = max(0, -x) if self.folded else max(0, -x, x - self.own + 1)
        side = max(0, reach - far)
        lo = max(0, self.first_row - side) // 8 * 8
        hi = min(self.rows, -(-(self.first_row + self.own_rows + side) // 8) * 8)
        return lo, hi - lo

    def put(self, dst, i, at, value):
        dst[i, at, :] = value
        if self.folded and i == self.planes - 1:
            dst[i + 1, at, :] = swap_lanes(value)


def swap_lanes(value):
    return jnp.where(lanes(value.shape[0]) % 2 == 0, roll(value, -1), roll(value, 1))


def build(level, scale, beta, rhs, shift, work, planes=None):
    wx, wy, wym, wz, wzm, diag, inv, rhs_n, start = work
    rep, half, last_span = level.rep, 0.5 * scale, None
    planes = range(level.planes) if planes is None else planes
    for base, i in [(base, i) for base in level.bases for i in planes]:
        lo, n = level.span(i, level.depth)
        lo += base
        if (lo, n, i) != last_span:
            prev, cur = beta[i, pl.ds(8 + lo, n), :], beta[i + 1, pl.ds(8 + lo, n), :]
            wx_prev = half * (prev + cur)
            if i:
                wx[i - 1, pl.ds(lo, n), :] = wx_prev
            lane = lanes(n)
            first, last = lane < rep, lane >= 128 - rep
        last_span = (lo, n, i + 1)
        at = pl.ds(lo, n)
        nxt = beta[i + 2, pl.ds(8 + lo, n), :]
        wx_next = half * (cur + nxt)
        w_up = half * (cur + beta[i + 1, pl.ds(9 + lo, n), :])
        w_down = half * (cur + beta[i + 1, pl.ds(7 + lo, n), :])
        w_right = half * (cur + jnp.where(last, 0.0, roll(cur, -rep)))
        w_left = half * (cur + jnp.where(first, 0.0, roll(cur, rep)))
        d = shift(i, at) + (wx_prev + wx_next + w_up + w_down + w_right + w_left)
        iv = jnp.where(cur > 0.0, 1.0 / d, 0.0)
        c = rhs(i, at) * iv
        wx[i, at, :] = wx_next
        wy[i, at, :] = w_up
        wym[i, at, :] = w_down
        wz[i, at, :] = jnp.where(last, 0.0, w_right)
        wzm[i, at, :] = jnp.where(first, 0.0, w_left)
        diag[i, at, :] = d
        inv[i, at, :] = iv
        rhs_n[i, at, :] = c
        level.put(start, i, pl.ds(8 + lo, n), c * (1.0 / THETA))
        cur, wx_prev = nxt, wx_next


def scaled_residual(level, src, planes, reach, work, emit):
    wx, wy, wym, wz, wzm, _, inv, rhs_n, _ = work
    rep, last_span = level.rep, None
    for base, i in [(base, i) for base in level.bases for i in planes]:
        lo, n = level.span(i, reach)
        lo += base
        at, dom = pl.ds(lo, n), pl.ds(8 + lo, n)
        if (lo, n, i) != last_span:
            prev, cur, wx_prev = src[i - 1, dom, :], src[i, dom, :], wx[i - 1, at, :]
        last_span = (lo, n, i + 1)
        nxt, wx_next = src[i + 1, dom, :], wx[i, at, :]
        t = wx_next * nxt + wx_prev * prev
        t = t + wy[i, at, :] * src[i, pl.ds(9 + lo, n), :] + wym[i, at, :] * src[i, pl.ds(7 + lo, n), :]
        t = t + wz[i, at, :] * roll(cur, -rep) + wzm[i, at, :] * roll(cur, rep)
        emit(i, lo, n, cur, rhs_n[i, at, :] + inv[i, at, :] * t - cur)
        prev, cur, wx_prev = cur, nxt, wx_next


def sweeps(level, work, fields, step, planes):
    for k, (a, g) in enumerate(coefficients()):

        def emit(i, lo, n, cur, e, a=a, g=g, k=k, dst=fields[k + 1]):
            before = cur if k == 0 else step[i, pl.ds(lo, n), :]
            d = a * before + g * e
            if k < SWEEPS - 2:
                step[i, pl.ds(lo, n), :] = d
            level.put(dst, i, pl.ds(8 + lo, n), cur + d)

        scaled_residual(level, fields[k], planes(k + 1), level.depth - k - 1, work, emit)
    return fields[-1]


def smooth(level, work, other, step):
    fields = (work[8], other) * 2
    return sweeps(level, work, fields, step, lambda k: range(*level.cut(k)))


class Split:
    def __init__(self, inner, outer, first, last):
        self.inner, self.outer, self.first, self.last = inner, outer, first, last

    def __getitem__(self, at):
        return (self.inner if self.first <= at[0] <= self.last else self.outer)[at]

    def __setitem__(self, at, value):
        if not self.first <= at[0] <= self.last:
            self.outer[at] = value


FINE = Level(4, 16, 32, 32, 1)
STRIP = Level(4, 16, 16, 16, 1, bases=(0, 24))
MID = Level(10, 8, 40, 16, 2, folded=True)
LOW = Level(3, 4, 16, 8, 4, folded=True)


def table(entries):
    rows, at = {}, 0
    for key, count in entries:
        rows[key] = (at, count)
        at += count
    return rows, -(-at // 8) * 8


FACE_Y, FACE_Y_SIZE = table([((f, x), 8) for x in range(16) for f in (0, 2)] + [((1, x), 9) for x in range(16)])

MID_Y = {0: 4, 1: 6, 2: 5}
HALO_X = [-1, -2, -3, -4, -5, 16, 17, 18, 19, 20]


def away(x):
    return -x if x < 0 else x - 15


SECOND_Y, SECOND_Y_SIZE = table(
    [((f, "mid", m), MID_Y[f]) for f in range(3) for m in range(8)]
    + [((f, "fine", x), 8 + (f == 1) - away(x)) for f in range(3) for x in HALO_X if away(x) < 5 + (f == 1)]
)


def side_rows(field, far):
    return -(-max(0, 10 + (field == 1) - far) // 2)


NEAR_X, NEAR_X_SIZE = table([((f, d), 8 + 2 * side_rows(f, d)) for f in range(3) for d in range(1, 9)])
FAR_X, FAR_X_SIZE = table([((f, d), 8 + 2 * side_rows(f, d)) for f in range(3) for d in range(9, 11 + (f == 1))])


def flag(condition):
    return jnp.where(condition, 1.0, 0.0).astype(F32)


def x_flags():
    i, n = lax.axis_index("gx"), lax.axis_size("gx")
    return {-2: flag(i > 1), -1: flag(i > 0), 1: flag(i < n - 1), 2: flag(i < n - 2)}


def y_flags():
    j, n = lax.axis_index("gy"), lax.axis_size("gy")
    return flag(j > 0), flag(j < n - 1)


def upward(axis, by):
    return lax.rem(lax.axis_index(axis), 2 * by) >= by


def swaps(first, second, axis, by):
    axes = ("gx", "gy")
    size = [lax.axis_size(name) for name in axes]
    dim = axes.index(axis)
    orders = []
    for sign in (1, -1):
        pairs = []
        for i in range(size[0]):
            for j in range(size[1]):
                to = [i, j]
                to[dim] += sign * by if to[dim] % (2 * by) >= by else -sign * by
                if not 0 <= to[dim] < size[dim]:
                    to = [i, j]
                    to[1 - dim] ^= 1
                pairs.append((i * size[1] + j, to[0] * size[1] + to[1]))
        orders.append(pairs)
    return lax.ppermute(first, axes, orders[0]), lax.ppermute(second, axes, orders[1])


COUNTS = (4, 5, 4)
STARTS = (0, 4, 9)


def pack_fine_x(fields):
    ends = [f[:n] for f, n in zip(fields, COUNTS)] + [f[16 - n:] for f, n in zip(fields, COUNTS)]
    first, last = jnp.concatenate(ends[:3], axis=0), jnp.concatenate(ends[3:], axis=0)
    first, last = lax.optimization_barrier((first, last))
    up = upward("gx", 1)
    return jnp.where(up, last, first), jnp.where(up, first, last)


def fine_plane(field, x, own, in_a, in_b, up):
    if 0 <= x < 16:
        return own[field][x]
    i = STARTS[field] + (x + COUNTS[field] if x < 0 else x - 16)
    return jnp.where(up, in_b[i], in_a[i]) if x < 0 else jnp.where(up, in_a[i], in_b[i])


def pick(ref, rows, key):
    at, count = rows[key]
    return ref[pl.ds(at, count), :]


def put_both(out_a, out_b, rows, key, up, higher, lower):
    at, count = rows[key]
    out_a[pl.ds(at, count), :] = jnp.where(up, higher, lower)
    out_b[pl.ds(at, count), :] = jnp.where(up, lower, higher)


def pack_face_y(b, beta, shift, out_a, out_b):
    up = upward("gy", 1)
    for field, src in enumerate((b, beta, shift)):
        for x in range(16):
            n = FACE_Y[field, x][1]
            put_both(out_a, out_b, FACE_Y, (field, x), up, src[x, pl.ds(32 - n, n), :], src[x, pl.ds(0, n), :])


def y_sides(rows, key, in_a, in_b, up):
    a, b = pick(in_a, rows, key), pick(in_b, rows, key)
    return jnp.where(up, b, a), jnp.where(up, a, b)


def pack_pairs(pair, plane, start, count):
    even = lanes(count) % 2 == 0
    e = pair[plane, pl.ds(start, count, 4), :] + pair[plane, pl.ds(start + 1, count, 4), :]
    o = pair[plane, pl.ds(start + 2, count, 4), :] + pair[plane, pl.ds(start + 3, count, 4), :]
    return jnp.where(even, e + roll(e, -1), o + roll(o, 1)) * 0.125


def pair_residual(level, src, work, pair, first, planes):
    diag, held = work[5], {}

    def emit(i, lo, n, cur, e):
        r = e * diag[i, pl.ds(lo, n), :]
        if i % 2 == 0:
            held[0] = r
        else:
            pair[first + (i - 4) // 2, pl.ds(lo, n), :] = held[0] + r

    scaled_residual(level, src, planes, 0, work, emit)


def inner_kernel(
    b, beta, shift, xa_in, xb_in, ya_in, yb_in, x_out, packed, out_a, out_b,
    be, bb, ss, wx, wy, wym, wz, wzm, diag, inv, rhs_n, xa, xb, step, pair,
):
    near, (low, high) = x_flags(), y_flags()
    up_x, up_y = upward("gx", 1), upward("gy", 1)
    own = (b, beta, shift)
    for x in range(-5, 21):
        p = fine_plane(1, x, own, xa_in, xb_in, up_x)
        be[x + 5, 8:40, :] = p if 0 <= x < 16 else p * (near[-1] if x < 0 else near[1])
        if 0 <= x < 16:
            lo, hi = y_sides(FACE_Y, (1, x), ya_in, yb_in, up_y)
            be[x + 5, 7:8, :] = lo[8:9] * low
            be[x + 5, 40:41, :] = hi[0:1] * high
        else:
            at = SECOND_Y[1, "fine", x][1]
            put_both(out_a, out_b, SECOND_Y, (1, "fine", x), up_y, p[32 - at:32], p[0:at])
    for field, dst in ((0, bb), (2, ss)):
        for x in range(-4, 20):
            if 0 <= x < 16:
                continue
            p = fine_plane(field, x, own, xa_in, xb_in, up_x)
            dst[x + 4] = p
            at = SECOND_Y[field, "fine", x][1]
            put_both(out_a, out_b, SECOND_Y, (field, "fine", x), up_y, p[32 - at:32], p[0:at])
    work = (wx, wy, wym, wz, wzm, diag, inv, rhs_n, xa)

    def plane_of(src, halo):
        return lambda i, at: src[i - 4] if 4 <= i < 20 else halo[i]

    build(FINE, 1.0, be, plane_of(b, bb), plane_of(shift, ss), work)
    x = smooth(FINE, work, xb, step)
    for m in range(8):
        pair[m] = beta[2 * m] + beta[2 * m + 1]
        pair[m + 8] = shift[2 * m] + shift[2 * m + 1]
    pair_residual(FINE, x, work, pair, 16, range(4, 20))
    for m in range(8):
        packed[1, m] = pack_pairs(pair, m, 0, 8)
        packed[2, m] = pack_pairs(pair, m + 8, 0, 8)
        packed[0, m] = pack_pairs(pair, m + 16, 0, 8)
    for m in range(8):
        for field, skip in ((0, 1), (1, 0), (2, 0)):
            n = MID_Y[field]
            higher = packed[field, m, pl.ds(8 - skip - n, n), :]
            lower = packed[field, m, pl.ds(skip, n), :]
            put_both(out_a, out_b, SECOND_Y, (field, "mid", m), up_y, higher, lower)
    for i in range(16):
        x_out[i] = x[i + 4, pl.ds(8, 32), :]


def INNER(k):
    return range(5 + k, 19 - k)


def strip_kernel(
    b, beta, shift, ya_in, yb_in,
    wx, wy, wym, wz, wzm, diag, inv, rhs_n, x0, x1, x2, x3, step, pair, be, bb, ss,
):
    (low, high), up_y = y_flags(), upward("gy", 1)
    for x in range(16):
        lo, hi = y_sides(FACE_Y, (1, x), ya_in, yb_in, up_y)
        be[x + 5, 16:25, :] = beta[x, 0:9, :]
        be[x + 5, 31:40, :] = beta[x, 23:32, :]
        be[x + 5, 7:16, :] = lo * low
        be[x + 5, 40:49, :] = hi * high
    for field, src, dst in ((0, b, bb), (2, shift, ss)):
        for x in range(1, 15):
            lo, hi = y_sides(FACE_Y, (field, x), ya_in, yb_in, up_y)
            dst[x + 4, 8:16, :] = src[x, 0:8, :]
            dst[x + 4, 24:32, :] = src[x, 24:32, :]
            dst[x + 4, 0:8, :] = lo
            dst[x + 4, 32:40, :] = hi
    work = (wx, wy, wym, wz, wzm, diag, inv, rhs_n, x0)
    build(STRIP, 1.0, be, lambda i, at: bb[i, at, :], lambda i, at: ss[i, at, :], work, INNER(0))
    sweeps(STRIP, work, (x0, x1, x2, x3), step, INNER)
    pair_residual(STRIP, x3, work, pair, 0, range(10, 14))


def edge_kernel(
    b, beta, shift, xa_in, xb_in, ya_in, yb_in, packed, ya2, yb2,
    i_wx, i_wy, i_wym, i_wz, i_wzm, i_diag, i_inv, i_rhs_n, i_x0, i_x1, i_x2, i_x3, i_step, i_pair,
    x_out, ext, near_a, near_b, far_a, far_b,
    be, bb, ss, wx, wy, wym, wz, wzm, diag, inv, rhs_n, x0, x1, step, x2, x3, pair,
):
    near, (low, high) = x_flags(), y_flags()
    up_x, up_y = upward("gx", 1), upward("gy", 1)
    own = (b, beta, shift)

    def sides(field, x):
        if 0 <= x < 16:
            return y_sides(FACE_Y, (field, x), ya_in, yb_in, up_y)
        return y_sides(SECOND_Y, (field, "fine", x), ya2, yb2, up_y)

    for x in [*range(-5, 2), *range(14, 21)]:
        p = fine_plane(1, x, own, xa_in, xb_in, up_x)
        lo, hi = sides(1, x)
        n = lo.shape[0]
        f = 1.0 if 0 <= x < 16 else near[-1] if x < 0 else near[1]
        if not 0 <= x < 16:
            p = p * f
        be[x + 5, 16:25, :] = p[0:9]
        be[x + 5, 31:40, :] = p[23:32]
        be[x + 5, pl.ds(16 - n, n), :] = lo * (low * f)
        be[x + 5, pl.ds(40, n), :] = hi * (high * f)
    for field, dst in ((0, bb), (2, ss)):
        for x in [*range(-4, 1), *range(15, 20)]:
            p = fine_plane(field, x, own, xa_in, xb_in, up_x)
            lo, hi = sides(field, x)
            n = lo.shape[0]
            dst[x + 4, 8:16, :] = p[0:8]
            dst[x + 4, 24:32, :] = p[24:32]
            dst[x + 4, pl.ds(8 - n, n), :] = lo
            dst[x + 4, pl.ds(32, n), :] = hi
    inner = (i_wx, i_wy, i_wym, i_wz, i_wzm, i_diag, i_inv, i_rhs_n, i_x0)
    outer = (wx, wy, wym, wz, wzm, diag, inv, rhs_n, x0)
    work = tuple(Split(i, o, 5, 18) for i, o in zip(inner, outer))
    fields = [work[8]] + [
        Split(i, o, INNER(k)[0], INNER(k)[-1]) for k, i, o in ((1, i_x1, x1), (2, i_x2, x2), (3, i_x3, x3))
    ]

    def rest(k):
        return [i for i in range(k, 24 - k) if i not in INNER(k)]

    class Step:
        def __getitem__(self, at):
            return (i_step if at[0] in INNER(1) and at[0] not in seen else step)[at]

        def __setitem__(self, at, value):
            step[at] = value
            if at[1].start >= STRIP.bases[-1]:
                seen.add(at[0])

    seen = set()
    build(STRIP, 1.0, be, lambda i, at: bb[i, at, :], lambda i, at: ss[i, at, :], work, rest(0))
    x = sweeps(STRIP, work, fields, Step(), rest)
    both = Split(i_pair, pair, 3, 4)
    pair_residual(STRIP, x, work, both, 0, [*range(4, 10), *range(14, 20)])
    pair = both
    for m in range(8):
        ext[0, m, 7:13, :] = packed[0, m, 1:7, :]
        ext[0, m, 5:7, :] = pack_pairs(pair, m, 4, 2)
        ext[0, m, 13:15, :] = pack_pairs(pair, m, 28, 2)
        for field, skip, scale in ((0, 1, (None, None)), (1, 0, (low, high)), (2, 0, (None, None))):
            if field:
                ext[field, m, 6:14, :] = packed[field, m]
            n = MID_Y[field]
            lo, hi = y_sides(SECOND_Y, (field, "mid", m), ya2, yb2, up_y)
            ext[field, m, pl.ds(6 - skip - n, n), :] = lo if scale[0] is None else lo * scale[0]
            ext[field, m, pl.ds(14 + skip, n), :] = hi if scale[1] is None else hi * scale[1]
    up2 = upward("gx", 2)
    for rows, up, a, c, first in ((NEAR_X, up_x, near_a, near_b, 1), (FAR_X, up2, far_a, far_b, 9)):
        for field, d in rows:
            n = side_rows(field, d)
            at = pl.ds(6 - n, 8 + 2 * n)
            higher, lower = ext[field, 8 - d + (first - 1), at, :], ext[field, d - first, at, :]
            put_both(a, c, rows, (field, d), up, higher, lower)
    for i in range(16):
        x_out[i, 0:4, :] = x[i + 4, pl.ds(16, 4), :]
        x_out[i, 4:8, :] = x[i + 4, pl.ds(36, 4), :]


def coarse_kernel(
    x_fine, x_edge, ext, near_a, near_b, far_a, far_b, out, mid_out,
    be, bb, ss, wx, wy, wym, wz, wzm, diag, inv, rhs_n, xa, xb, step, pair,
    be2, ss2, wx2, wy2, wym2, wz2, wzm2, diag2, inv2, rhs_n2, xa2, xb2, step2,
    rep_mid, rep_fine, mids,
):
    flags = x_flags()
    up, up2 = upward("gx", 1), upward("gx", 2)

    def spread(dst, plane, start, a, b):
        n = a.shape[0]
        even = lanes(n) % 2 == 0
        dst[plane, pl.ds(start, n, 2), :] = jnp.where(even, a, roll(b, 1))
        dst[plane, pl.ds(start + 1, n, 2), :] = jnp.where(even, roll(a, -1), b)

    def gather(field, d):
        if d <= 0:
            n = side_rows(field, 0)
            at = pl.ds(6 - n, 8 + 2 * n)
            return ext[field, -d, at, :], ext[field, 7 + d, at, :]
        rows, a, c, u = (NEAR_X, near_a, near_b, up) if d <= 8 else (FAR_X, far_a, far_b, up2)
        a, c = pick(a, rows, (field, d)), pick(c, rows, (field, d))
        lower, higher = jnp.where(u, c, a), jnp.where(u, a, c)
        if field == 1:
            hop = 1 if d <= 8 else 2
            return lower * flags[-hop], higher * flags[hop]
        return lower, higher

    for field, dst, first in ((1, be, 20), (0, bb, 12), (2, ss, 12)):
        reach = 11 if field == 1 else 10
        for i in range(reach + 4):
            a, b = gather(field, reach - i)
            spread(dst, i, first - (a.shape[0] - 8), a, b)
    be[15, pl.ds(8, 40), :] = swap_lanes(be[14, pl.ds(8, 40), :])
    work = (wx, wy, wym, wz, wzm, diag, inv, rhs_n, xa)
    build(MID, 0.25, be, lambda i, at: bb[i, at, :], lambda i, at: ss[i, at, :], work)
    x1 = smooth(MID, work, xb, step)

    low_pair = lanes(16) % 4 < 2

    def down_sample(plane):
        s = pair[plane, pl.ds(4, 16, 2), :] + pair[plane, pl.ds(5, 16, 2), :]
        return (s + jnp.where(low_pair, roll(s, -2), roll(s, 2))) * 0.125

    for m in range(6):
        pair[m] = be[2 * m + 3, pl.ds(8, 40), :] + be[2 * m + 4, pl.ds(8, 40), :]
    for m in range(5):
        pair[6 + m] = ss[2 * m + 4] + ss[2 * m + 5]
    for m in range(6):
        be2[m, 8:24, :] = down_sample(m)
    be2[6, 8:24, :] = swap_lanes(be2[5, 8:24, :])
    for m in range(5):
        ss2[m] = down_sample(6 + m)
    held = {}

    def emit(i, lo, n, cur, e):
        r = e * diag[i, pl.ds(lo, n), :]
        if i % 2 == 0:
            held[0] = lo, n, r
        else:
            lo0, n0, r0 = held[0]
            at, end = max(lo, lo0), min(lo + n, lo0 + n0)
            total = r0[at - lo0:end - lo0] + r[at - lo:end - lo]
            pair[11 + (i - 4) // 2, pl.ds(at, end - at), :] = total

    scaled_residual(MID, x1, range(4, 14), 6, work, emit)
    work2 = (wx2, wy2, wym2, wz2, wzm2, diag2, inv2, rhs_n2, xa2)
    build(LOW, 0.0625, be2, lambda i, at: down_sample(11 + i), lambda i, at: ss2[i, at, :], work2)
    x2 = smooth(LOW, work2, xb2, step2)

    for m in range(2):
        low_x = x2[m + 3, pl.ds(12, 8), :]
        rep_mid[m, pl.ds(0, 8, 2), :] = low_x
        rep_mid[m, pl.ds(1, 8, 2), :] = low_x
    even = lanes(16) % 2 == 0
    for m in range(4):
        both = x1[m + 10, pl.ds(20, 16), :] + rep_mid[m // 2]
        for x, mid in (
            (m, jnp.where(even, both, roll(both, 1))),
            (7 - m, jnp.where(even, roll(both, -1), both)),
        ):
            mids[pl.ds(16 * x, 16), :] = mid
            rep_fine[x, pl.ds(0, 16, 2), :] = mid
            rep_fine[x, pl.ds(1, 16, 2), :] = mid
    for i in range(16):
        out[i, 4:28, :] = x_fine[i, 4:28, :] + rep_fine[i // 2, 4:28, :]
        out[i, 0:4, :] = x_edge[i, 0:4, :] + rep_fine[i // 2, 0:4, :]
        out[i, 28:32, :] = x_edge[i, 4:8, :] + rep_fine[i // 2, 28:32, :]
    row = lax.broadcasted_iota(jnp.int32, (128, 64), 0)
    col = lax.broadcasted_iota(jnp.int32, (128, 64), 1)
    even_lanes = jnp.where(row == 2 * col, 1.0, 0.0).astype(F32)
    compact = jnp.dot(mids[...], even_lanes, precision=lax.Precision.HIGHEST, preferred_element_type=F32)
    for m in range(8):
        mid_out[m] = compact[16 * m:16 * m + 16]


def vmem(*shape):
    return pltpu.VMEM(shape, F32)


def call(kernel, ins, outs, scratch=(), limit=24 * 2**20, space=pltpu.VMEM):
    return pl.pallas_call(
        kernel,
        out_shape=[jax.ShapeDtypeStruct(s, F32) for s in outs],
        in_specs=[pl.BlockSpec(memory_space=space)] * len(ins),
        out_specs=[pl.BlockSpec(memory_space=pltpu.VMEM)] * len(outs),
        scratch_shapes=list(scratch),
        compiler_params=pltpu.CompilerParams(vmem_limit_bytes=limit),
    )(*ins)


def work_scratch(planes, rows):
    flat = [vmem(planes, rows, 128) for _ in range(8)]
    return flat + [vmem(planes + 1, rows + 16, 128) for _ in range(2)] + [vmem(planes, rows, 128)]


def level_scratch(planes, rows):
    return [vmem(planes + 2, rows + 16, 128)] + [vmem(planes, rows, 128)] * 2 + work_scratch(planes, rows)


def local(b, beta, shift):
    fields = (b, beta, shift)
    a, c = pack_fine_x(fields)
    xs = swaps(a, c, "gx", 1)
    a, c = call(pack_face_y, fields, [(FACE_Y_SIZE, 128)] * 2)
    ys = swaps(a, c, "gy", 1)
    x_fine, packed, a, c = call(
        inner_kernel,
        (*fields, *xs, *ys),
        [(16, 32, 128), (3, 8, 8, 128)] + [(SECOND_Y_SIZE, 128)] * 2,
        level_scratch(FINE.planes, 32) + [vmem(24, 32, 128)],
    )
    second = swaps(a, c, "gy", 1)
    flat, tall = (24, 40, 128), (25, 56, 128)
    inner = call(
        strip_kernel,
        (*fields, *ys),
        [flat] * 8 + [tall] * 4 + [flat, (8, 40, 128)],
        [vmem(26, 56, 128), vmem(*flat), vmem(*flat)],
    )
    x_edge, ext, near_a, near_b, far_a, far_b = call(
        edge_kernel,
        (*fields, *xs, *ys, packed, *second, *inner),
        [(16, 8, 128), (3, 8, 24, 128)] + [(NEAR_X_SIZE, 128)] * 2 + [(FAR_X_SIZE, 128)] * 2,
        level_scratch(24, 40) + [vmem(*tall)] * 2 + [vmem(8, 40, 128)],
    )
    around = (*swaps(near_a, near_b, "gx", 1), *swaps(far_a, far_b, "gx", 2))
    low = [vmem(LOW.planes + 2, 32, 128), vmem(LOW.planes, 16, 128)] + work_scratch(LOW.planes, 16)
    return tuple(call(
        coarse_kernel,
        (x_fine, x_edge, ext, *around),
        [(16, 32, 128), (8, 16, 64)],
        level_scratch(MID.planes, 40) + [vmem(16, 40, 128)] + low
        + [vmem(2, 16, 128), vmem(8, 32, 128), vmem(128, 128)],
    ))


def solution(mesh):
    placed = P("gx", "gy", None)
    return jax.shard_map(
        local, mesh=mesh, in_specs=(placed,) * 3, out_specs=(placed, placed), check_vma=False
    )
```

```python
import jax
import jax.numpy as jnp
from jax import lax
from jax.experimental import pallas as pl
from jax.experimental.pallas import tpu as pltpu
from jax.sharding import PartitionSpec as P

SWEEPS = 4
THETA, DELTA = 1.15, 0.85
SIGMA = THETA / DELTA
F32 = jnp.float32


def coefficients():
    rho, out = 1.0 / SIGMA, []
    for _ in range(SWEEPS - 1):
        new = 1.0 / (2.0 * SIGMA - rho)
        out.append((new * rho, 2.0 * new / DELTA))
        rho = new
    return out


def lanes(rows):
    return lax.broadcasted_iota(jnp.int32, (rows, 128), 1)


def roll(value, shift):
    return pltpu.roll(value, shift % 128, 1)


class StepSplit:
    def __init__(self, inner, outer, planes, level):
        self.inner, self.outer, self.planes, self.level, self.own = inner, outer, planes, level, set()

    def __getitem__(self, at):
        return (self.inner if at[0] in self.planes and at[0] not in self.own else self.outer)[at]

    def __setitem__(self, at, value):
        self.outer[at] = value
        if at[1].start >= self.level.bases[-1]:
            self.own.add(at[0])


class Level:
    def __init__(self, depth, own_planes, rows, own_rows, rep, folded=False, bases=(0,)):
        self.bases = bases
        self.depth, self.own, self.rep, self.folded = depth, own_planes, rep, folded
        self.planes = depth + own_planes // 2 if folded else own_planes + 2 * depth
        self.rows, self.first_row, self.own_rows = rows, (rows - own_rows) // 2, own_rows

    def cut(self, k):
        return k, self.planes - (0 if self.folded else k)

    def span(self, plane, reach):
        x = plane - self.depth
        far = max(0, -x) if self.folded else max(0, -x, x - self.own + 1)
        side = max(0, reach - far)
        lo = max(0, self.first_row - side) // 8 * 8
        hi = min(self.rows, -(-(self.first_row + self.own_rows + side) // 8) * 8)
        return lo, hi - lo

    def put(self, dst, i, at, value):
        dst[i, at, :] = value
        if self.folded and i == self.planes - 1:
            dst[i + 1, at, :] = swap_lanes(value)


def swap_lanes(value):
    return jnp.where(lanes(value.shape[0]) % 2 == 0, roll(value, -1), roll(value, 1))


def build(level, scale, beta, rhs, shift, work, planes=None):
    wx, wy, wym, wz, wzm, diag, inv, rhs_n, start = work
    rep, half, last_span = level.rep, 0.5 * scale, None
    planes = range(level.planes) if planes is None else planes
    for base, i in [(base, i) for base in level.bases for i in planes]:
        lo, n = level.span(i, level.depth)
        lo += base
        if (lo, n, i) != last_span:
            prev, cur = beta[i, pl.ds(8 + lo, n), :], beta[i + 1, pl.ds(8 + lo, n), :]
            wx_prev = half * (prev + cur)
            if i:
                wx[i - 1, pl.ds(lo, n), :] = wx_prev
            lane = lanes(n)
            first, last = lane < rep, lane >= 128 - rep
        last_span = (lo, n, i + 1)
        at = pl.ds(lo, n)
        nxt = beta[i + 2, pl.ds(8 + lo, n), :]
        wx_next = half * (cur + nxt)
        w_up = half * (cur + beta[i + 1, pl.ds(9 + lo, n), :])
        w_down = half * (cur + beta[i + 1, pl.ds(7 + lo, n), :])
        w_right = half * (cur + jnp.where(last, 0.0, roll(cur, -rep)))
        w_left = half * (cur + jnp.where(first, 0.0, roll(cur, rep)))
        d = shift(i, at) + (wx_prev + wx_next + w_up + w_down + w_right + w_left)
        iv = jnp.where(cur > 0.0, 1.0 / d, 0.0)
        wx[i, at, :] = wx_next
        wy[i, at, :] = w_up
        wym[i, at, :] = w_down
        wz[i, at, :] = jnp.where(last, 0.0, w_right)
        wzm[i, at, :] = jnp.where(first, 0.0, w_left)
        diag[i, at, :] = d
        inv[i, at, :] = iv
        if rhs is not None:
            begin(level, i, lo, n, rhs, iv, rhs_n, start)
        cur, wx_prev = nxt, wx_next


def begin(level, i, lo, n, rhs, iv, rhs_n, start):
    c = rhs(i, pl.ds(lo, n)) * iv
    rhs_n[i, pl.ds(lo, n), :] = c
    level.put(start, i, pl.ds(8 + lo, n), c * (1.0 / THETA))


def scaled_residual(level, src, planes, reach, work, emit):
    wx, wy, wym, wz, wzm, _, inv, rhs_n, _ = work
    rep, last_span = level.rep, None
    for base, i in [(base, i) for base in level.bases for i in planes]:
        lo, n = level.span(i, reach)
        lo += base
        at, dom = pl.ds(lo, n), pl.ds(8 + lo, n)
        if (lo, n, i) != last_span:
            prev, cur, wx_prev = src[i - 1, dom, :], src[i, dom, :], wx[i - 1, at, :]
        last_span = (lo, n, i + 1)
        nxt, wx_next = src[i + 1, dom, :], wx[i, at, :]
        t = wx_next * nxt + wx_prev * prev
        t = t + wy[i, at, :] * src[i, pl.ds(9 + lo, n), :] + wym[i, at, :] * src[i, pl.ds(7 + lo, n), :]
        t = t + wz[i, at, :] * roll(cur, -rep) + wzm[i, at, :] * roll(cur, rep)
        emit(i, lo, n, cur, rhs_n[i, at, :] + inv[i, at, :] * t - cur)
        prev, cur, wx_prev = cur, nxt, wx_next


def sweeps(level, work, fields, step, planes):
    for k, (a, g) in enumerate(coefficients()):

        def emit(i, lo, n, cur, e, a=a, g=g, k=k, dst=fields[k + 1]):
            before = cur if k == 0 else step[i, pl.ds(lo, n), :]
            d = a * before + g * e
            if k < SWEEPS - 2:
                step[i, pl.ds(lo, n), :] = d
            level.put(dst, i, pl.ds(8 + lo, n), cur + d)

        scaled_residual(level, fields[k], planes(k + 1), level.depth - k - 1, work, emit)
    return fields[-1]


def smooth(level, work, other, step):
    fields = (work[8], other) * 2
    return sweeps(level, work, fields, step, lambda k: range(*level.cut(k)))


class Split:
    def __init__(self, inner, outer, first, last):
        self.inner, self.outer, self.first, self.last = inner, outer, first, last

    def __getitem__(self, at):
        return (self.inner if self.first <= at[0] <= self.last else self.outer)[at]

    def __setitem__(self, at, value):
        if not self.first <= at[0] <= self.last:
            self.outer[at] = value


FINE = Level(4, 16, 32, 32, 1)
STRIP = Level(4, 16, 16, 16, 1, bases=(0, 24))
MID = Level(10, 8, 40, 16, 2, folded=True)
LOW = Level(3, 4, 16, 8, 4, folded=True)


def table(entries):
    rows, at = {}, 0
    for key, count in entries:
        rows[key] = (at, count)
        at += count
    return rows, -(-at // 8) * 8


FACE_Y, FACE_Y_SIZE = table([((f, x), 8) for x in range(16) for f in (0, 2)] + [((1, x), 9) for x in range(16)])

MID_Y = {0: 4, 1: 6, 2: 5}
HALO_X = [-1, -2, -3, -4, -5, 16, 17, 18, 19, 20]


def away(x):
    return -x if x < 0 else x - 15


SECOND_Y, SECOND_Y_SIZE = table(
    [((f, "mid", m), MID_Y[f]) for f in range(3) for m in range(8)]
    + [((f, "fine", x), 8 + (f == 1) - away(x)) for f in range(3) for x in HALO_X if away(x) < 5 + (f == 1)]
)


def side_rows(field, far):
    return -(-max(0, 10 + (field == 1) - far) // 2)


NEAR_X, NEAR_X_SIZE = table([((f, d), 8 + 2 * side_rows(f, d)) for f in range(3) for d in range(1, 9)])
FAR_X, FAR_X_SIZE = table([((f, d), 8 + 2 * side_rows(f, d)) for f in range(3) for d in range(9, 11 + (f == 1))])


def flag(condition):
    return jnp.where(condition, 1.0, 0.0).astype(F32)


def x_flags():
    i, n = lax.axis_index("gx"), lax.axis_size("gx")
    return {-2: flag(i > 1), -1: flag(i > 0), 1: flag(i < n - 1), 2: flag(i < n - 2)}


def y_flags():
    j, n = lax.axis_index("gy"), lax.axis_size("gy")
    return flag(j > 0), flag(j < n - 1)


def upward(axis, by):
    return lax.rem(lax.axis_index(axis), 2 * by) >= by


def swaps(first, second, axis, by):
    axes = ("gx", "gy")
    size = [lax.axis_size(name) for name in axes]
    dim = axes.index(axis)
    orders = []
    for sign in (1, -1):
        pairs = []
        for i in range(size[0]):
            for j in range(size[1]):
                to = [i, j]
                to[dim] += sign * by if to[dim] % (2 * by) >= by else -sign * by
                if not 0 <= to[dim] < size[dim]:
                    to = [i, j]
                    to[1 - dim] ^= 1
                pairs.append((i * size[1] + j, to[0] * size[1] + to[1]))
        orders.append(pairs)
    return lax.ppermute(first, axes, orders[0]), lax.ppermute(second, axes, orders[1])


COUNTS = (4, 5, 4)
STARTS = (0, 4, 9)


def pack_fine_x(fields):
    ends = [f[:n] for f, n in zip(fields, COUNTS)] + [f[16 - n:] for f, n in zip(fields, COUNTS)]
    first, last = jnp.concatenate(ends[:3], axis=0), jnp.concatenate(ends[3:], axis=0)
    first, last = lax.optimization_barrier((first, last))
    up = upward("gx", 1)
    return jnp.where(up, last, first), jnp.where(up, first, last)


def fine_plane(field, x, own, in_a, in_b, up):
    if 0 <= x < 16:
        return own[field][x]
    i = STARTS[field] + (x + COUNTS[field] if x < 0 else x - 16)
    return jnp.where(up, in_b[i], in_a[i]) if x < 0 else jnp.where(up, in_a[i], in_b[i])


def pick(ref, rows, key):
    at, count = rows[key]
    return ref[pl.ds(at, count), :]


def put_both(out_a, out_b, rows, key, up, higher, lower):
    at, count = rows[key]
    out_a[pl.ds(at, count), :] = jnp.where(up, higher, lower)
    out_b[pl.ds(at, count), :] = jnp.where(up, lower, higher)


def pack_face_y(b, beta, shift, out_a, out_b):
    up = upward("gy", 1)
    for field, src in enumerate((b, beta, shift)):
        for x in range(16):
            n = FACE_Y[field, x][1]
            put_both(out_a, out_b, FACE_Y, (field, x), up, src[x, pl.ds(32 - n, n), :], src[x, pl.ds(0, n), :])


def y_sides(rows, key, in_a, in_b, up):
    a, b = pick(in_a, rows, key), pick(in_b, rows, key)
    return jnp.where(up, b, a), jnp.where(up, a, b)


def pack_pairs(pair, plane, start, count):
    even = lanes(count) % 2 == 0
    e = pair[plane, pl.ds(start, count, 4), :] + pair[plane, pl.ds(start + 1, count, 4), :]
    o = pair[plane, pl.ds(start + 2, count, 4), :] + pair[plane, pl.ds(start + 3, count, 4), :]
    return jnp.where(even, e + roll(e, -1), o + roll(o, 1)) * 0.125


def pair_residual(level, src, work, pair, first, planes):
    diag, held = work[5], {}

    def emit(i, lo, n, cur, e):
        r = e * diag[i, pl.ds(lo, n), :]
        if i % 2 == 0:
            held[0] = r
        else:
            pair[first + (i - 4) // 2, pl.ds(lo, n), :] = held[0] + r

    scaled_residual(level, src, planes, 0, work, emit)


def inner_kernel(
    b, beta, shift, xa_in, xb_in, ya_in, yb_in, x_out, packed, out_a, out_b,
    be, bb, ss, wx, wy, wym, wz, wzm, diag, inv, rhs_n, xa, xb, step, pair,
):
    near, (low, high) = x_flags(), y_flags()
    up_x, up_y = upward("gx", 1), upward("gy", 1)
    own = (b, beta, shift)
    for x in range(-5, 21):
        p = fine_plane(1, x, own, xa_in, xb_in, up_x)
        be[x + 5, 8:40, :] = p if 0 <= x < 16 else p * (near[-1] if x < 0 else near[1])
        if 0 <= x < 16:
            lo, hi = y_sides(FACE_Y, (1, x), ya_in, yb_in, up_y)
            be[x + 5, 7:8, :] = lo[8:9] * low
            be[x + 5, 40:41, :] = hi[0:1] * high
        else:
            at = SECOND_Y[1, "fine", x][1]
            put_both(out_a, out_b, SECOND_Y, (1, "fine", x), up_y, p[32 - at:32], p[0:at])
    for field, dst in ((0, bb), (2, ss)):
        for x in range(-4, 20):
            if 0 <= x < 16:
                continue
            p = fine_plane(field, x, own, xa_in, xb_in, up_x)
            dst[x + 4] = p
            at = SECOND_Y[field, "fine", x][1]
            put_both(out_a, out_b, SECOND_Y, (field, "fine", x), up_y, p[32 - at:32], p[0:at])
    work = (wx, wy, wym, wz, wzm, diag, inv, rhs_n, xa)

    def plane_of(src, halo):
        return lambda i, at: src[i - 4] if 4 <= i < 20 else halo[i]

    build(FINE, 1.0, be, plane_of(b, bb), plane_of(shift, ss), work)
    x = smooth(FINE, work, xb, step)
    for m in range(8):
        pair[m] = beta[2 * m] + beta[2 * m + 1]
        pair[m + 8] = shift[2 * m] + shift[2 * m + 1]
    pair_residual(FINE, x, work, pair, 16, range(4, 20))
    for m in range(8):
        packed[1, m] = pack_pairs(pair, m, 0, 8)
        packed[2, m] = pack_pairs(pair, m + 8, 0, 8)
        packed[0, m] = pack_pairs(pair, m + 16, 0, 8)
    for m in range(8):
        for field, skip in ((0, 1), (1, 0), (2, 0)):
            n = MID_Y[field]
            higher = packed[field, m, pl.ds(8 - skip - n, n), :]
            lower = packed[field, m, pl.ds(skip, n), :]
            put_both(out_a, out_b, SECOND_Y, (field, "mid", m), up_y, higher, lower)
    for i in range(16):
        x_out[i] = x[i + 4, pl.ds(8, 32), :]


def INNER(k):
    return range(5 + k, 19 - k)


def strip_kernel(
    b, beta, shift, ya_in, yb_in,
    wx, wy, wym, wz, wzm, diag, inv, rhs_n, x0, x1, x2, x3, step, pair, be, bb, ss,
):
    (low, high), up_y = y_flags(), upward("gy", 1)
    for x in range(16):
        lo, hi = y_sides(FACE_Y, (1, x), ya_in, yb_in, up_y)
        be[x + 5, 16:25, :] = beta[x, 0:9, :]
        be[x + 5, 31:40, :] = beta[x, 23:32, :]
        be[x + 5, 7:16, :] = lo * low
        be[x + 5, 40:49, :] = hi * high
    for field, src, dst in ((0, b, bb), (2, shift, ss)):
        for x in range(1, 15):
            lo, hi = y_sides(FACE_Y, (field, x), ya_in, yb_in, up_y)
            dst[x + 4, 8:16, :] = src[x, 0:8, :]
            dst[x + 4, 24:32, :] = src[x, 24:32, :]
            dst[x + 4, 0:8, :] = lo
            dst[x + 4, 32:40, :] = hi
    work = (wx, wy, wym, wz, wzm, diag, inv, rhs_n, x0)
    build(STRIP, 1.0, be, lambda i, at: bb[i, at, :], lambda i, at: ss[i, at, :], work, INNER(0))
    sweeps(STRIP, work, (x0, x1, x2, x3), step, INNER)
    pair_residual(STRIP, x3, work, pair, 0, range(10, 14))


def edge_kernel(
    b, beta, shift, xa_in, xb_in, ya_in, yb_in, packed, ya2, yb2,
    i_wx, i_wy, i_wym, i_wz, i_wzm, i_diag, i_inv, i_rhs_n, i_x0, i_x1, i_x2, i_x3, i_step, i_pair,
    x_out, ext, near_a, near_b, far_a, far_b,
    be, bb, ss, wx, wy, wym, wz, wzm, diag, inv, rhs_n, x0, x1, step, x2, x3, pair,
):
    near, (low, high) = x_flags(), y_flags()
    up_x, up_y = upward("gx", 1), upward("gy", 1)
    own = (b, beta, shift)

    def sides(field, x):
        if 0 <= x < 16:
            return y_sides(FACE_Y, (field, x), ya_in, yb_in, up_y)
        return y_sides(SECOND_Y, (field, "fine", x), ya2, yb2, up_y)

    for x in [*range(-5, 2), *range(14, 21)]:
        p = fine_plane(1, x, own, xa_in, xb_in, up_x)
        lo, hi = sides(1, x)
        n = lo.shape[0]
        f = 1.0 if 0 <= x < 16 else near[-1] if x < 0 else near[1]
        if not 0 <= x < 16:
            p = p * f
        be[x + 5, 16:25, :] = p[0:9]
        be[x + 5, 31:40, :] = p[23:32]
        be[x + 5, pl.ds(16 - n, n), :] = lo * (low * f)
        be[x + 5, pl.ds(40, n), :] = hi * (high * f)
    for field, dst in ((0, bb), (2, ss)):
        for x in [*range(-4, 1), *range(15, 20)]:
            p = fine_plane(field, x, own, xa_in, xb_in, up_x)
            lo, hi = sides(field, x)
            n = lo.shape[0]
            dst[x + 4, 8:16, :] = p[0:8]
            dst[x + 4, 24:32, :] = p[24:32]
            dst[x + 4, pl.ds(8 - n, n), :] = lo
            dst[x + 4, pl.ds(32, n), :] = hi
    inner = (i_wx, i_wy, i_wym, i_wz, i_wzm, i_diag, i_inv, i_rhs_n, i_x0)
    outer = (wx, wy, wym, wz, wzm, diag, inv, rhs_n, x0)
    work = tuple(Split(i, o, 5, 18) for i, o in zip(inner, outer))
    fields = [work[8]] + [
        Split(i, o, INNER(k)[0], INNER(k)[-1]) for k, i, o in ((1, i_x1, x1), (2, i_x2, x2), (3, i_x3, x3))
    ]

    def rest(k):
        return [i for i in range(k, 24 - k) if i not in INNER(k)]

    build(STRIP, 1.0, be, lambda i, at: bb[i, at, :], lambda i, at: ss[i, at, :], work, rest(0))
    x = sweeps(STRIP, work, fields, StepSplit(i_step, step, INNER(1), STRIP), rest)
    both = Split(i_pair, pair, 3, 4)
    pair_residual(STRIP, x, work, both, 0, [*range(4, 10), *range(14, 20)])
    pair = both
    for m in range(8):
        ext[0, m, 7:13, :] = packed[0, m, 1:7, :]
        ext[0, m, 5:7, :] = pack_pairs(pair, m, 4, 2)
        ext[0, m, 13:15, :] = pack_pairs(pair, m, 28, 2)
        for field, skip, scale in ((0, 1, (None, None)), (1, 0, (low, high)), (2, 0, (None, None))):
            if field:
                ext[field, m, 6:14, :] = packed[field, m]
            n = MID_Y[field]
            lo, hi = y_sides(SECOND_Y, (field, "mid", m), ya2, yb2, up_y)
            ext[field, m, pl.ds(6 - skip - n, n), :] = lo if scale[0] is None else lo * scale[0]
            ext[field, m, pl.ds(14 + skip, n), :] = hi if scale[1] is None else hi * scale[1]
    up2 = upward("gx", 2)
    for rows, up, a, c, first in ((NEAR_X, up_x, near_a, near_b, 1), (FAR_X, up2, far_a, far_b, 9)):
        for field, d in rows:
            n = side_rows(field, d)
            at = pl.ds(6 - n, 8 + 2 * n)
            higher, lower = ext[field, 8 - d + (first - 1), at, :], ext[field, d - first, at, :]
            put_both(a, c, rows, (field, d), up, higher, lower)
    for i in range(16):
        x_out[i, 0:4, :] = x[i + 4, pl.ds(16, 4), :]
        x_out[i, 4:8, :] = x[i + 4, pl.ds(36, 4), :]


def spread(dst, plane, start, a, b):
    n = a.shape[0]
    even = lanes(n) % 2 == 0
    dst[plane, pl.ds(start, n, 2), :] = jnp.where(even, a, roll(b, 1))
    dst[plane, pl.ds(start + 1, n, 2), :] = jnp.where(even, roll(a, -1), b)


def gather(field, d, ext, near, far=None):
    if d <= 0:
        n = side_rows(field, 0)
        at = pl.ds(6 - n, 8 + 2 * n)
        return ext[field, -d, at, :], ext[field, 7 + d, at, :]
    hop, rows, (a, c) = (1, NEAR_X, near) if d <= 8 else (2, FAR_X, far)
    u = upward("gx", hop)
    a, c = pick(a, rows, (field, d)), pick(c, rows, (field, d))
    lower, higher = jnp.where(u, c, a), jnp.where(u, a, c)
    if field == 1:
        flags = x_flags()
        return lower * flags[-hop], higher * flags[hop]
    return lower, higher


def unpack_mid(field, planes, dst, first, reach, *messages):
    for i in planes:
        a, b = gather(field, reach - i, *messages)
        spread(dst, i, first - (a.shape[0] - 8), a, b)


def down_sample(pair, plane):
    low_pair = lanes(16) % 4 < 2
    s = pair[plane, pl.ds(4, 16, 2), :] + pair[plane, pl.ds(5, 16, 2), :]
    return (s + jnp.where(low_pair, roll(s, -2), roll(s, 2))) * 0.125


def pair_mid_residual(src, work, pair, planes):
    diag, held = work[5], {}

    def emit(i, lo, n, cur, e):
        r = e * diag[i, pl.ds(lo, n), :]
        if i % 2 == 0:
            held[0] = lo, n, r
        else:
            lo0, n0, r0 = held[0]
            at, end = max(lo, lo0), min(lo + n, lo0 + n0)
            total = r0[at - lo0:end - lo0] + r[at - lo:end - lo]
            pair[(i - 4) // 2, pl.ds(at, end - at), :] = total

    scaled_residual(MID, src, planes, 6, work, emit)


def MID_INNER(k):
    return range(3 + k, 14)


def mid_kernel(
    ext, near_a, near_b,
    wx, wy, wym, wz, wzm, diag, inv, rhs_n, x0, x1, x2, x3, step, pair,
    wx2, wy2, wym2, wz2, wzm2, diag2, inv2,
    be, bb, ss, be2, ss2, sums,
):
    messages = ext, (near_a, near_b)
    unpack_mid(1, range(3, 15), be, 20, 11, *messages)
    unpack_mid(0, range(3, 14), bb, 12, 10, *messages)
    unpack_mid(2, range(3, 14), ss, 12, 10, *messages)
    be[15, pl.ds(8, 40), :] = swap_lanes(be[14, pl.ds(8, 40), :])
    work = (wx, wy, wym, wz, wzm, diag, inv, rhs_n, x0)
    build(MID, 0.25, be, lambda i, at: bb[i, at, :], lambda i, at: ss[i, at, :], work, MID_INNER(0))
    sweeps(MID, work, (x0, x1, x2, x3), step, MID_INNER)
    pair_mid_residual(x3, work, pair, range(8, 14))

    for m in range(6):
        sums[m] = be[2 * m + 3, pl.ds(8, 40), :] + be[2 * m + 4, pl.ds(8, 40), :]
    for m in range(5):
        sums[6 + m] = ss[2 * m + 4] + ss[2 * m + 5]
    for m in range(6):
        be2[m, 8:24, :] = down_sample(sums, m)
    be2[6, 8:24, :] = swap_lanes(be2[5, 8:24, :])
    for m in range(5):
        ss2[m] = down_sample(sums, 6 + m)
    work2 = (wx2, wy2, wym2, wz2, wzm2, diag2, inv2, None, None)
    build(LOW, 0.0625, be2, None, lambda i, at: ss2[i, at, :], work2)


def coarse_kernel(
    x_fine, x_edge, ext, near_a, near_b, far_a, far_b,
    i_wx, i_wy, i_wym, i_wz, i_wzm, i_diag, i_inv, i_rhs_n, i_x0, i_x1, i_x2, i_x3, i_step, i_pair,
    wx2, wy2, wym2, wz2, wzm2, diag2, inv2,
    out, mid_out,
    be, bb, ss, wx, wy, wym, wz, wzm, diag, inv, rhs_n, x0, x1, step, x2, x3, pair,
    rhs_n2, xa2, xb2, step2, rep_mid, rep_fine, mids,
):
    messages = ext, (near_a, near_b), (far_a, far_b)
    unpack_mid(1, range(5), be, 20, 11, *messages)
    unpack_mid(0, range(3), bb, 12, 10, *messages)
    unpack_mid(2, range(3), ss, 12, 10, *messages)
    inner = (i_wx, i_wy, i_wym, i_wz, i_wzm, i_diag, i_inv, i_rhs_n, i_x0)
    outer = (wx, wy, wym, wz, wzm, diag, inv, rhs_n, x0)
    work = tuple(Split(i, o, 3, 14) for i, o in zip(inner, outer))
    fields = [work[8]] + [Split(i, o, 3 + k, 14) for k, i, o in ((1, i_x1, x1), (2, i_x2, x2), (3, i_x3, x3))]

    def rest(k):
        return range(k, 3 + k)

    build(MID, 0.25, be, lambda i, at: bb[i, at, :], lambda i, at: ss[i, at, :], work, rest(0))
    x1 = sweeps(MID, work, fields, StepSplit(i_step, step, MID_INNER(1), MID), rest)
    pair = Split(i_pair, pair, 2, 4)
    pair_mid_residual(x1, work, pair, range(4, 8))
    for i in range(LOW.planes):
        lo, n = LOW.span(i, LOW.depth)
        begin(LOW, i, lo, n, lambda i, at: down_sample(pair, i), inv2[i], rhs_n2, xa2)
    work2 = (wx2, wy2, wym2, wz2, wzm2, diag2, inv2, rhs_n2, xa2)
    x2 = smooth(LOW, work2, xb2, step2)

    for m in range(2):
        low_x = x2[m + 3, pl.ds(12, 8), :]
        rep_mid[m, pl.ds(0, 8, 2), :] = low_x
        rep_mid[m, pl.ds(1, 8, 2), :] = low_x
    even = lanes(16) % 2 == 0
    for m in range(4):
        both = x1[m + 10, pl.ds(20, 16), :] + rep_mid[m // 2]
        for x, mid in (
            (m, jnp.where(even, both, roll(both, 1))),
            (7 - m, jnp.where(even, roll(both, -1), both)),
        ):
            mids[pl.ds(16 * x, 16), :] = mid
            rep_fine[x, pl.ds(0, 16, 2), :] = mid
            rep_fine[x, pl.ds(1, 16, 2), :] = mid
    for i in range(16):
        out[i, 4:28, :] = x_fine[i, 4:28, :] + rep_fine[i // 2, 4:28, :]
        out[i, 0:4, :] = x_edge[i, 0:4, :] + rep_fine[i // 2, 0:4, :]
        out[i, 28:32, :] = x_edge[i, 4:8, :] + rep_fine[i // 2, 28:32, :]
    row = lax.broadcasted_iota(jnp.int32, (128, 64), 0)
    col = lax.broadcasted_iota(jnp.int32, (128, 64), 1)
    even_lanes = jnp.where(row == 2 * col, 1.0, 0.0).astype(F32)
    compact = jnp.dot(mids[...], even_lanes, precision=lax.Precision.HIGHEST, preferred_element_type=F32)
    for m in range(8):
        mid_out[m] = compact[16 * m:16 * m + 16]


def vmem(*shape):
    return pltpu.VMEM(shape, F32)


def call(kernel, ins, outs, scratch=(), limit=24 * 2**20, space=pltpu.VMEM):
    return pl.pallas_call(
        kernel,
        out_shape=[jax.ShapeDtypeStruct(s, F32) for s in outs],
        in_specs=[pl.BlockSpec(memory_space=space)] * len(ins),
        out_specs=[pl.BlockSpec(memory_space=pltpu.VMEM)] * len(outs),
        scratch_shapes=list(scratch),
        compiler_params=pltpu.CompilerParams(vmem_limit_bytes=limit),
    )(*ins)


def work_scratch(planes, rows):
    flat = [vmem(planes, rows, 128) for _ in range(8)]
    return flat + [vmem(planes + 1, rows + 16, 128) for _ in range(2)] + [vmem(planes, rows, 128)]


def level_scratch(planes, rows):
    return [vmem(planes + 2, rows + 16, 128)] + [vmem(planes, rows, 128)] * 2 + work_scratch(planes, rows)


def local(b, beta, shift):
    fields = (b, beta, shift)
    a, c = pack_fine_x(fields)
    xs = swaps(a, c, "gx", 1)
    a, c = call(pack_face_y, fields, [(FACE_Y_SIZE, 128)] * 2)
    ys = swaps(a, c, "gy", 1)
    x_fine, packed, a, c = call(
        inner_kernel,
        (*fields, *xs, *ys),
        [(16, 32, 128), (3, 8, 8, 128)] + [(SECOND_Y_SIZE, 128)] * 2,
        level_scratch(FINE.planes, 32) + [vmem(24, 32, 128)],
    )
    second = swaps(a, c, "gy", 1)
    flat, tall = (24, 40, 128), (25, 56, 128)
    inner = call(
        strip_kernel,
        (*fields, *ys),
        [flat] * 8 + [tall] * 4 + [flat, (8, 40, 128)],
        [vmem(26, 56, 128), vmem(*flat), vmem(*flat)],
    )
    x_edge, ext, near_a, near_b, far_a, far_b = call(
        edge_kernel,
        (*fields, *xs, *ys, packed, *second, *inner),
        [(16, 8, 128), (3, 8, 24, 128)] + [(NEAR_X_SIZE, 128)] * 2 + [(FAR_X_SIZE, 128)] * 2,
        level_scratch(24, 40) + [vmem(*tall)] * 2 + [vmem(8, 40, 128)],
    )
    near = swaps(near_a, near_b, "gx", 1)
    far = swaps(far_a, far_b, "gx", 2)
    flat, tall, small = (14, 40, 128), (15, 56, 128), (5, 16, 128)
    inner = call(
        mid_kernel,
        (ext, *near),
        [flat] * 8 + [tall] * 4 + [flat, (5, 40, 128)] + [small] * 7,
        [vmem(16, 56, 128), vmem(*flat), vmem(*flat), vmem(7, 32, 128), vmem(*small), vmem(11, 40, 128)],
    )
    return tuple(call(
        coarse_kernel,
        (x_fine, x_edge, ext, *near, *far, *inner),
        [(16, 32, 128), (8, 16, 64)],
        level_scratch(14, 40) + [vmem(*tall)] * 2 + [vmem(5, 40, 128)]
        + [vmem(*small), vmem(6, 32, 128), vmem(6, 32, 128), vmem(*small)]
        + [vmem(2, 16, 128), vmem(8, 32, 128), vmem(128, 128)],
    ))


def solution(mesh):
    placed = P("gx", "gy", None)
    return jax.shard_map(
        local, mesh=mesh, in_specs=(placed,) * 3, out_specs=(placed, placed), check_vma=False
    )
```

```python
import jax
import jax.numpy as jnp
from jax import lax
from jax.experimental import pallas as pl
from jax.experimental.pallas import tpu as pltpu
from jax.sharding import PartitionSpec as P

SWEEPS = 4
THETA, DELTA = 1.15, 0.85
SIGMA = THETA / DELTA
F32 = jnp.float32


def coefficients():
    rho, out = 1.0 / SIGMA, []
    for _ in range(SWEEPS - 1):
        new = 1.0 / (2.0 * SIGMA - rho)
        out.append((new * rho, 2.0 * new / DELTA))
        rho = new
    return out


def lanes(rows):
    return lax.broadcasted_iota(jnp.int32, (rows, 128), 1)


def roll(value, shift):
    return pltpu.roll(value, shift % 128, 1)


class StepSplit:
    def __init__(self, inner, outer, planes, level):
        self.inner, self.outer, self.planes, self.level, self.own = inner, outer, planes, level, set()

    def __getitem__(self, at):
        return (self.inner if at[0] in self.planes and at[0] not in self.own else self.outer)[at]

    def __setitem__(self, at, value):
        self.outer[at] = value
        if at[1].start >= self.level.bases[-1]:
            self.own.add(at[0])


class Level:
    def __init__(self, depth, own_planes, rows, own_rows, rep, folded=False, bases=(0,)):
        self.bases = bases
        self.depth, self.own, self.rep, self.folded = depth, own_planes, rep, folded
        self.planes = depth + own_planes // 2 if folded else own_planes + 2 * depth
        self.rows, self.first_row, self.own_rows = rows, (rows - own_rows) // 2, own_rows

    def cut(self, k):
        return k, self.planes - (0 if self.folded else k)

    def span(self, plane, reach):
        x = plane - self.depth
        far = max(0, -x) if self.folded else max(0, -x, x - self.own + 1)
        side = max(0, reach - far)
        lo = max(0, self.first_row - side) // 8 * 8
        hi = min(self.rows, -(-(self.first_row + self.own_rows + side) // 8) * 8)
        return lo, hi - lo

    def put(self, dst, i, at, value):
        dst[i, at, :] = value
        if self.folded and i == self.planes - 1:
            dst[i + 1, at, :] = swap_lanes(value)


def swap_lanes(value):
    return jnp.where(lanes(value.shape[0]) % 2 == 0, roll(value, -1), roll(value, 1))


def build(level, scale, beta, rhs, shift, work, planes=None):
    wx, wy, wym, wz, wzm, diag, inv, rhs_n, start = work
    rep, half, last_span = level.rep, 0.5 * scale, None
    planes = range(level.planes) if planes is None else planes
    for base, i in [(base, i) for base in level.bases for i in planes]:
        lo, n = level.span(i, level.depth)
        lo += base
        if (lo, n, i) != last_span:
            prev, cur = beta[i, pl.ds(8 + lo, n), :], beta[i + 1, pl.ds(8 + lo, n), :]
            wx_prev = half * (prev + cur)
            if i:
                wx[i - 1, pl.ds(lo, n), :] = wx_prev
            lane = lanes(n)
            first, last = lane < rep, lane >= 128 - rep
        last_span = (lo, n, i + 1)
        at = pl.ds(lo, n)
        nxt = beta[i + 2, pl.ds(8 + lo, n), :]
        wx_next = half * (cur + nxt)
        w_up = half * (cur + beta[i + 1, pl.ds(9 + lo, n), :])
        w_down = half * (cur + beta[i + 1, pl.ds(7 + lo, n), :])
        w_right = half * (cur + jnp.where(last, 0.0, roll(cur, -rep)))
        w_left = half * (cur + jnp.where(first, 0.0, roll(cur, rep)))
        d = shift(i, at) + (wx_prev + wx_next + w_up + w_down + w_right + w_left)
        iv = jnp.where(cur > 0.0, 1.0 / d, 0.0)
        wx[i, at, :] = wx_next
        wy[i, at, :] = w_up
        wym[i, at, :] = w_down
        wz[i, at, :] = jnp.where(last, 0.0, w_right)
        wzm[i, at, :] = jnp.where(first, 0.0, w_left)
        diag[i, at, :] = d
        inv[i, at, :] = iv
        if rhs is not None:
            begin(level, i, lo, n, rhs, iv, rhs_n, start)
        cur, wx_prev = nxt, wx_next


def begin(level, i, lo, n, rhs, iv, rhs_n, start):
    c = rhs(i, pl.ds(lo, n)) * iv
    rhs_n[i, pl.ds(lo, n), :] = c
    level.put(start, i, pl.ds(8 + lo, n), c * (1.0 / THETA))


def scaled_residual(level, src, planes, reach, work, emit):
    wx, wy, wym, wz, wzm, _, inv, rhs_n, _ = work
    rep, last_span = level.rep, None
    for base, i in [(base, i) for base in level.bases for i in planes]:
        lo, n = level.span(i, reach)
        lo += base
        at, dom = pl.ds(lo, n), pl.ds(8 + lo, n)
        if (lo, n, i) != last_span:
            prev, cur, wx_prev = src[i - 1, dom, :], src[i, dom, :], wx[i - 1, at, :]
        last_span = (lo, n, i + 1)
        nxt, wx_next = src[i + 1, dom, :], wx[i, at, :]
        t = wx_next * nxt + wx_prev * prev
        t = t + wy[i, at, :] * src[i, pl.ds(9 + lo, n), :] + wym[i, at, :] * src[i, pl.ds(7 + lo, n), :]
        t = t + wz[i, at, :] * roll(cur, -rep) + wzm[i, at, :] * roll(cur, rep)
        emit(i, lo, n, cur, rhs_n[i, at, :] + inv[i, at, :] * t - cur)
        prev, cur, wx_prev = cur, nxt, wx_next


def sweeps(level, work, fields, step, planes):
    for k, (a, g) in enumerate(coefficients()):

        def emit(i, lo, n, cur, e, a=a, g=g, k=k, dst=fields[k + 1]):
            before = cur if k == 0 else step[i, pl.ds(lo, n), :]
            d = a * before + g * e
            if k < SWEEPS - 2:
                step[i, pl.ds(lo, n), :] = d
            level.put(dst, i, pl.ds(8 + lo, n), cur + d)

        scaled_residual(level, fields[k], planes(k + 1), level.depth - k - 1, work, emit)
    return fields[-1]


def smooth(level, work, other, step):
    fields = (work[8], other) * 2
    return sweeps(level, work, fields, step, lambda k: range(*level.cut(k)))


class Split:
    def __init__(self, inner, outer, first, last):
        self.inner, self.outer, self.first, self.last = inner, outer, first, last

    def __getitem__(self, at):
        return (self.inner if self.first <= at[0] <= self.last else self.outer)[at]

    def __setitem__(self, at, value):
        if not self.first <= at[0] <= self.last:
            self.outer[at] = value


FINE = Level(4, 16, 32, 32, 1)
STRIP = Level(4, 16, 16, 16, 1, bases=(0, 24))
MID = Level(10, 8, 40, 16, 2, folded=True)
LOW = Level(3, 4, 16, 8, 4, folded=True)


def table(entries):
    rows, at = {}, 0
    for key, count in entries:
        rows[key] = (at, count)
        at += count
    return rows, -(-at // 8) * 8


FACE_Y, FACE_Y_SIZE = table([((f, x), 8) for x in range(16) for f in (0, 2)] + [((1, x), 9) for x in range(16)])

MID_Y = {0: 4, 1: 4, 2: 3}
HALO_X = [-1, -2, -3, -4, -5, 16, 17, 18, 19, 20]


def away(x):
    return -x if x < 0 else x - 15


SECOND_Y, SECOND_Y_SIZE = table(
    [((f, "mid", m), MID_Y[f]) for f in range(3) for m in range(8)]
    + [((f, "fine", x), 8 + (f == 1) - away(x)) for f in range(3) for x in HALO_X if away(x) < 5 + (f == 1)]
)


def side_rows(field, far):
    return -(-max(0, 10 + (field == 1) - far) // 2)


NEAR_X, NEAR_X_SIZE = table([((f, d), 8 + 2 * side_rows(f, d)) for f in range(3) for d in range(1, 9)])
FAR_X, FAR_X_SIZE = table([((f, d), 8 + 2 * side_rows(f, d)) for f in range(3) for d in range(9, 11 + (f == 1))])


def flag(condition):
    return jnp.where(condition, 1.0, 0.0).astype(F32)


def x_flags():
    i, n = lax.axis_index("gx"), lax.axis_size("gx")
    return {-2: flag(i > 1), -1: flag(i > 0), 1: flag(i < n - 1), 2: flag(i < n - 2)}


def y_flags():
    j, n = lax.axis_index("gy"), lax.axis_size("gy")
    return flag(j > 0), flag(j < n - 1)


def upward(axis, by):
    return lax.rem(lax.axis_index(axis), 2 * by) >= by


def swaps(first, second, axis, by):
    axes = ("gx", "gy")
    size = [lax.axis_size(name) for name in axes]
    dim = axes.index(axis)
    orders = []
    for sign in (1, -1):
        pairs = []
        for i in range(size[0]):
            for j in range(size[1]):
                to = [i, j]
                to[dim] += sign * by if to[dim] % (2 * by) >= by else -sign * by
                if not 0 <= to[dim] < size[dim]:
                    to = [i, j]
                    to[1 - dim] ^= 1
                pairs.append((i * size[1] + j, to[0] * size[1] + to[1]))
        orders.append(pairs)
    return lax.ppermute(first, axes, orders[0]), lax.ppermute(second, axes, orders[1])


COUNTS = (4, 5, 4)
STARTS = (0, 4, 9)


def pack_fine_x(fields):
    ends = [f[:n] for f, n in zip(fields, COUNTS)] + [f[16 - n:] for f, n in zip(fields, COUNTS)]
    first, last = jnp.concatenate(ends[:3], axis=0), jnp.concatenate(ends[3:], axis=0)
    first, last = lax.optimization_barrier((first, last))
    up = upward("gx", 1)
    return jnp.where(up, last, first), jnp.where(up, first, last)


def fine_plane(field, x, own, in_a, in_b, up):
    if 0 <= x < 16:
        return own[field][x]
    i = STARTS[field] + (x + COUNTS[field] if x < 0 else x - 16)
    return jnp.where(up, in_b[i], in_a[i]) if x < 0 else jnp.where(up, in_a[i], in_b[i])


def pick(ref, rows, key):
    at, count = rows[key]
    return ref[pl.ds(at, count), :]


def put_both(out_a, out_b, rows, key, up, higher, lower):
    at, count = rows[key]
    out_a[pl.ds(at, count), :] = jnp.where(up, higher, lower)
    out_b[pl.ds(at, count), :] = jnp.where(up, lower, higher)


def pack_face_y(b, beta, shift, out_a, out_b, packed, pair):
    up = upward("gy", 1)
    for field, src in ((1, beta), (2, shift)):
        for m in range(8):
            at = 8 * field + m - 8
            pair[at] = src[2 * m] + src[2 * m + 1]
            packed[field - 1, m] = pack_pairs(pair, at, 0, 8)
    for field, src in enumerate((b, beta, shift)):
        for x in range(16):
            n = FACE_Y[field, x][1]
            put_both(out_a, out_b, FACE_Y, (field, x), up, src[x, pl.ds(32 - n, n), :], src[x, pl.ds(0, n), :])


def y_sides(rows, key, in_a, in_b, up):
    a, b = pick(in_a, rows, key), pick(in_b, rows, key)
    return jnp.where(up, b, a), jnp.where(up, a, b)


def pack_pairs(pair, plane, start, count):
    even = lanes(count) % 2 == 0
    e = pair[plane, pl.ds(start, count, 4), :] + pair[plane, pl.ds(start + 1, count, 4), :]
    o = pair[plane, pl.ds(start + 2, count, 4), :] + pair[plane, pl.ds(start + 3, count, 4), :]
    return jnp.where(even, e + roll(e, -1), o + roll(o, 1)) * 0.125


def pair_residual(level, src, work, pair, first, planes):
    diag, held = work[5], {}

    def emit(i, lo, n, cur, e):
        r = e * diag[i, pl.ds(lo, n), :]
        if i % 2 == 0:
            held[0] = r
        else:
            pair[first + (i - 4) // 2, pl.ds(lo, n), :] = held[0] + r

    scaled_residual(level, src, planes, 0, work, emit)


def INNER(k):
    return range(5 + k, 19 - k)


def rest(k):
    return [i for i in range(k, 24 - k) if i not in INNER(k)]


def split_work(inner, outer, level):
    work = tuple(Split(i, o, 5, 18) for i, o in zip(inner[:9], outer[:9]))
    fields = [work[8]]
    for k in (1, 2, 3):
        fields.append(Split(inner[8 + k], outer[8 + k], INNER(k)[0], INNER(k)[-1]))
    step = StepSplit(inner[12], outer[12], INNER(1), level)
    return work, fields, step, Split(inner[13], outer[13], 3, 4)


def edge_rows(be, x, beta, ya_in, yb_in):
    (low, high), up = y_flags(), upward("gy", 1)
    lo, hi = y_sides(FACE_Y, (1, x), ya_in, yb_in, up)
    be[x + 5, 8:40, :] = beta[x]
    be[x + 5, 7:8, :] = lo[8:9] * low
    be[x + 5, 40:41, :] = hi[0:1] * high


def inner_kernel(
    b, beta, shift, ya_in, yb_in,
    wx, wy, wym, wz, wzm, diag, inv, rhs_n, x0, x1, x2, x3, step, pair, be,
):
    for x in range(16):
        edge_rows(be, x, beta, ya_in, yb_in)
    work = (wx, wy, wym, wz, wzm, diag, inv, rhs_n, x0)
    build(FINE, 1.0, be, lambda i, at: b[i - 4], lambda i, at: shift[i - 4], work, INNER(0))
    sweeps(FINE, work, (x0, x1, x2, x3), step, INNER)
    pair_residual(FINE, x3, work, pair, 0, range(10, 14))


def outer_kernel(
    b, beta, shift, coarse, xa_in, xb_in, ya_in, yb_in, *refs,
):
    inner, refs = refs[:14], refs[14:]
    (x_out, packed, out_a, out_b, be, bb, ss), outer = refs[:7], refs[7:]
    near, up_x, up_y = x_flags(), upward("gx", 1), upward("gy", 1)
    own = (b, beta, shift)
    for x in [*range(-5, 2), *range(14, 21)]:
        if 0 <= x < 16:
            edge_rows(be, x, beta, ya_in, yb_in)
            continue
        p = fine_plane(1, x, own, xa_in, xb_in, up_x)
        be[x + 5, 8:40, :] = p * (near[-1] if x < 0 else near[1])
        at = SECOND_Y[1, "fine", x][1]
        put_both(out_a, out_b, SECOND_Y, (1, "fine", x), up_y, p[32 - at:32], p[0:at])
    for field, dst in ((0, bb), (2, ss)):
        for x in [*range(-4, 0), *range(16, 20)]:
            p = fine_plane(field, x, own, xa_in, xb_in, up_x)
            dst[x + 4] = p
            at = SECOND_Y[field, "fine", x][1]
            put_both(out_a, out_b, SECOND_Y, (field, "fine", x), up_y, p[32 - at:32], p[0:at])
    work, fields, step, pair = split_work(inner, outer, FINE)

    def plane_of(src, halo):
        return lambda i, at: src[i - 4] if 4 <= i < 20 else halo[i]

    build(FINE, 1.0, be, plane_of(b, bb), plane_of(shift, ss), work, rest(0))
    x = sweeps(FINE, work, fields, step, rest)
    pair_residual(FINE, x, work, pair, 0, [*range(4, 10), *range(14, 20)])
    for m in range(8):
        packed[m] = pack_pairs(pair, m, 0, 8)
        put_both(out_a, out_b, SECOND_Y, (0, "mid", m), up_y, packed[m, 3:7, :], packed[m, 1:5, :])
        for field in (1, 2):
            n = MID_Y[field]
            higher, lower = coarse[field - 1, m, 6 - n:6, :], coarse[field - 1, m, 2:2 + n, :]
            put_both(out_a, out_b, SECOND_Y, (field, "mid", m), up_y, higher, lower)
    for i in range(16):
        x_out[i] = x[i + 4, pl.ds(8, 32), :]


def strip_kernel(
    b, beta, shift, packed, ya_in, yb_in,
    wx, wy, wym, wz, wzm, diag, inv, rhs_n, x0, x1, x2, x3, step, pair, ext, be, bb, ss, sums,
):
    (low, high), up_y = y_flags(), upward("gy", 1)
    for x in range(16):
        lo, hi = y_sides(FACE_Y, (1, x), ya_in, yb_in, up_y)
        be[x + 5, 16:25, :] = beta[x, 0:9, :]
        be[x + 5, 31:40, :] = beta[x, 23:32, :]
        be[x + 5, 7:16, :] = lo * low
        be[x + 5, 40:49, :] = hi * high
    for field, src, dst in ((0, b, bb), (2, shift, ss)):
        for x in range(16):
            lo, hi = y_sides(FACE_Y, (field, x), ya_in, yb_in, up_y)
            dst[x + 4, 8:16, :] = src[x, 0:8, :]
            dst[x + 4, 24:32, :] = src[x, 24:32, :]
            dst[x + 4, 0:8, :] = lo
            dst[x + 4, 32:40, :] = hi
    work = (wx, wy, wym, wz, wzm, diag, inv, rhs_n, x0)
    build(STRIP, 1.0, be, lambda i, at: bb[i, at, :], lambda i, at: ss[i, at, :], work, INNER(0))
    sweeps(STRIP, work, (x0, x1, x2, x3), step, INNER)
    pair_residual(STRIP, x3, work, pair, 0, range(10, 14))

    for m in range(8):
        sums[m] = be[2 * m + 5] + be[2 * m + 6]
        sums[m + 8, 0:40, :] = ss[2 * m + 4] + ss[2 * m + 5]
        for field, plane, at in ((1, m, 8), (2, m + 8, 0)):
            dst = ext.at[field - 1, m]
            dst[4:6, :] = pack_pairs(sums, plane, at, 2)
            dst[6:14, :] = packed[field - 1, m]
            dst[14:16, :] = pack_pairs(sums, plane, at + 32, 2)


def edge_kernel(
    b, beta, shift, xa_in, xb_in, ya_in, yb_in, packed, ya2, yb2, *refs,
):
    inner, ext_c, refs = refs[:14], refs[14], refs[15:]
    (x_out, ext, near_a, near_b, far_a, far_b, be, bb, ss), outer = refs[:9], refs[9:]
    near, (low, high) = x_flags(), y_flags()
    up_x, up_y = upward("gx", 1), upward("gy", 1)
    own = (b, beta, shift)

    def sides(field, x):
        if 0 <= x < 16:
            return y_sides(FACE_Y, (field, x), ya_in, yb_in, up_y)
        return y_sides(SECOND_Y, (field, "fine", x), ya2, yb2, up_y)

    for x in [*range(-5, 2), *range(14, 21)]:
        p = fine_plane(1, x, own, xa_in, xb_in, up_x)
        lo, hi = sides(1, x)
        n = lo.shape[0]
        f = 1.0 if 0 <= x < 16 else near[-1] if x < 0 else near[1]
        if not 0 <= x < 16:
            p = p * f
        be[x + 5, 16:25, :] = p[0:9]
        be[x + 5, 31:40, :] = p[23:32]
        be[x + 5, pl.ds(16 - n, n), :] = lo * (low * f)
        be[x + 5, pl.ds(40, n), :] = hi * (high * f)
    for field, dst in ((0, bb), (2, ss)):
        for x in [*range(-4, 1), *range(15, 20)]:
            p = fine_plane(field, x, own, xa_in, xb_in, up_x)
            lo, hi = sides(field, x)
            n = lo.shape[0]
            dst[x + 4, 8:16, :] = p[0:8]
            dst[x + 4, 24:32, :] = p[24:32]
            dst[x + 4, pl.ds(8 - n, n), :] = lo
            dst[x + 4, pl.ds(32, n), :] = hi
    work, fields, step, pair = split_work(inner, outer, STRIP)
    build(STRIP, 1.0, be, lambda i, at: bb[i, at, :], lambda i, at: ss[i, at, :], work, rest(0))
    x = sweeps(STRIP, work, fields, step, rest)
    pair_residual(STRIP, x, work, pair, 0, [*range(4, 10), *range(14, 20)])
    for m in range(8):
        lo, hi = y_sides(SECOND_Y, (0, "mid", m), ya2, yb2, up_y)
        ext[0, m, 1:5, :] = lo
        ext[0, m, 5:7, :] = pack_pairs(pair, m, 4, 2)
        ext[0, m, 7:13, :] = packed[m, 1:7, :]
        ext[0, m, 13:15, :] = pack_pairs(pair, m, 28, 2)
        ext[0, m, 15:19, :] = hi
        for field in (1, 2):
            n = MID_Y[field]
            lo, hi = y_sides(SECOND_Y, (field, "mid", m), ya2, yb2, up_y)
            ext[field, m, 4 - n:4, :] = lo * low if field == 1 else lo
            ext[field, m, 4:16, :] = ext_c[field - 1, m, 4:16, :]
            ext[field, m, 16:16 + n, :] = hi * high if field == 1 else hi
    up2 = upward("gx", 2)
    for rows, up, a, c, first in ((NEAR_X, up_x, near_a, near_b, 1), (FAR_X, up2, far_a, far_b, 9)):
        for field, d in rows:
            n = side_rows(field, d)
            at = pl.ds(6 - n, 8 + 2 * n)
            higher, lower = ext[field, 8 - d + (first - 1), at, :], ext[field, d - first, at, :]
            put_both(a, c, rows, (field, d), up, higher, lower)
    for i in range(16):
        x_out[i, 0:4, :] = x[i + 4, pl.ds(16, 4), :]
        x_out[i, 4:8, :] = x[i + 4, pl.ds(36, 4), :]


def spread(dst, plane, start, a, b):
    n = a.shape[0]
    even = lanes(n) % 2 == 0
    dst[plane, pl.ds(start, n, 2), :] = jnp.where(even, a, roll(b, 1))
    dst[plane, pl.ds(start + 1, n, 2), :] = jnp.where(even, roll(a, -1), b)


def gather(field, d, ext, near, far=None):
    if d <= 0:
        n = side_rows(field, 0)
        at = pl.ds(6 - n, 8 + 2 * n)
        return ext[field, -d, at, :], ext[field, 7 + d, at, :]
    hop, rows, (a, c) = (1, NEAR_X, near) if d <= 8 else (2, FAR_X, far)
    u = upward("gx", hop)
    a, c = pick(a, rows, (field, d)), pick(c, rows, (field, d))
    lower, higher = jnp.where(u, c, a), jnp.where(u, a, c)
    if field == 1:
        flags = x_flags()
        return lower * flags[-hop], higher * flags[hop]
    return lower, higher


def unpack_mid(field, planes, dst, first, reach, *messages):
    for i in planes:
        a, b = gather(field, reach - i, *messages)
        spread(dst, i, first - (a.shape[0] - 8), a, b)


def down_sample(pair, plane):
    low_pair = lanes(16) % 4 < 2
    s = pair[plane, pl.ds(4, 16, 2), :] + pair[plane, pl.ds(5, 16, 2), :]
    return (s + jnp.where(low_pair, roll(s, -2), roll(s, 2))) * 0.125


def pair_mid_residual(src, work, pair, planes):
    diag, held = work[5], {}

    def emit(i, lo, n, cur, e):
        r = e * diag[i, pl.ds(lo, n), :]
        if i % 2 == 0:
            held[0] = lo, n, r
        else:
            lo0, n0, r0 = held[0]
            at, end = max(lo, lo0), min(lo + n, lo0 + n0)
            total = r0[at - lo0:end - lo0] + r[at - lo:end - lo]
            pair[(i - 4) // 2, pl.ds(at, end - at), :] = total

    scaled_residual(MID, src, planes, 6, work, emit)


def MID_INNER(k):
    return range(3 + k, 14)


def mid_kernel(
    ext, near_a, near_b,
    wx, wy, wym, wz, wzm, diag, inv, rhs_n, x0, x1, x2, x3, step, pair,
    wx2, wy2, wym2, wz2, wzm2, diag2, inv2,
    be, bb, ss, be2, ss2, sums,
):
    messages = ext, (near_a, near_b)
    unpack_mid(1, range(3, 15), be, 20, 11, *messages)
    unpack_mid(0, range(3, 14), bb, 12, 10, *messages)
    unpack_mid(2, range(3, 14), ss, 12, 10, *messages)
    be[15, pl.ds(8, 40), :] = swap_lanes(be[14, pl.ds(8, 40), :])
    work = (wx, wy, wym, wz, wzm, diag, inv, rhs_n, x0)
    build(MID, 0.25, be, lambda i, at: bb[i, at, :], lambda i, at: ss[i, at, :], work, MID_INNER(0))
    sweeps(MID, work, (x0, x1, x2, x3), step, MID_INNER)
    pair_mid_residual(x3, work, pair, range(8, 14))

    for m in range(6):
        sums[m] = be[2 * m + 3, pl.ds(8, 40), :] + be[2 * m + 4, pl.ds(8, 40), :]
    for m in range(5):
        sums[6 + m] = ss[2 * m + 4] + ss[2 * m + 5]
    for m in range(6):
        be2[m, 8:24, :] = down_sample(sums, m)
    be2[6, 8:24, :] = swap_lanes(be2[5, 8:24, :])
    for m in range(5):
        ss2[m] = down_sample(sums, 6 + m)
    work2 = (wx2, wy2, wym2, wz2, wzm2, diag2, inv2, None, None)
    build(LOW, 0.0625, be2, None, lambda i, at: ss2[i, at, :], work2)


def coarse_kernel(
    x_fine, x_edge, ext, near_a, near_b, far_a, far_b,
    i_wx, i_wy, i_wym, i_wz, i_wzm, i_diag, i_inv, i_rhs_n, i_x0, i_x1, i_x2, i_x3, i_step, i_pair,
    wx2, wy2, wym2, wz2, wzm2, diag2, inv2,
    out, mid_out,
    be, bb, ss, wx, wy, wym, wz, wzm, diag, inv, rhs_n, x0, x1, x2, x3, step, pair,
    rhs_n2, xa2, xb2, step2, rep_mid, rep_fine, mids,
):
    messages = ext, (near_a, near_b), (far_a, far_b)
    unpack_mid(1, range(5), be, 20, 11, *messages)
    unpack_mid(0, range(3), bb, 12, 10, *messages)
    unpack_mid(2, range(3), ss, 12, 10, *messages)
    inner = (i_wx, i_wy, i_wym, i_wz, i_wzm, i_diag, i_inv, i_rhs_n, i_x0)
    outer = (wx, wy, wym, wz, wzm, diag, inv, rhs_n, x0)
    work = tuple(Split(i, o, 3, 14) for i, o in zip(inner, outer))
    fields = [work[8]] + [Split(i, o, 3 + k, 14) for k, i, o in ((1, i_x1, x1), (2, i_x2, x2), (3, i_x3, x3))]

    def rest(k):
        return range(k, 3 + k)

    build(MID, 0.25, be, lambda i, at: bb[i, at, :], lambda i, at: ss[i, at, :], work, rest(0))
    x1 = sweeps(MID, work, fields, StepSplit(i_step, step, MID_INNER(1), MID), rest)
    pair = Split(i_pair, pair, 2, 4)
    pair_mid_residual(x1, work, pair, range(4, 8))
    for i in range(LOW.planes):
        lo, n = LOW.span(i, LOW.depth)
        begin(LOW, i, lo, n, lambda i, at: down_sample(pair, i), inv2[i], rhs_n2, xa2)
    work2 = (wx2, wy2, wym2, wz2, wzm2, diag2, inv2, rhs_n2, xa2)
    x2 = smooth(LOW, work2, xb2, step2)

    for m in range(2):
        low_x = x2[m + 3, pl.ds(12, 8), :]
        rep_mid[m, pl.ds(0, 8, 2), :] = low_x
        rep_mid[m, pl.ds(1, 8, 2), :] = low_x
    even = lanes(16) % 2 == 0
    for m in range(4):
        both = x1[m + 10, pl.ds(20, 16), :] + rep_mid[m // 2]
        for x, mid in (
            (m, jnp.where(even, both, roll(both, 1))),
            (7 - m, jnp.where(even, roll(both, -1), both)),
        ):
            mids[pl.ds(16 * x, 16), :] = mid
            rep_fine[x, pl.ds(0, 16, 2), :] = mid
            rep_fine[x, pl.ds(1, 16, 2), :] = mid
    for i in range(16):
        out[i, 4:28, :] = x_fine[i, 4:28, :] + rep_fine[i // 2, 4:28, :]
        out[i, 0:4, :] = x_edge[i, 0:4, :] + rep_fine[i // 2, 0:4, :]
        out[i, 28:32, :] = x_edge[i, 4:8, :] + rep_fine[i // 2, 28:32, :]
    row = lax.broadcasted_iota(jnp.int32, (128, 64), 0)
    col = lax.broadcasted_iota(jnp.int32, (128, 64), 1)
    even_lanes = jnp.where(row == 2 * col, 1.0, 0.0).astype(F32)
    compact = jnp.dot(mids[...], even_lanes, precision=lax.Precision.HIGHEST, preferred_element_type=F32)
    for m in range(8):
        mid_out[m] = compact[16 * m:16 * m + 16]


def vmem(*shape):
    return pltpu.VMEM(shape, F32)


def call(kernel, ins, outs, scratch=(), limit=24 * 2**20, space=pltpu.VMEM):
    return pl.pallas_call(
        kernel,
        out_shape=[jax.ShapeDtypeStruct(s, F32) for s in outs],
        in_specs=[pl.BlockSpec(memory_space=space)] * len(ins),
        out_specs=[pl.BlockSpec(memory_space=pltpu.VMEM)] * len(outs),
        scratch_shapes=list(scratch),
        compiler_params=pltpu.CompilerParams(vmem_limit_bytes=limit),
    )(*ins)


def work_shapes(planes, rows, pairs):
    flat, tall = (planes, rows, 128), (planes + 1, rows + 16, 128)
    return [flat] * 8 + [tall] * 4 + [flat, (pairs, rows, 128)]


def level_scratch(planes, rows):
    return [vmem(planes + 2, rows + 16, 128)] + [vmem(planes, rows, 128)] * 2


def work_scratch(planes, rows, pairs):
    return [vmem(*shape) for shape in work_shapes(planes, rows, pairs)]


def local(b, beta, shift):
    fields = (b, beta, shift)
    a, c = pack_fine_x(fields)
    xs = swaps(a, c, "gx", 1)
    a, c, packed_c = call(
        pack_face_y, fields, [(FACE_Y_SIZE, 128)] * 2 + [(2, 8, 8, 128)], [vmem(16, 32, 128)]
    )
    ys = swaps(a, c, "gy", 1)
    inner = call(inner_kernel, (*fields, *ys), work_shapes(24, 32, 8), [vmem(26, 48, 128)])
    x_fine, packed, a, c = call(
        outer_kernel,
        (*fields, packed_c, *xs, *ys, *inner),
        [(16, 32, 128), (8, 8, 128)] + [(SECOND_Y_SIZE, 128)] * 2,
        level_scratch(24, 32) + work_scratch(24, 32, 8),
    )
    second = swaps(a, c, "gy", 1)
    *inner, ext_c = call(
        strip_kernel,
        (*fields, packed_c, *ys),
        work_shapes(24, 40, 8) + [(2, 8, 24, 128)],
        level_scratch(24, 40) + [vmem(16, 56, 128)],
    )
    x_edge, ext, near_a, near_b, far_a, far_b = call(
        edge_kernel,
        (*fields, *xs, *ys, packed, *second, *inner, ext_c),
        [(16, 8, 128), (3, 8, 24, 128)] + [(NEAR_X_SIZE, 128)] * 2 + [(FAR_X_SIZE, 128)] * 2,
        level_scratch(24, 40) + work_scratch(24, 40, 8),
    )
    near = swaps(near_a, near_b, "gx", 1)
    far = swaps(far_a, far_b, "gx", 2)
    small = (5, 16, 128)
    inner = call(
        mid_kernel,
        (ext, *near),
        work_shapes(14, 40, 5) + [small] * 7,
        level_scratch(14, 40) + [vmem(7, 32, 128), vmem(*small), vmem(11, 40, 128)],
    )
    return tuple(call(
        coarse_kernel,
        (x_fine, x_edge, ext, *near, *far, *inner),
        [(16, 32, 128), (8, 16, 64)],
        level_scratch(14, 40) + work_scratch(14, 40, 5)
        + [vmem(*small), vmem(6, 32, 128), vmem(6, 32, 128), vmem(*small)]
        + [vmem(2, 16, 128), vmem(8, 32, 128), vmem(128, 128)],
    ))


def solution(mesh):
    placed = P("gx", "gy", None)
    return jax.shard_map(
        local, mesh=mesh, in_specs=(placed,) * 3, out_specs=(placed, placed), check_vma=False
    )
```

```python
import jax
import jax.numpy as jnp
from jax import lax
from jax.experimental import pallas as pl
from jax.experimental.pallas import tpu as pltpu
from jax.sharding import PartitionSpec as P

SWEEPS = 4
THETA, DELTA = 1.15, 0.85
SIGMA = THETA / DELTA
F32 = jnp.float32


def coefficients():
    rho, out = 1.0 / SIGMA, []
    for _ in range(SWEEPS - 1):
        new = 1.0 / (2.0 * SIGMA - rho)
        out.append((new * rho, 2.0 * new / DELTA))
        rho = new
    return out


def lanes(rows):
    return lax.broadcasted_iota(jnp.int32, (rows, 128), 1)


def roll(value, shift):
    return pltpu.roll(value, shift % 128, 1)


class StepSplit:
    def __init__(self, inner, outer, planes, level):
        self.inner, self.outer, self.planes, self.level, self.own = inner, outer, planes, level, set()

    def __getitem__(self, at):
        return (self.inner if at[0] in self.planes and at[0] not in self.own else self.outer)[at]

    def __setitem__(self, at, value):
        self.outer[at] = value
        if at[1].start >= self.level.bases[-1]:
            self.own.add(at[0])


class Level:
    def __init__(self, depth, own_planes, rows, own_rows, rep, folded=False, bases=(0,)):
        self.bases = bases
        self.depth, self.own, self.rep, self.folded = depth, own_planes, rep, folded
        self.planes = depth + own_planes // 2 if folded else own_planes + 2 * depth
        self.rows, self.first_row, self.own_rows = rows, (rows - own_rows) // 2, own_rows

    def cut(self, k):
        return k, self.planes - (0 if self.folded else k)

    def span(self, plane, reach):
        x = plane - self.depth
        far = max(0, -x) if self.folded else max(0, -x, x - self.own + 1)
        side = max(0, reach - far)
        lo = max(0, self.first_row - side) // 8 * 8
        hi = min(self.rows, -(-(self.first_row + self.own_rows + side) // 8) * 8)
        return lo, hi - lo

    def put(self, dst, i, at, value):
        dst[i, at, :] = value
        if self.folded and i == self.planes - 1:
            dst[i + 1, at, :] = swap_lanes(value)


def swap_lanes(value):
    return jnp.where(lanes(value.shape[0]) % 2 == 0, roll(value, -1), roll(value, 1))


def build(level, scale, beta, rhs, shift, work, planes=None):
    wx, wy, wym, wz, wzm, diag, inv, rhs_n, start = work
    rep, half, last_span = level.rep, 0.5 * scale, None
    planes = range(level.planes) if planes is None else planes
    for base, i in [(base, i) for base in level.bases for i in planes]:
        lo, n = level.span(i, level.depth)
        lo += base
        if (lo, n, i) != last_span:
            prev, cur = beta[i, pl.ds(8 + lo, n), :], beta[i + 1, pl.ds(8 + lo, n), :]
            wx_prev = half * (prev + cur)
            if i:
                wx[i - 1, pl.ds(lo, n), :] = wx_prev
            lane = lanes(n)
            first, last = lane < rep, lane >= 128 - rep
        last_span = (lo, n, i + 1)
        at = pl.ds(lo, n)
        nxt = beta[i + 2, pl.ds(8 + lo, n), :]
        wx_next = half * (cur + nxt)
        w_up = half * (cur + beta[i + 1, pl.ds(9 + lo, n), :])
        w_down = half * (cur + beta[i + 1, pl.ds(7 + lo, n), :])
        w_right = half * (cur + jnp.where(last, 0.0, roll(cur, -rep)))
        w_left = half * (cur + jnp.where(first, 0.0, roll(cur, rep)))
        d = shift(i, at) + (wx_prev + wx_next + w_up + w_down + w_right + w_left)
        iv = jnp.where(cur > 0.0, 1.0 / d, 0.0)
        wx[i, at, :] = wx_next
        wy[i, at, :] = w_up
        wym[i, at, :] = w_down
        wz[i, at, :] = jnp.where(last, 0.0, w_right)
        wzm[i, at, :] = jnp.where(first, 0.0, w_left)
        diag[i, at, :] = d
        inv[i, at, :] = iv
        if rhs is not None:
            begin(level, i, lo, n, rhs, iv, rhs_n, start)
        cur, wx_prev = nxt, wx_next


def begin(level, i, lo, n, rhs, iv, rhs_n, start):
    c = rhs(i, pl.ds(lo, n)) * iv
    rhs_n[i, pl.ds(lo, n), :] = c
    level.put(start, i, pl.ds(8 + lo, n), c * (1.0 / THETA))


def scaled_residual(level, src, planes, reach, work, emit):
    wx, wy, wym, wz, wzm, _, inv, rhs_n, _ = work
    rep, last_span = level.rep, None
    for base, i in [(base, i) for base in level.bases for i in planes]:
        lo, n = level.span(i, reach)
        lo += base
        at, dom = pl.ds(lo, n), pl.ds(8 + lo, n)
        if (lo, n, i) != last_span:
            prev, cur, wx_prev = src[i - 1, dom, :], src[i, dom, :], wx[i - 1, at, :]
        last_span = (lo, n, i + 1)
        nxt, wx_next = src[i + 1, dom, :], wx[i, at, :]
        t = wx_next * nxt + wx_prev * prev
        t = t + wy[i, at, :] * src[i, pl.ds(9 + lo, n), :] + wym[i, at, :] * src[i, pl.ds(7 + lo, n), :]
        t = t + wz[i, at, :] * roll(cur, -rep) + wzm[i, at, :] * roll(cur, rep)
        emit(i, lo, n, cur, rhs_n[i, at, :] + inv[i, at, :] * t - cur)
        prev, cur, wx_prev = cur, nxt, wx_next


def sweeps(level, work, fields, step, planes):
    for k, (a, g) in enumerate(coefficients()):

        def emit(i, lo, n, cur, e, a=a, g=g, k=k, dst=fields[k + 1]):
            before = cur if k == 0 else step[i, pl.ds(lo, n), :]
            d = a * before + g * e
            if k < SWEEPS - 2:
                step[i, pl.ds(lo, n), :] = d
            level.put(dst, i, pl.ds(8 + lo, n), cur + d)

        scaled_residual(level, fields[k], planes(k + 1), level.depth - k - 1, work, emit)
    return fields[-1]


def smooth(level, work, other, step):
    fields = (work[8], other) * 2
    return sweeps(level, work, fields, step, lambda k: range(*level.cut(k)))


class Split:
    def __init__(self, inner, outer, first, last):
        self.inner, self.outer, self.first, self.last = inner, outer, first, last

    def __getitem__(self, at):
        return (self.inner if self.first <= at[0] <= self.last else self.outer)[at]

    def __setitem__(self, at, value):
        if not self.first <= at[0] <= self.last:
            self.outer[at] = value


FINE = Level(4, 16, 32, 32, 1)
STRIP = Level(4, 16, 16, 16, 1, bases=(0, 24))
MID = Level(10, 8, 40, 16, 2, folded=True)
LOW = Level(3, 4, 16, 8, 4, folded=True)


def table(entries):
    rows, at = {}, 0
    for key, count in entries:
        rows[key] = (at, count)
        at += count
    return rows, -(-at // 8) * 8


FACE_Y, FACE_Y_SIZE = table([((f, x), 8) for x in range(16) for f in (0, 2)] + [((1, x), 9) for x in range(16)])

MID_Y = {0: 4, 1: 4, 2: 3}
HALO_X = [-1, -2, -3, -4, -5, 16, 17, 18, 19, 20]


def away(x):
    return -x if x < 0 else x - 15


SECOND_Y, SECOND_Y_SIZE = table(
    [((f, "mid", m), MID_Y[f]) for f in range(3) for m in range(8)]
    + [((f, "fine", x), 8 + (f == 1) - away(x)) for f in range(3) for x in HALO_X if away(x) < 5 + (f == 1)]
)


def side_rows(field, far):
    return -(-max(0, 10 + (field == 1) - far) // 2)


NEAR_X, NEAR_X_SIZE = table([((f, d), 8 + 2 * side_rows(f, d)) for f in range(3) for d in range(1, 9)])
FAR_X, FAR_X_SIZE = table([((f, d), 8 + 2 * side_rows(f, d)) for f in range(3) for d in range(9, 11 + (f == 1))])


def flag(condition):
    return jnp.where(condition, 1.0, 0.0).astype(F32)


def x_flags():
    i, n = lax.axis_index("gx"), lax.axis_size("gx")
    return {-2: flag(i > 1), -1: flag(i > 0), 1: flag(i < n - 1), 2: flag(i < n - 2)}


def y_flags():
    j, n = lax.axis_index("gy"), lax.axis_size("gy")
    return flag(j > 0), flag(j < n - 1)


def upward(axis, by, low=0):
    return lax.rem(lax.axis_index(axis) + low * by, 2 * by) >= by


def swaps(first, second, axis, by, low=0):
    axes = ("gx", "gy")
    size = [lax.axis_size(name) for name in axes]
    dim = axes.index(axis)
    orders = []
    for sign in (1, -1):
        pairs = []
        for i in range(size[0]):
            for j in range(size[1]):
                to = [i, j]
                to[dim] += sign * by if (to[dim] + low * by) % (2 * by) >= by else -sign * by
                if not 0 <= to[dim] < size[dim]:
                    to = [i, j]
                    to[1 - dim] ^= 1
                pairs.append((i * size[1] + j, to[0] * size[1] + to[1]))
        orders.append(pairs)
    return lax.ppermute(first, axes, orders[0]), lax.ppermute(second, axes, orders[1])


COUNTS = (4, 5, 4)
STARTS = (0, 4, 9)


def pack_fine_x(fields):
    ends = [f[:n] for f, n in zip(fields, COUNTS)] + [f[16 - n:] for f, n in zip(fields, COUNTS)]
    first, last = jnp.concatenate(ends[:3], axis=0), jnp.concatenate(ends[3:], axis=0)
    first, last = lax.optimization_barrier((first, last))
    up = upward("gx", 1)
    return jnp.where(up, last, first), jnp.where(up, first, last)


def fine_plane(field, x, own, in_a, in_b, up):
    if 0 <= x < 16:
        return own[field][x]
    i = STARTS[field] + (x + COUNTS[field] if x < 0 else x - 16)
    return jnp.where(up, in_b[i], in_a[i]) if x < 0 else jnp.where(up, in_a[i], in_b[i])


def pick(ref, rows, key):
    at, count = rows[key]
    return ref[pl.ds(at, count), :]


def put_both(out_a, out_b, rows, key, up, higher, lower):
    at, count = rows[key]
    out_a[pl.ds(at, count), :] = jnp.where(up, higher, lower)
    out_b[pl.ds(at, count), :] = jnp.where(up, lower, higher)


def pack_face_y(b, beta, shift, out_a, out_b, packed, pair):
    up = upward("gy", 1)
    for field, src in ((1, beta), (2, shift)):
        for m in range(8):
            at = 8 * field + m - 8
            pair[at] = src[2 * m] + src[2 * m + 1]
            packed[field - 1, m] = pack_pairs(pair, at, 0, 8)
    for field, src in enumerate((b, beta, shift)):
        for x in range(16):
            n = FACE_Y[field, x][1]
            put_both(out_a, out_b, FACE_Y, (field, x), up, src[x, pl.ds(32 - n, n), :], src[x, pl.ds(0, n), :])


def y_sides(rows, key, in_a, in_b, up):
    a, b = pick(in_a, rows, key), pick(in_b, rows, key)
    return jnp.where(up, b, a), jnp.where(up, a, b)


def pack_pairs(pair, plane, start, count):
    even = lanes(count) % 2 == 0
    e = pair[plane, pl.ds(start, count, 4), :] + pair[plane, pl.ds(start + 1, count, 4), :]
    o = pair[plane, pl.ds(start + 2, count, 4), :] + pair[plane, pl.ds(start + 3, count, 4), :]
    return jnp.where(even, e + roll(e, -1), o + roll(o, 1)) * 0.125


def pair_residual(level, src, work, pair, first, planes):
    diag, held = work[5], {}

    def emit(i, lo, n, cur, e):
        r = e * diag[i, pl.ds(lo, n), :]
        if i % 2 == 0:
            held[0] = r
        else:
            pair[first + (i - 4) // 2, pl.ds(lo, n), :] = held[0] + r

    scaled_residual(level, src, planes, 0, work, emit)


def INNER(k):
    return range(5 + k, 19 - k)


def rest(k):
    return [i for i in range(k, 24 - k) if i not in INNER(k)]


def split_work(inner, outer, level):
    work = tuple(Split(i, o, 5, 18) for i, o in zip(inner[:9], outer[:9]))
    fields = [work[8]]
    for k in (1, 2, 3):
        fields.append(Split(inner[8 + k], outer[8 + k], INNER(k)[0], INNER(k)[-1]))
    step = StepSplit(inner[12], outer[12], INNER(1), level)
    return work, fields, step, Split(inner[13], outer[13], 3, 4)


def edge_rows(be, x, beta, ya_in, yb_in):
    (low, high), up = y_flags(), upward("gy", 1)
    lo, hi = y_sides(FACE_Y, (1, x), ya_in, yb_in, up)
    be[x + 5, 8:40, :] = beta[x]
    be[x + 5, 7:8, :] = lo[8:9] * low
    be[x + 5, 40:41, :] = hi[0:1] * high


def inner_kernel(
    b, beta, shift, ya_in, yb_in,
    wx, wy, wym, wz, wzm, diag, inv, rhs_n, x0, x1, x2, x3, step, pair, be,
):
    for x in range(16):
        edge_rows(be, x, beta, ya_in, yb_in)
    work = (wx, wy, wym, wz, wzm, diag, inv, rhs_n, x0)
    build(FINE, 1.0, be, lambda i, at: b[i - 4], lambda i, at: shift[i - 4], work, INNER(0))
    sweeps(FINE, work, (x0, x1, x2, x3), step, INNER)
    pair_residual(FINE, x3, work, pair, 0, range(10, 14))


def outer_kernel(
    b, beta, shift, coarse, xa_in, xb_in, ya_in, yb_in, *refs,
):
    inner, refs = refs[:14], refs[14:]
    (x_out, packed, out_a, out_b, be, bb, ss), outer = refs[:7], refs[7:]
    near, up_x, up_y = x_flags(), upward("gx", 1), upward("gy", 1)
    own = (b, beta, shift)
    for x in [*range(-5, 2), *range(14, 21)]:
        if 0 <= x < 16:
            edge_rows(be, x, beta, ya_in, yb_in)
            continue
        p = fine_plane(1, x, own, xa_in, xb_in, up_x)
        be[x + 5, 8:40, :] = p * (near[-1] if x < 0 else near[1])
        at = SECOND_Y[1, "fine", x][1]
        put_both(out_a, out_b, SECOND_Y, (1, "fine", x), up_y, p[32 - at:32], p[0:at])
    for field, dst in ((0, bb), (2, ss)):
        for x in [*range(-4, 0), *range(16, 20)]:
            p = fine_plane(field, x, own, xa_in, xb_in, up_x)
            dst[x + 4] = p
            at = SECOND_Y[field, "fine", x][1]
            put_both(out_a, out_b, SECOND_Y, (field, "fine", x), up_y, p[32 - at:32], p[0:at])
    work, fields, step, pair = split_work(inner, outer, FINE)

    def plane_of(src, halo):
        return lambda i, at: src[i - 4] if 4 <= i < 20 else halo[i]

    build(FINE, 1.0, be, plane_of(b, bb), plane_of(shift, ss), work, rest(0))
    x = sweeps(FINE, work, fields, step, rest)
    pair_residual(FINE, x, work, pair, 0, [*range(4, 10), *range(14, 20)])
    for m in range(8):
        packed[m] = pack_pairs(pair, m, 0, 8)
        put_both(out_a, out_b, SECOND_Y, (0, "mid", m), up_y, packed[m, 3:7, :], packed[m, 1:5, :])
        for field in (1, 2):
            n = MID_Y[field]
            higher, lower = coarse[field - 1, m, 6 - n:6, :], coarse[field - 1, m, 2:2 + n, :]
            put_both(out_a, out_b, SECOND_Y, (field, "mid", m), up_y, higher, lower)
    for i in range(16):
        x_out[i] = x[i + 4, pl.ds(8, 32), :]


def strip_kernel(
    b, beta, shift, packed, ya_in, yb_in,
    wx, wy, wym, wz, wzm, diag, inv, rhs_n, x0, x1, x2, x3, step, pair, ext, be, bb, ss, sums,
):
    (low, high), up_y = y_flags(), upward("gy", 1)
    for x in range(16):
        lo, hi = y_sides(FACE_Y, (1, x), ya_in, yb_in, up_y)
        be[x + 5, 16:25, :] = beta[x, 0:9, :]
        be[x + 5, 31:40, :] = beta[x, 23:32, :]
        be[x + 5, 7:16, :] = lo * low
        be[x + 5, 40:49, :] = hi * high
    for field, src, dst in ((0, b, bb), (2, shift, ss)):
        for x in range(16):
            lo, hi = y_sides(FACE_Y, (field, x), ya_in, yb_in, up_y)
            dst[x + 4, 8:16, :] = src[x, 0:8, :]
            dst[x + 4, 24:32, :] = src[x, 24:32, :]
            dst[x + 4, 0:8, :] = lo
            dst[x + 4, 32:40, :] = hi
    work = (wx, wy, wym, wz, wzm, diag, inv, rhs_n, x0)
    build(STRIP, 1.0, be, lambda i, at: bb[i, at, :], lambda i, at: ss[i, at, :], work, INNER(0))
    sweeps(STRIP, work, (x0, x1, x2, x3), step, INNER)
    pair_residual(STRIP, x3, work, pair, 0, range(10, 14))

    for m in range(8):
        sums[m] = be[2 * m + 5] + be[2 * m + 6]
        sums[m + 8, 0:40, :] = ss[2 * m + 4] + ss[2 * m + 5]
        for field, plane, at in ((1, m, 8), (2, m + 8, 0)):
            dst = ext.at[field - 1, m]
            dst[4:6, :] = pack_pairs(sums, plane, at, 2)
            dst[6:14, :] = packed[field - 1, m]
            dst[14:16, :] = pack_pairs(sums, plane, at + 32, 2)


def edge_kernel(
    b, beta, shift, xa_in, xb_in, ya_in, yb_in, packed, ya2, yb2, *refs,
):
    inner, ext_c, refs = refs[:14], refs[14], refs[15:]
    (x_out, ext, near_a, near_b, far_a, far_b, be, bb, ss), outer = refs[:9], refs[9:]
    near, (low, high) = x_flags(), y_flags()
    up_x, up_y = upward("gx", 1), upward("gy", 1)
    own = (b, beta, shift)

    def sides(field, x):
        if 0 <= x < 16:
            return y_sides(FACE_Y, (field, x), ya_in, yb_in, up_y)
        return y_sides(SECOND_Y, (field, "fine", x), ya2, yb2, up_y)

    for x in [*range(-5, 2), *range(14, 21)]:
        p = fine_plane(1, x, own, xa_in, xb_in, up_x)
        lo, hi = sides(1, x)
        n = lo.shape[0]
        f = 1.0 if 0 <= x < 16 else near[-1] if x < 0 else near[1]
        if not 0 <= x < 16:
            p = p * f
        be[x + 5, 16:25, :] = p[0:9]
        be[x + 5, 31:40, :] = p[23:32]
        be[x + 5, pl.ds(16 - n, n), :] = lo * (low * f)
        be[x + 5, pl.ds(40, n), :] = hi * (high * f)
    for field, dst in ((0, bb), (2, ss)):
        for x in [*range(-4, 1), *range(15, 20)]:
            p = fine_plane(field, x, own, xa_in, xb_in, up_x)
            lo, hi = sides(field, x)
            n = lo.shape[0]
            dst[x + 4, 8:16, :] = p[0:8]
            dst[x + 4, 24:32, :] = p[24:32]
            dst[x + 4, pl.ds(8 - n, n), :] = lo
            dst[x + 4, pl.ds(32, n), :] = hi
    work, fields, step, pair = split_work(inner, outer, STRIP)
    build(STRIP, 1.0, be, lambda i, at: bb[i, at, :], lambda i, at: ss[i, at, :], work, rest(0))
    x = sweeps(STRIP, work, fields, step, rest)
    pair_residual(STRIP, x, work, pair, 0, [*range(4, 10), *range(14, 20)])
    for m in range(8):
        lo, hi = y_sides(SECOND_Y, (0, "mid", m), ya2, yb2, up_y)
        ext[0, m, 1:5, :] = lo
        ext[0, m, 5:7, :] = pack_pairs(pair, m, 4, 2)
        ext[0, m, 7:13, :] = packed[m, 1:7, :]
        ext[0, m, 13:15, :] = pack_pairs(pair, m, 28, 2)
        ext[0, m, 15:19, :] = hi
        for field in (1, 2):
            n = MID_Y[field]
            lo, hi = y_sides(SECOND_Y, (field, "mid", m), ya2, yb2, up_y)
            ext[field, m, 4 - n:4, :] = lo * low if field == 1 else lo
            ext[field, m, 4:16, :] = ext_c[field - 1, m, 4:16, :]
            ext[field, m, 16:16 + n, :] = hi * high if field == 1 else hi
    up2 = upward("gx", 2)
    for rows, up, a, c, first in ((NEAR_X, upward("gx", 1, 1), near_a, near_b, 1), (FAR_X, up2, far_a, far_b, 9)):
        for field, d in rows:
            n = side_rows(field, d)
            at = pl.ds(6 - n, 8 + 2 * n)
            higher, lower = ext[field, 8 - d + (first - 1), at, :], ext[field, d - first, at, :]
            put_both(a, c, rows, (field, d), up, higher, lower)
    for i in range(16):
        x_out[i, 0:4, :] = x[i + 4, pl.ds(16, 4), :]
        x_out[i, 4:8, :] = x[i + 4, pl.ds(36, 4), :]


def spread(dst, plane, start, a, b):
    n = a.shape[0]
    even = lanes(n) % 2 == 0
    dst[plane, pl.ds(start, n, 2), :] = jnp.where(even, a, roll(b, 1))
    dst[plane, pl.ds(start + 1, n, 2), :] = jnp.where(even, roll(a, -1), b)


def gather(field, d, ext, near, far=None):
    if d <= 0:
        n = side_rows(field, 0)
        at = pl.ds(6 - n, 8 + 2 * n)
        return ext[field, -d, at, :], ext[field, 7 + d, at, :]
    hop, rows, (a, c) = (1, NEAR_X, near) if d <= 8 else (2, FAR_X, far)
    u = upward("gx", hop, 2 - hop)
    a, c = pick(a, rows, (field, d)), pick(c, rows, (field, d))
    lower, higher = jnp.where(u, c, a), jnp.where(u, a, c)
    if field == 1:
        flags = x_flags()
        return lower * flags[-hop], higher * flags[hop]
    return lower, higher


def unpack_mid(field, planes, dst, first, reach, *messages):
    for i in planes:
        a, b = gather(field, reach - i, *messages)
        spread(dst, i, first - (a.shape[0] - 8), a, b)


def down_sample(pair, plane):
    low_pair = lanes(16) % 4 < 2
    s = pair[plane, pl.ds(4, 16, 2), :] + pair[plane, pl.ds(5, 16, 2), :]
    return (s + jnp.where(low_pair, roll(s, -2), roll(s, 2))) * 0.125


def pair_mid_residual(src, work, pair, planes):
    diag, held = work[5], {}

    def emit(i, lo, n, cur, e):
        r = e * diag[i, pl.ds(lo, n), :]
        if i % 2 == 0:
            held[0] = lo, n, r
        else:
            lo0, n0, r0 = held[0]
            at, end = max(lo, lo0), min(lo + n, lo0 + n0)
            total = r0[at - lo0:end - lo0] + r[at - lo:end - lo]
            pair[(i - 4) // 2, pl.ds(at, end - at), :] = total

    scaled_residual(MID, src, planes, 6, work, emit)


def MID_INNER(k):
    return range(3 + k, 14)


def mid_kernel(
    ext, near_a, near_b,
    wx, wy, wym, wz, wzm, diag, inv, rhs_n, x0, x1, x2, x3, step, pair,
    wx2, wy2, wym2, wz2, wzm2, diag2, inv2,
    be, bb, ss, be2, ss2, sums,
):
    messages = ext, (near_a, near_b)
    unpack_mid(1, range(3, 15), be, 20, 11, *messages)
    unpack_mid(0, range(3, 14), bb, 12, 10, *messages)
    unpack_mid(2, range(3, 14), ss, 12, 10, *messages)
    be[15, pl.ds(8, 40), :] = swap_lanes(be[14, pl.ds(8, 40), :])
    work = (wx, wy, wym, wz, wzm, diag, inv, rhs_n, x0)
    build(MID, 0.25, be, lambda i, at: bb[i, at, :], lambda i, at: ss[i, at, :], work, MID_INNER(0))
    sweeps(MID, work, (x0, x1, x2, x3), step, MID_INNER)
    pair_mid_residual(x3, work, pair, range(8, 14))

    for m in range(6):
        sums[m] = be[2 * m + 3, pl.ds(8, 40), :] + be[2 * m + 4, pl.ds(8, 40), :]
    for m in range(5):
        sums[6 + m] = ss[2 * m + 4] + ss[2 * m + 5]
    for m in range(6):
        be2[m, 8:24, :] = down_sample(sums, m)
    be2[6, 8:24, :] = swap_lanes(be2[5, 8:24, :])
    for m in range(5):
        ss2[m] = down_sample(sums, 6 + m)
    work2 = (wx2, wy2, wym2, wz2, wzm2, diag2, inv2, None, None)
    build(LOW, 0.0625, be2, None, lambda i, at: ss2[i, at, :], work2)


def coarse_kernel(
    x_fine, x_edge, ext, near_a, near_b, far_a, far_b,
    i_wx, i_wy, i_wym, i_wz, i_wzm, i_diag, i_inv, i_rhs_n, i_x0, i_x1, i_x2, i_x3, i_step, i_pair,
    wx2, wy2, wym2, wz2, wzm2, diag2, inv2,
    out, mid_out,
    be, bb, ss, wx, wy, wym, wz, wzm, diag, inv, rhs_n, x0, x1, x2, x3, step, pair,
    rhs_n2, xa2, xb2, step2, rep_mid, rep_fine, mids,
):
    messages = ext, (near_a, near_b), (far_a, far_b)
    unpack_mid(1, range(5), be, 20, 11, *messages)
    unpack_mid(0, range(3), bb, 12, 10, *messages)
    unpack_mid(2, range(3), ss, 12, 10, *messages)
    inner = (i_wx, i_wy, i_wym, i_wz, i_wzm, i_diag, i_inv, i_rhs_n, i_x0)
    outer = (wx, wy, wym, wz, wzm, diag, inv, rhs_n, x0)
    work = tuple(Split(i, o, 3, 14) for i, o in zip(inner, outer))
    fields = [work[8]] + [Split(i, o, 3 + k, 14) for k, i, o in ((1, i_x1, x1), (2, i_x2, x2), (3, i_x3, x3))]

    def rest(k):
        return range(k, 3 + k)

    build(MID, 0.25, be, lambda i, at: bb[i, at, :], lambda i, at: ss[i, at, :], work, rest(0))
    x1 = sweeps(MID, work, fields, StepSplit(i_step, step, MID_INNER(1), MID), rest)
    pair = Split(i_pair, pair, 2, 4)
    pair_mid_residual(x1, work, pair, range(4, 8))
    for i in range(LOW.planes):
        lo, n = LOW.span(i, LOW.depth)
        begin(LOW, i, lo, n, lambda i, at: down_sample(pair, i), inv2[i], rhs_n2, xa2)
    work2 = (wx2, wy2, wym2, wz2, wzm2, diag2, inv2, rhs_n2, xa2)
    x2 = smooth(LOW, work2, xb2, step2)

    for m in range(2):
        low_x = x2[m + 3, pl.ds(12, 8), :]
        rep_mid[m, pl.ds(0, 8, 2), :] = low_x
        rep_mid[m, pl.ds(1, 8, 2), :] = low_x
    even = lanes(16) % 2 == 0
    for m in range(4):
        both = x1[m + 10, pl.ds(20, 16), :] + rep_mid[m // 2]
        for x, mid in (
            (m, jnp.where(even, both, roll(both, 1))),
            (7 - m, jnp.where(even, roll(both, -1), both)),
        ):
            mids[pl.ds(16 * x, 16), :] = mid
            rep_fine[x, pl.ds(0, 16, 2), :] = mid
            rep_fine[x, pl.ds(1, 16, 2), :] = mid
    for i in range(16):
        out[i, 4:28, :] = x_fine[i, 4:28, :] + rep_fine[i // 2, 4:28, :]
        out[i, 0:4, :] = x_edge[i, 0:4, :] + rep_fine[i // 2, 0:4, :]
        out[i, 28:32, :] = x_edge[i, 4:8, :] + rep_fine[i // 2, 28:32, :]
    row = lax.broadcasted_iota(jnp.int32, (128, 64), 0)
    col = lax.broadcasted_iota(jnp.int32, (128, 64), 1)
    even_lanes = jnp.where(row == 2 * col, 1.0, 0.0).astype(F32)
    compact = jnp.dot(mids[...], even_lanes, precision=lax.Precision.HIGHEST, preferred_element_type=F32)
    for m in range(8):
        mid_out[m] = compact[16 * m:16 * m + 16]


def vmem(*shape):
    return pltpu.VMEM(shape, F32)


def call(kernel, ins, outs, scratch=(), limit=24 * 2**20, space=pltpu.VMEM):
    return pl.pallas_call(
        kernel,
        out_shape=[jax.ShapeDtypeStruct(s, F32) for s in outs],
        in_specs=[pl.BlockSpec(memory_space=space)] * len(ins),
        out_specs=[pl.BlockSpec(memory_space=pltpu.VMEM)] * len(outs),
        scratch_shapes=list(scratch),
        compiler_params=pltpu.CompilerParams(vmem_limit_bytes=limit),
    )(*ins)


def work_shapes(planes, rows, pairs):
    flat, tall = (planes, rows, 128), (planes + 1, rows + 16, 128)
    return [flat] * 8 + [tall] * 4 + [flat, (pairs, rows, 128)]


def level_scratch(planes, rows):
    return [vmem(planes + 2, rows + 16, 128)] + [vmem(planes, rows, 128)] * 2


def work_scratch(planes, rows, pairs):
    return [vmem(*shape) for shape in work_shapes(planes, rows, pairs)]


def local(b, beta, shift):
    fields = (b, beta, shift)
    a, c = pack_fine_x(fields)
    xs = swaps(a, c, "gx", 1)
    a, c, packed_c = call(
        pack_face_y, fields, [(FACE_Y_SIZE, 128)] * 2 + [(2, 8, 8, 128)], [vmem(16, 32, 128)]
    )
    ys = swaps(a, c, "gy", 1)
    inner = call(inner_kernel, (*fields, *ys), work_shapes(24, 32, 8), [vmem(26, 48, 128)])
    x_fine, packed, a, c = call(
        outer_kernel,
        (*fields, packed_c, *xs, *ys, *inner),
        [(16, 32, 128), (8, 8, 128)] + [(SECOND_Y_SIZE, 128)] * 2,
        level_scratch(24, 32) + work_scratch(24, 32, 8),
    )
    second = swaps(a, c, "gy", 1)
    *inner, ext_c = call(
        strip_kernel,
        (*fields, packed_c, *ys),
        work_shapes(24, 40, 8) + [(2, 8, 24, 128)],
        level_scratch(24, 40) + [vmem(16, 56, 128)],
    )
    x_edge, ext, near_a, near_b, far_a, far_b = call(
        edge_kernel,
        (*fields, *xs, *ys, packed, *second, *inner, ext_c),
        [(16, 8, 128), (3, 8, 24, 128)] + [(NEAR_X_SIZE, 128)] * 2 + [(FAR_X_SIZE, 128)] * 2,
        level_scratch(24, 40) + work_scratch(24, 40, 8),
    )
    near = swaps(near_a, near_b, "gx", 1, 1)
    far = swaps(far_a, far_b, "gx", 2)
    small = (5, 16, 128)
    inner = call(
        mid_kernel,
        (ext, *near),
        work_shapes(14, 40, 5) + [small] * 7,
        level_scratch(14, 40) + [vmem(7, 32, 128), vmem(*small), vmem(11, 40, 128)],
    )
    return tuple(call(
        coarse_kernel,
        (x_fine, x_edge, ext, *near, *far, *inner),
        [(16, 32, 128), (8, 16, 64)],
        level_scratch(14, 40) + work_scratch(14, 40, 5)
        + [vmem(*small), vmem(6, 32, 128), vmem(6, 32, 128), vmem(*small)]
        + [vmem(2, 16, 128), vmem(8, 32, 128), vmem(128, 128)],
    ))


def solution(mesh):
    placed = P("gx", "gy", None)
    return jax.shard_map(
        local, mesh=mesh, in_specs=(placed,) * 3, out_specs=(placed, placed), check_vma=False
    )
```

```python
import jax
import jax.numpy as jnp
from jax import lax
from jax.experimental import pallas as pl
from jax.experimental.pallas import tpu as pltpu
from jax.sharding import PartitionSpec as P

SWEEPS = 4
THETA, DELTA = 1.15, 0.85
SIGMA = THETA / DELTA
F32 = jnp.float32


def coefficients():
    rho, out = 1.0 / SIGMA, []
    for _ in range(SWEEPS - 1):
        new = 1.0 / (2.0 * SIGMA - rho)
        out.append((new * rho, 2.0 * new / DELTA))
        rho = new
    return out


def lanes(rows):
    return lax.broadcasted_iota(jnp.int32, (rows, 128), 1)


def roll(value, shift):
    return pltpu.roll(value, shift % 128, 1)


class StepSplit:
    def __init__(self, inner, outer, planes, level):
        self.inner, self.outer, self.planes, self.level, self.own = inner, outer, planes, level, set()

    def __getitem__(self, at):
        return (self.inner if at[0] in self.planes and at[0] not in self.own else self.outer)[at]

    def __setitem__(self, at, value):
        self.outer[at] = value
        if at[1].start >= self.level.bases[-1]:
            self.own.add(at[0])


class Level:
    def __init__(self, depth, own_planes, rows, own_rows, rep, folded=False, bases=(0,)):
        self.bases = bases
        self.depth, self.own, self.rep, self.folded = depth, own_planes, rep, folded
        self.planes = depth + own_planes // 2 if folded else own_planes + 2 * depth
        self.rows, self.first_row, self.own_rows = rows, (rows - own_rows) // 2, own_rows

    def cut(self, k):
        return k, self.planes - (0 if self.folded else k)

    def span(self, plane, reach):
        x = plane - self.depth
        far = max(0, -x) if self.folded else max(0, -x, x - self.own + 1)
        side = max(0, reach - far)
        lo = max(0, self.first_row - side) // 8 * 8
        hi = min(self.rows, -(-(self.first_row + self.own_rows + side) // 8) * 8)
        return lo, hi - lo

    def put(self, dst, i, at, value):
        dst[i, at, :] = value
        if self.folded and i == self.planes - 1:
            dst[i + 1, at, :] = swap_lanes(value)


def swap_lanes(value):
    return jnp.where(lanes(value.shape[0]) % 2 == 0, roll(value, -1), roll(value, 1))


def build(level, beta, rhs, shift, work, planes=None):
    wx, wy, wym, wz, wzm, diag, inv, rhs_n, start = work
    rep, last_span = level.rep, None
    planes = range(level.planes) if planes is None else planes
    for base, i in [(base, i) for base in level.bases for i in planes]:
        lo, n = level.span(i, level.depth)
        lo += base
        if (lo, n, i) != last_span:
            prev, cur = beta[i, pl.ds(8 + lo, n), :], beta[i + 1, pl.ds(8 + lo, n), :]
            wx_prev = prev + cur
            if i:
                wx[i - 1, pl.ds(lo, n), :] = wx_prev
            lane = lanes(n)
            first, last = lane < rep, lane >= 128 - rep
        last_span = (lo, n, i + 1)
        at = pl.ds(lo, n)
        nxt = beta[i + 2, pl.ds(8 + lo, n), :]
        wx_next = cur + nxt
        w_up = cur + beta[i + 1, pl.ds(9 + lo, n), :]
        w_down = cur + beta[i + 1, pl.ds(7 + lo, n), :]
        w_right = cur + jnp.where(last, 0.0, roll(cur, -rep))
        w_left = cur + jnp.where(first, 0.0, roll(cur, rep))
        d = shift(i, at) + (wx_prev + wx_next + w_up + w_down + w_right + w_left)
        iv = jnp.where(cur > 0.0, 1.0 / d, 0.0)
        wx[i, at, :] = wx_next
        wy[i, at, :] = w_up
        wym[i, at, :] = w_down
        wz[i, at, :] = jnp.where(last, 0.0, w_right)
        wzm[i, at, :] = jnp.where(first, 0.0, w_left)
        diag[i, at, :] = d
        inv[i, at, :] = iv
        if rhs is not None:
            begin(level, i, lo, n, rhs, iv, rhs_n, start)
        cur, wx_prev = nxt, wx_next


def begin(level, i, lo, n, rhs, iv, rhs_n, start):
    c = rhs(i, pl.ds(lo, n)) * iv
    rhs_n[i, pl.ds(lo, n), :] = c
    level.put(start, i, pl.ds(8 + lo, n), c * (1.0 / THETA))


def scaled_residual(level, src, planes, reach, work, emit):
    wx, wy, wym, wz, wzm, _, inv, rhs_n, _ = work
    rep, last_span = level.rep, None
    for base, i in [(base, i) for base in level.bases for i in planes]:
        lo, n = level.span(i, reach)
        lo += base
        at, dom = pl.ds(lo, n), pl.ds(8 + lo, n)
        if (lo, n, i) != last_span:
            prev, cur, wx_prev = src[i - 1, dom, :], src[i, dom, :], wx[i - 1, at, :]
        last_span = (lo, n, i + 1)
        nxt, wx_next = src[i + 1, dom, :], wx[i, at, :]
        t = wx_next * nxt + wx_prev * prev
        t = t + wy[i, at, :] * src[i, pl.ds(9 + lo, n), :] + wym[i, at, :] * src[i, pl.ds(7 + lo, n), :]
        t = t + wz[i, at, :] * roll(cur, -rep) + wzm[i, at, :] * roll(cur, rep)
        emit(i, lo, n, cur, rhs_n[i, at, :] + inv[i, at, :] * t - cur)
        prev, cur, wx_prev = cur, nxt, wx_next


def sweeps(level, work, fields, step, planes):
    for k, (a, g) in enumerate(coefficients()):

        def emit(i, lo, n, cur, e, a=a, g=g, k=k, dst=fields[k + 1]):
            before = cur if k == 0 else step[i, pl.ds(lo, n), :]
            d = a * before + g * e
            if k < SWEEPS - 2:
                step[i, pl.ds(lo, n), :] = d
            level.put(dst, i, pl.ds(8 + lo, n), cur + d)

        scaled_residual(level, fields[k], planes(k + 1), level.depth - k - 1, work, emit)
    return fields[-1]


def smooth(level, work, other, step):
    fields = (work[8], other) * 2
    return sweeps(level, work, fields, step, lambda k: range(*level.cut(k)))


class Split:
    def __init__(self, inner, outer, first, last):
        self.inner, self.outer, self.first, self.last = inner, outer, first, last

    def __getitem__(self, at):
        return (self.inner if self.first <= at[0] <= self.last else self.outer)[at]

    def __setitem__(self, at, value):
        if not self.first <= at[0] <= self.last:
            self.outer[at] = value


FINE = Level(4, 16, 32, 32, 1)
STRIP = Level(4, 16, 16, 16, 1, bases=(0, 24))
MID = Level(10, 8, 40, 16, 2, folded=True)
LOW = Level(3, 4, 16, 8, 4, folded=True)


def table(entries):
    rows, at = {}, 0
    for key, count in entries:
        rows[key] = (at, count)
        at += count
    return rows, -(-at // 8) * 8


FACE_Y, FACE_Y_SIZE = table([((f, x), 8) for x in range(16) for f in (0, 2)] + [((1, x), 9) for x in range(16)])

MID_Y = {0: 4, 1: 4, 2: 3}
HALO_X = [-1, -2, -3, -4, -5, 16, 17, 18, 19, 20]


def away(x):
    return -x if x < 0 else x - 15


SECOND_Y, SECOND_Y_SIZE = table(
    [((f, "mid", m), MID_Y[f]) for f in range(3) for m in range(8)]
    + [((f, "fine", x), 8 + (f == 1) - away(x)) for f in range(3) for x in HALO_X if away(x) < 5 + (f == 1)]
)


def side_rows(field, far):
    return -(-max(0, 10 + (field == 1) - far) // 2)


NEAR_X, NEAR_X_SIZE = table([((f, d), 8 + 2 * side_rows(f, d)) for f in range(3) for d in range(1, 9)])
FAR_X, FAR_X_SIZE = table([((f, d), 8 + 2 * side_rows(f, d)) for f in range(3) for d in range(9, 11 + (f == 1))])


def flag(condition):
    return jnp.where(condition, 1.0, 0.0).astype(F32)


def x_flags():
    i, n = lax.axis_index("gx"), lax.axis_size("gx")
    return {-2: flag(i > 1), -1: flag(i > 0), 1: flag(i < n - 1), 2: flag(i < n - 2)}


def y_flags():
    j, n = lax.axis_index("gy"), lax.axis_size("gy")
    return flag(j > 0), flag(j < n - 1)


def upward(axis, by, low=0):
    return lax.rem(lax.axis_index(axis) + low * by, 2 * by) >= by


def swaps(first, second, axis, by, low=0):
    axes = ("gx", "gy")
    size = [lax.axis_size(name) for name in axes]
    dim = axes.index(axis)
    orders = []
    for sign in (1, -1):
        pairs = []
        for i in range(size[0]):
            for j in range(size[1]):
                to = [i, j]
                to[dim] += sign * by if (to[dim] + low * by) % (2 * by) >= by else -sign * by
                if not 0 <= to[dim] < size[dim]:
                    to = [i, j]
                    to[1 - dim] ^= 1
                pairs.append((i * size[1] + j, to[0] * size[1] + to[1]))
        orders.append(pairs)
    return lax.ppermute(first, axes, orders[0]), lax.ppermute(second, axes, orders[1])


COUNTS = (4, 5, 4)
STARTS = (0, 4, 9)


def pack_fine_x(fields):
    ends = [f[:n] for f, n in zip(fields, COUNTS)] + [f[16 - n:] for f, n in zip(fields, COUNTS)]
    first, last = jnp.concatenate(ends[:3], axis=0), jnp.concatenate(ends[3:], axis=0)
    first, last = lax.optimization_barrier((first, last))
    up = upward("gx", 1)
    return jnp.where(up, last, first), jnp.where(up, first, last)


def fine_plane(field, x, own, in_a, in_b, up):
    if 0 <= x < 16:
        return own[field][x]
    i = STARTS[field] + (x + COUNTS[field] if x < 0 else x - 16)
    return jnp.where(up, in_b[i], in_a[i]) if x < 0 else jnp.where(up, in_a[i], in_b[i])


def pick(ref, rows, key):
    at, count = rows[key]
    return ref[pl.ds(at, count), :]


def put_both(out_a, out_b, rows, key, up, higher, lower):
    at, count = rows[key]
    out_a[pl.ds(at, count), :] = jnp.where(up, higher, lower)
    out_b[pl.ds(at, count), :] = jnp.where(up, lower, higher)


def pack_face_y(b, beta, shift, out_a, out_b):
    up = upward("gy", 1)
    for field, src in enumerate((b, beta, shift)):
        for x in range(16):
            n = FACE_Y[field, x][1]
            put_both(out_a, out_b, FACE_Y, (field, x), up, src[x, pl.ds(32 - n, n), :], src[x, pl.ds(0, n), :])


def y_sides(rows, key, in_a, in_b, up):
    a, b = pick(in_a, rows, key), pick(in_b, rows, key)
    return jnp.where(up, b, a), jnp.where(up, a, b)


def pack_pairs(pair, plane, start, count):
    even = lanes(count) % 2 == 0
    e = pair[plane, pl.ds(start, count, 4), :] + pair[plane, pl.ds(start + 1, count, 4), :]
    o = pair[plane, pl.ds(start + 2, count, 4), :] + pair[plane, pl.ds(start + 3, count, 4), :]
    return jnp.where(even, e + roll(e, -1), o + roll(o, 1)) * 0.125


def pair_residual(level, src, work, pair, first, planes):
    diag, held = work[5], {}

    def emit(i, lo, n, cur, e):
        r = e * diag[i, pl.ds(lo, n), :]
        if i % 2 == 0:
            held[0] = r
        else:
            pair[first + (i - 4) // 2, pl.ds(lo, n), :] = held[0] + r

    scaled_residual(level, src, planes, 0, work, emit)


def INNER(k):
    return range(5 + k, 19 - k)


def rest(k):
    return [i for i in range(k, 24 - k) if i not in INNER(k)]


def split_work(inner, outer, level):
    work = tuple(Split(i, o, 5, 18) for i, o in zip(inner[:9], outer[:9]))
    fields = [work[8]]
    for k in (1, 2, 3):
        fields.append(Split(inner[8 + k], outer[8 + k], INNER(k)[0], INNER(k)[-1]))
    step = StepSplit(inner[12], outer[12], INNER(1), level)
    return work, fields, step, Split(inner[13], outer[13], 3, 4)


def edge_rows(be, x, beta, ya_in, yb_in):
    (low, high), up = y_flags(), upward("gy", 1)
    lo, hi = y_sides(FACE_Y, (1, x), ya_in, yb_in, up)
    be[x + 5, 8:40, :] = beta[x] * 0.5
    be[x + 5, 7:8, :] = lo[8:9] * (0.5 * low)
    be[x + 5, 40:41, :] = hi[0:1] * (0.5 * high)


def inner_kernel(
    b, beta, shift, ya_in, yb_in,
    wx, wy, wym, wz, wzm, diag, inv, rhs_n, x0, x1, x2, x3, step, pair, packed, be, sums,
):
    for field, src in ((1, beta), (2, shift)):
        for m in range(8):
            at = 8 * field + m - 8
            sums[at] = src[2 * m] + src[2 * m + 1]
            packed[field - 1, m] = pack_pairs(sums, at, 0, 8)
    for x in range(16):
        edge_rows(be, x, beta, ya_in, yb_in)
    work = (wx, wy, wym, wz, wzm, diag, inv, rhs_n, x0)
    build(FINE, be, lambda i, at: b[i - 4], lambda i, at: shift[i - 4], work, INNER(0))
    sweeps(FINE, work, (x0, x1, x2, x3), step, INNER)
    pair_residual(FINE, x3, work, pair, 0, range(10, 14))


def outer_kernel(
    b, beta, shift, coarse, xa_in, xb_in, ya_in, yb_in, *refs,
):
    inner, refs = refs[:14], refs[14:]
    (x_out, packed, out_a, out_b, be, bb, ss), outer = refs[:7], refs[7:]
    near, up_x, up_y = x_flags(), upward("gx", 1), upward("gy", 1)
    own = (b, beta, shift)
    for x in [*range(-5, 2), *range(14, 21)]:
        if 0 <= x < 16:
            edge_rows(be, x, beta, ya_in, yb_in)
            continue
        p = fine_plane(1, x, own, xa_in, xb_in, up_x)
        be[x + 5, 8:40, :] = p * (0.5 * (near[-1] if x < 0 else near[1]))
        at = SECOND_Y[1, "fine", x][1]
        put_both(out_a, out_b, SECOND_Y, (1, "fine", x), up_y, p[32 - at:32], p[0:at])
    for field, dst in ((0, bb), (2, ss)):
        for x in [*range(-4, 0), *range(16, 20)]:
            p = fine_plane(field, x, own, xa_in, xb_in, up_x)
            dst[x + 4] = p
            at = SECOND_Y[field, "fine", x][1]
            put_both(out_a, out_b, SECOND_Y, (field, "fine", x), up_y, p[32 - at:32], p[0:at])
    work, fields, step, pair = split_work(inner, outer, FINE)

    def plane_of(src, halo):
        return lambda i, at: src[i - 4] if 4 <= i < 20 else halo[i]

    build(FINE, be, plane_of(b, bb), plane_of(shift, ss), work, rest(0))
    x = sweeps(FINE, work, fields, step, rest)
    pair_residual(FINE, x, work, pair, 0, [*range(4, 10), *range(14, 20)])
    for m in range(8):
        packed[m] = pack_pairs(pair, m, 0, 8)
        put_both(out_a, out_b, SECOND_Y, (0, "mid", m), up_y, packed[m, 3:7, :], packed[m, 1:5, :])
        for field in (1, 2):
            n = MID_Y[field]
            higher, lower = coarse[field - 1, m, 6 - n:6, :], coarse[field - 1, m, 2:2 + n, :]
            put_both(out_a, out_b, SECOND_Y, (field, "mid", m), up_y, higher, lower)
    for i in range(16):
        x_out[i] = x[i + 4, pl.ds(8, 32), :]


def strip_kernel(
    b, beta, shift, packed, ya_in, yb_in,
    wx, wy, wym, wz, wzm, diag, inv, rhs_n, x0, x1, x2, x3, step, pair, ext, be, bb, ss, sums,
):
    (low, high), up_y = y_flags(), upward("gy", 1)
    for x in range(16):
        lo, hi = y_sides(FACE_Y, (1, x), ya_in, yb_in, up_y)
        be[x + 5, 16:25, :] = beta[x, 0:9, :] * 0.5
        be[x + 5, 31:40, :] = beta[x, 23:32, :] * 0.5
        be[x + 5, 7:16, :] = lo * (0.5 * low)
        be[x + 5, 40:49, :] = hi * (0.5 * high)
    for field, src, dst in ((0, b, bb), (2, shift, ss)):
        for x in range(16):
            lo, hi = y_sides(FACE_Y, (field, x), ya_in, yb_in, up_y)
            dst[x + 4, 8:16, :] = src[x, 0:8, :]
            dst[x + 4, 24:32, :] = src[x, 24:32, :]
            dst[x + 4, 0:8, :] = lo
            dst[x + 4, 32:40, :] = hi
    work = (wx, wy, wym, wz, wzm, diag, inv, rhs_n, x0)
    build(STRIP, be, lambda i, at: bb[i, at, :], lambda i, at: ss[i, at, :], work, INNER(0))
    sweeps(STRIP, work, (x0, x1, x2, x3), step, INNER)
    pair_residual(STRIP, x3, work, pair, 0, range(10, 14))

    for m in range(8):
        sums[m] = (be[2 * m + 5] + be[2 * m + 6]) * 2.0
        sums[m + 8, 0:40, :] = ss[2 * m + 4] + ss[2 * m + 5]
        for field, plane, at in ((1, m, 8), (2, m + 8, 0)):
            dst = ext.at[field - 1, m]
            dst[4:6, :] = pack_pairs(sums, plane, at, 2)
            dst[6:14, :] = packed[field - 1, m]
            dst[14:16, :] = pack_pairs(sums, plane, at + 32, 2)


def edge_kernel(
    b, beta, shift, xa_in, xb_in, ya_in, yb_in, packed, ya2, yb2, *refs,
):
    inner, ext_c, refs = refs[:14], refs[14], refs[15:]
    (x_out, ext, near_a, near_b, far_a, far_b, be, bb, ss), outer = refs[:9], refs[9:]
    near, (low, high) = x_flags(), y_flags()
    up_x, up_y = upward("gx", 1), upward("gy", 1)
    own = (b, beta, shift)

    def sides(field, x):
        if 0 <= x < 16:
            return y_sides(FACE_Y, (field, x), ya_in, yb_in, up_y)
        return y_sides(SECOND_Y, (field, "fine", x), ya2, yb2, up_y)

    for x in [*range(-5, 2), *range(14, 21)]:
        p = fine_plane(1, x, own, xa_in, xb_in, up_x)
        lo, hi = sides(1, x)
        n = lo.shape[0]
        f = 0.5 if 0 <= x < 16 else 0.5 * (near[-1] if x < 0 else near[1])
        p = p * f
        be[x + 5, 16:25, :] = p[0:9]
        be[x + 5, 31:40, :] = p[23:32]
        be[x + 5, pl.ds(16 - n, n), :] = lo * (low * f)
        be[x + 5, pl.ds(40, n), :] = hi * (high * f)
    for field, dst in ((0, bb), (2, ss)):
        for x in [*range(-4, 1), *range(15, 20)]:
            p = fine_plane(field, x, own, xa_in, xb_in, up_x)
            lo, hi = sides(field, x)
            n = lo.shape[0]
            dst[x + 4, 8:16, :] = p[0:8]
            dst[x + 4, 24:32, :] = p[24:32]
            dst[x + 4, pl.ds(8 - n, n), :] = lo
            dst[x + 4, pl.ds(32, n), :] = hi
    work, fields, step, pair = split_work(inner, outer, STRIP)
    build(STRIP, be, lambda i, at: bb[i, at, :], lambda i, at: ss[i, at, :], work, rest(0))
    x = sweeps(STRIP, work, fields, step, rest)
    pair_residual(STRIP, x, work, pair, 0, [*range(4, 10), *range(14, 20)])
    for m in range(8):
        lo, hi = y_sides(SECOND_Y, (0, "mid", m), ya2, yb2, up_y)
        ext[0, m, 1:5, :] = lo
        ext[0, m, 5:7, :] = pack_pairs(pair, m, 4, 2)
        ext[0, m, 7:13, :] = packed[m, 1:7, :]
        ext[0, m, 13:15, :] = pack_pairs(pair, m, 28, 2)
        ext[0, m, 15:19, :] = hi
        for field in (1, 2):
            n = MID_Y[field]
            lo, hi = y_sides(SECOND_Y, (field, "mid", m), ya2, yb2, up_y)
            ext[field, m, 4 - n:4, :] = lo * low if field == 1 else lo
            ext[field, m, 4:16, :] = ext_c[field - 1, m, 4:16, :]
            ext[field, m, 16:16 + n, :] = hi * high if field == 1 else hi
    up2 = upward("gx", 2)
    for rows, up, a, c, first in ((NEAR_X, upward("gx", 1, 1), near_a, near_b, 1), (FAR_X, up2, far_a, far_b, 9)):
        for field, d in rows:
            n = side_rows(field, d)
            at = pl.ds(6 - n, 8 + 2 * n)
            higher, lower = ext[field, 8 - d + (first - 1), at, :], ext[field, d - first, at, :]
            put_both(a, c, rows, (field, d), up, higher, lower)
    for i in range(16):
        x_out[i, 0:4, :] = x[i + 4, pl.ds(16, 4), :]
        x_out[i, 4:8, :] = x[i + 4, pl.ds(36, 4), :]


def spread(dst, plane, start, a, b):
    n = a.shape[0]
    even = lanes(n) % 2 == 0
    dst[plane, pl.ds(start, n, 2), :] = jnp.where(even, a, roll(b, 1))
    dst[plane, pl.ds(start + 1, n, 2), :] = jnp.where(even, roll(a, -1), b)


def gather(field, d, ext, near, far=None):
    if d <= 0:
        n = side_rows(field, 0)
        at = pl.ds(6 - n, 8 + 2 * n)
        lower, higher = ext[field, -d, at, :], ext[field, 7 + d, at, :]
        return (lower * 0.125, higher * 0.125) if field == 1 else (lower, higher)
    hop, rows, (a, c) = (1, NEAR_X, near) if d <= 8 else (2, FAR_X, far)
    u = upward("gx", hop, 2 - hop)
    a, c = pick(a, rows, (field, d)), pick(c, rows, (field, d))
    lower, higher = jnp.where(u, c, a), jnp.where(u, a, c)
    if field == 1:
        flags = x_flags()
        return lower * (0.125 * flags[-hop]), higher * (0.125 * flags[hop])
    return lower, higher


def unpack_mid(field, planes, dst, first, reach, *messages):
    for i in planes:
        a, b = gather(field, reach - i, *messages)
        spread(dst, i, first - (a.shape[0] - 8), a, b)


def down_sample(pair, plane):
    low_pair = lanes(16) % 4 < 2
    s = pair[plane, pl.ds(4, 16, 2), :] + pair[plane, pl.ds(5, 16, 2), :]
    return (s + jnp.where(low_pair, roll(s, -2), roll(s, 2))) * 0.125


def pair_mid_residual(src, work, pair, planes):
    diag, held = work[5], {}

    def emit(i, lo, n, cur, e):
        r = e * diag[i, pl.ds(lo, n), :]
        if i % 2 == 0:
            held[0] = lo, n, r
        else:
            lo0, n0, r0 = held[0]
            at, end = max(lo, lo0), min(lo + n, lo0 + n0)
            total = r0[at - lo0:end - lo0] + r[at - lo:end - lo]
            pair[(i - 4) // 2, pl.ds(at, end - at), :] = total

    scaled_residual(MID, src, planes, 6, work, emit)


def MID_INNER(k):
    return range(3 + k, 14)


def mid_kernel(
    ext, near_a, near_b,
    wx, wy, wym, wz, wzm, diag, inv, rhs_n, x0, x1, x2, x3, step, pair,
    wx2, wy2, wym2, wz2, wzm2, diag2, inv2,
    be, bb, ss, be2, ss2, sums,
):
    messages = ext, (near_a, near_b)
    unpack_mid(1, range(3, 15), be, 20, 11, *messages)
    unpack_mid(0, range(3, 14), bb, 12, 10, *messages)
    unpack_mid(2, range(3, 14), ss, 12, 10, *messages)
    be[15, pl.ds(8, 40), :] = swap_lanes(be[14, pl.ds(8, 40), :])
    work = (wx, wy, wym, wz, wzm, diag, inv, rhs_n, x0)
    build(MID, be, lambda i, at: bb[i, at, :], lambda i, at: ss[i, at, :], work, MID_INNER(0))
    sweeps(MID, work, (x0, x1, x2, x3), step, MID_INNER)
    pair_mid_residual(x3, work, pair, range(8, 14))

    for m in range(6):
        sums[m] = be[2 * m + 3, pl.ds(8, 40), :] + be[2 * m + 4, pl.ds(8, 40), :]
    for m in range(5):
        sums[6 + m] = ss[2 * m + 4] + ss[2 * m + 5]
    for m in range(6):
        be2[m, 8:24, :] = down_sample(sums, m) * 0.25
    be2[6, 8:24, :] = swap_lanes(be2[5, 8:24, :])
    for m in range(5):
        ss2[m] = down_sample(sums, 6 + m)
    work2 = (wx2, wy2, wym2, wz2, wzm2, diag2, inv2, None, None)
    build(LOW, be2, None, lambda i, at: ss2[i, at, :], work2)


def coarse_kernel(
    x_fine, x_edge, ext, near_a, near_b, far_a, far_b,
    i_wx, i_wy, i_wym, i_wz, i_wzm, i_diag, i_inv, i_rhs_n, i_x0, i_x1, i_x2, i_x3, i_step, i_pair,
    wx2, wy2, wym2, wz2, wzm2, diag2, inv2,
    out, mid_out,
    be, bb, ss, wx, wy, wym, wz, wzm, diag, inv, rhs_n, x0, x1, x2, x3, step, pair,
    rhs_n2, xa2, xb2, step2, rep_mid, rep_fine, mids,
):
    messages = ext, (near_a, near_b), (far_a, far_b)
    unpack_mid(1, range(5), be, 20, 11, *messages)
    unpack_mid(0, range(3), bb, 12, 10, *messages)
    unpack_mid(2, range(3), ss, 12, 10, *messages)
    inner = (i_wx, i_wy, i_wym, i_wz, i_wzm, i_diag, i_inv, i_rhs_n, i_x0)
    outer = (wx, wy, wym, wz, wzm, diag, inv, rhs_n, x0)
    work = tuple(Split(i, o, 3, 14) for i, o in zip(inner, outer))
    fields = [work[8]] + [Split(i, o, 3 + k, 14) for k, i, o in ((1, i_x1, x1), (2, i_x2, x2), (3, i_x3, x3))]

    def rest(k):
        return range(k, 3 + k)

    build(MID, be, lambda i, at: bb[i, at, :], lambda i, at: ss[i, at, :], work, rest(0))
    x1 = sweeps(MID, work, fields, StepSplit(i_step, step, MID_INNER(1), MID), rest)
    pair = Split(i_pair, pair, 2, 4)
    pair_mid_residual(x1, work, pair, range(4, 8))
    for i in range(LOW.planes):
        lo, n = LOW.span(i, LOW.depth)
        begin(LOW, i, lo, n, lambda i, at: down_sample(pair, i), inv2[i], rhs_n2, xa2)
    work2 = (wx2, wy2, wym2, wz2, wzm2, diag2, inv2, rhs_n2, xa2)
    x2 = smooth(LOW, work2, xb2, step2)

    for m in range(2):
        low_x = x2[m + 3, pl.ds(12, 8), :]
        rep_mid[m, pl.ds(0, 8, 2), :] = low_x
        rep_mid[m, pl.ds(1, 8, 2), :] = low_x
    even = lanes(16) % 2 == 0
    for m in range(4):
        both = x1[m + 10, pl.ds(20, 16), :] + rep_mid[m // 2]
        for x, mid in (
            (m, jnp.where(even, both, roll(both, 1))),
            (7 - m, jnp.where(even, roll(both, -1), both)),
        ):
            mids[pl.ds(16 * x, 16), :] = mid
            rep_fine[x, pl.ds(0, 16, 2), :] = mid
            rep_fine[x, pl.ds(1, 16, 2), :] = mid
    for i in range(16):
        out[i, 4:28, :] = x_fine[i, 4:28, :] + rep_fine[i // 2, 4:28, :]
        out[i, 0:4, :] = x_edge[i, 0:4, :] + rep_fine[i // 2, 0:4, :]
        out[i, 28:32, :] = x_edge[i, 4:8, :] + rep_fine[i // 2, 28:32, :]
    row = lax.broadcasted_iota(jnp.int32, (128, 64), 0)
    col = lax.broadcasted_iota(jnp.int32, (128, 64), 1)
    even_lanes = jnp.where(row == 2 * col, 1.0, 0.0).astype(F32)
    compact = jnp.dot(mids[...], even_lanes, precision=lax.Precision.HIGHEST, preferred_element_type=F32)
    for m in range(8):
        mid_out[m] = compact[16 * m:16 * m + 16]


def vmem(*shape):
    return pltpu.VMEM(shape, F32)


def call(kernel, ins, outs, scratch=(), limit=24 * 2**20, space=pltpu.VMEM):
    return pl.pallas_call(
        kernel,
        out_shape=[jax.ShapeDtypeStruct(s, F32) for s in outs],
        in_specs=[pl.BlockSpec(memory_space=space)] * len(ins),
        out_specs=[pl.BlockSpec(memory_space=pltpu.VMEM)] * len(outs),
        scratch_shapes=list(scratch),
        compiler_params=pltpu.CompilerParams(vmem_limit_bytes=limit),
    )(*ins)


def work_shapes(planes, rows, pairs):
    flat, tall = (planes, rows, 128), (planes + 1, rows + 16, 128)
    return [flat] * 8 + [tall] * 4 + [flat, (pairs, rows, 128)]


def level_scratch(planes, rows):
    return [vmem(planes + 2, rows + 16, 128)] + [vmem(planes, rows, 128)] * 2


def work_scratch(planes, rows, pairs):
    return [vmem(*shape) for shape in work_shapes(planes, rows, pairs)]


def local(b, beta, shift):
    fields = (b, beta, shift)
    a, c = pack_fine_x(fields)
    xs = swaps(a, c, "gx", 1)
    a, c = call(pack_face_y, fields, [(FACE_Y_SIZE, 128)] * 2)
    ys = swaps(a, c, "gy", 1)
    *inner, packed_c = call(
        inner_kernel,
        (*fields, *ys),
        work_shapes(24, 32, 8) + [(2, 8, 8, 128)],
        [vmem(26, 48, 128), vmem(16, 32, 128)],
    )
    x_fine, packed, a, c = call(
        outer_kernel,
        (*fields, packed_c, *xs, *ys, *inner),
        [(16, 32, 128), (8, 8, 128)] + [(SECOND_Y_SIZE, 128)] * 2,
        level_scratch(24, 32) + work_scratch(24, 32, 8),
    )
    second = swaps(a, c, "gy", 1)
    *inner, ext_c = call(
        strip_kernel,
        (*fields, packed_c, *ys),
        work_shapes(24, 40, 8) + [(2, 8, 24, 128)],
        level_scratch(24, 40) + [vmem(16, 56, 128)],
    )
    x_edge, ext, near_a, near_b, far_a, far_b = call(
        edge_kernel,
        (*fields, *xs, *ys, packed, *second, *inner, ext_c),
        [(16, 8, 128), (3, 8, 24, 128)] + [(NEAR_X_SIZE, 128)] * 2 + [(FAR_X_SIZE, 128)] * 2,
        level_scratch(24, 40) + work_scratch(24, 40, 8),
    )
    near = swaps(near_a, near_b, "gx", 1, 1)
    far = swaps(far_a, far_b, "gx", 2)
    small = (5, 16, 128)
    inner = call(
        mid_kernel,
        (ext, *near),
        work_shapes(14, 40, 5) + [small] * 7,
        level_scratch(14, 40) + [vmem(7, 32, 128), vmem(*small), vmem(11, 40, 128)],
    )
    return tuple(call(
        coarse_kernel,
        (x_fine, x_edge, ext, *near, *far, *inner),
        [(16, 32, 128), (8, 16, 64)],
        level_scratch(14, 40) + work_scratch(14, 40, 5)
        + [vmem(*small), vmem(6, 32, 128), vmem(6, 32, 128), vmem(*small)]
        + [vmem(2, 16, 128), vmem(8, 32, 128), vmem(128, 128)],
    ))


def solution(mesh):
    placed = P("gx", "gy", None)
    return jax.shard_map(
        local, mesh=mesh, in_specs=(placed,) * 3, out_specs=(placed, placed), check_vma=False
    )
```

```python
import jax
import jax.numpy as jnp
from jax import lax
from jax.experimental import pallas as pl
from jax.experimental.pallas import tpu as pltpu
from jax.sharding import PartitionSpec as P

SWEEPS = 4
THETA, DELTA = 1.15, 0.85
SIGMA = THETA / DELTA
F32 = jnp.float32


def coefficients():
    rho, out = 1.0 / SIGMA, []
    for _ in range(SWEEPS - 1):
        new = 1.0 / (2.0 * SIGMA - rho)
        out.append((new * rho, 2.0 * new / DELTA))
        rho = new
    return out


def lanes(rows):
    return lax.broadcasted_iota(jnp.int32, (rows, 128), 1)


def roll(value, shift):
    return pltpu.roll(value, shift % 128, 1)


class StepSplit:
    def __init__(self, inner, outer, planes, level):
        self.inner, self.outer, self.planes, self.level, self.own = inner, outer, planes, level, set()

    def __getitem__(self, at):
        return (self.inner if at[0] in self.planes and at[0] not in self.own else self.outer)[at]

    def __setitem__(self, at, value):
        self.outer[at] = value
        if at[1].start >= self.level.bases[-1]:
            self.own.add(at[0])


class Level:
    def __init__(self, depth, own_planes, rows, own_rows, rep, folded=False, bases=(0,)):
        self.bases = bases
        self.depth, self.own, self.rep, self.folded = depth, own_planes, rep, folded
        self.planes = depth + own_planes // 2 if folded else own_planes + 2 * depth
        self.rows, self.first_row, self.own_rows = rows, (rows - own_rows) // 2, own_rows

    def cut(self, k):
        return k, self.planes - (0 if self.folded else k)

    def span(self, plane, reach):
        x = plane - self.depth
        far = max(0, -x) if self.folded else max(0, -x, x - self.own + 1)
        side = max(0, reach - far)
        lo = max(0, self.first_row - side) // 8 * 8
        hi = min(self.rows, -(-(self.first_row + self.own_rows + side) // 8) * 8)
        return lo, hi - lo

    def put(self, dst, i, at, value):
        dst[i, at, :] = value
        if self.folded and i == self.planes - 1:
            dst[i + 1, at, :] = swap_lanes(value)


def swap_lanes(value):
    return jnp.where(lanes(value.shape[0]) % 2 == 0, roll(value, -1), roll(value, 1))


def build(level, beta, rhs, shift, work, planes=None):
    wx, wy, wym, wz, wzm, diag, inv, rhs_n, start = work
    rep, last_span = level.rep, None
    planes = range(level.planes) if planes is None else planes
    for base, i in [(base, i) for base in level.bases for i in planes]:
        lo, n = level.span(i, level.depth)
        lo += base
        if (lo, n, i) != last_span:
            prev, cur = beta[i, pl.ds(8 + lo, n), :], beta[i + 1, pl.ds(8 + lo, n), :]
            wx_prev = prev + cur
            if i:
                wx[i - 1, pl.ds(lo, n), :] = wx_prev
            lane = lanes(n)
            first, last = lane < rep, lane >= 128 - rep
        last_span = (lo, n, i + 1)
        at = pl.ds(lo, n)
        nxt = beta[i + 2, pl.ds(8 + lo, n), :]
        wx_next = cur + nxt
        w_up = cur + beta[i + 1, pl.ds(9 + lo, n), :]
        w_down = cur + beta[i + 1, pl.ds(7 + lo, n), :]
        w_right = cur + jnp.where(last, 0.0, roll(cur, -rep))
        w_left = cur + jnp.where(first, 0.0, roll(cur, rep))
        d = shift(i, at) + (wx_prev + wx_next + w_up + w_down + w_right + w_left)
        iv = jnp.where(cur > 0.0, 1.0 / d, 0.0)
        wx[i, at, :] = wx_next
        wy[i, at, :] = w_up
        wym[i, at, :] = w_down
        wz[i, at, :] = jnp.where(last, 0.0, w_right)
        diag[i, at, :] = d
        inv[i, at, :] = iv
        if rhs is not None:
            begin(level, i, lo, n, rhs, iv, rhs_n, start)
        cur, wx_prev = nxt, wx_next


def begin(level, i, lo, n, rhs, iv, rhs_n, start):
    c = rhs(i, pl.ds(lo, n)) * iv
    rhs_n[i, pl.ds(lo, n), :] = c
    level.put(start, i, pl.ds(8 + lo, n), c * (1.0 / THETA))


def scaled_residual(level, src, planes, reach, work, emit):
    wx, wy, wym, wz, wzm, _, inv, rhs_n, _ = work
    rep, last_span = level.rep, None
    for base, i in [(base, i) for base in level.bases for i in planes]:
        lo, n = level.span(i, reach)
        lo += base
        at, dom = pl.ds(lo, n), pl.ds(8 + lo, n)
        if (lo, n, i) != last_span:
            prev, cur, wx_prev = src[i - 1, dom, :], src[i, dom, :], wx[i - 1, at, :]
        last_span = (lo, n, i + 1)
        nxt, wx_next = src[i + 1, dom, :], wx[i, at, :]
        t = wx_next * nxt + wx_prev * prev
        t = t + wy[i, at, :] * src[i, pl.ds(9 + lo, n), :] + wym[i, at, :] * src[i, pl.ds(7 + lo, n), :]
        t = t + wz[i, at, :] * roll(cur, -rep) + roll(wz[i, at, :] * cur, rep)
        emit(i, lo, n, cur, rhs_n[i, at, :] + inv[i, at, :] * t - cur)
        prev, cur, wx_prev = cur, nxt, wx_next


def sweeps(level, work, fields, step, planes):
    for k, (a, g) in enumerate(coefficients()):

        def emit(i, lo, n, cur, e, a=a, g=g, k=k, dst=fields[k + 1]):
            before = cur if k == 0 else step[i, pl.ds(lo, n), :]
            d = a * before + g * e
            if k < SWEEPS - 2:
                step[i, pl.ds(lo, n), :] = d
            level.put(dst, i, pl.ds(8 + lo, n), cur + d)

        scaled_residual(level, fields[k], planes(k + 1), level.depth - k - 1, work, emit)
    return fields[-1]


def smooth(level, work, other, step):
    fields = (work[8], other) * 2
    return sweeps(level, work, fields, step, lambda k: range(*level.cut(k)))


class Split:
    def __init__(self, inner, outer, first, last):
        self.inner, self.outer, self.first, self.last = inner, outer, first, last

    def __getitem__(self, at):
        return (self.inner if self.first <= at[0] <= self.last else self.outer)[at]

    def __setitem__(self, at, value):
        if not self.first <= at[0] <= self.last:
            self.outer[at] = value


FINE = Level(4, 16, 32, 32, 1)
STRIP = Level(4, 16, 16, 16, 1, bases=(0, 24))
MID = Level(10, 8, 40, 16, 2, folded=True)
LOW = Level(3, 4, 16, 8, 4, folded=True)


def table(entries):
    rows, at = {}, 0
    for key, count in entries:
        rows[key] = (at, count)
        at += count
    return rows, -(-at // 8) * 8


FACE_Y, FACE_Y_SIZE = table([((f, x), 8) for x in range(16) for f in (0, 2)] + [((1, x), 9) for x in range(16)])

MID_Y = {0: 4, 1: 4, 2: 3}
HALO_X = [-1, -2, -3, -4, -5, 16, 17, 18, 19, 20]


def away(x):
    return -x if x < 0 else x - 15


SECOND_Y, SECOND_Y_SIZE = table(
    [((f, "mid", m), MID_Y[f]) for f in range(3) for m in range(8)]
    + [((f, "fine", x), 8 + (f == 1) - away(x)) for f in range(3) for x in HALO_X if away(x) < 5 + (f == 1)]
)


def side_rows(field, far):
    return -(-max(0, 10 + (field == 1) - far) // 2)


NEAR_X, NEAR_X_SIZE = table([((f, d), 8 + 2 * side_rows(f, d)) for f in range(3) for d in range(1, 9)])
FAR_X, FAR_X_SIZE = table([((f, d), 8 + 2 * side_rows(f, d)) for f in range(3) for d in range(9, 11 + (f == 1))])


def flag(condition):
    return jnp.where(condition, 1.0, 0.0).astype(F32)


def x_flags():
    i, n = lax.axis_index("gx"), lax.axis_size("gx")
    return {-2: flag(i > 1), -1: flag(i > 0), 1: flag(i < n - 1), 2: flag(i < n - 2)}


def y_flags():
    j, n = lax.axis_index("gy"), lax.axis_size("gy")
    return flag(j > 0), flag(j < n - 1)


def upward(axis, by, low=0):
    return lax.rem(lax.axis_index(axis) + low * by, 2 * by) >= by


def swaps(first, second, axis, by, low=0):
    axes = ("gx", "gy")
    size = [lax.axis_size(name) for name in axes]
    dim = axes.index(axis)
    orders = []
    for sign in (1, -1):
        pairs = []
        for i in range(size[0]):
            for j in range(size[1]):
                to = [i, j]
                to[dim] += sign * by if (to[dim] + low * by) % (2 * by) >= by else -sign * by
                if not 0 <= to[dim] < size[dim]:
                    to = [i, j]
                    to[1 - dim] ^= 1
                pairs.append((i * size[1] + j, to[0] * size[1] + to[1]))
        orders.append(pairs)
    return lax.ppermute(first, axes, orders[0]), lax.ppermute(second, axes, orders[1])


COUNTS = (4, 5, 4)
STARTS = (0, 4, 9)


def pack_fine_x(fields):
    ends = [f[:n] for f, n in zip(fields, COUNTS)] + [f[16 - n:] for f, n in zip(fields, COUNTS)]
    first, last = jnp.concatenate(ends[:3], axis=0), jnp.concatenate(ends[3:], axis=0)
    first, last = lax.optimization_barrier((first, last))
    up = upward("gx", 1)
    return jnp.where(up, last, first), jnp.where(up, first, last)


def fine_plane(field, x, own, in_a, in_b, up):
    if 0 <= x < 16:
        return own[field][x]
    i = STARTS[field] + (x + COUNTS[field] if x < 0 else x - 16)
    return jnp.where(up, in_b[i], in_a[i]) if x < 0 else jnp.where(up, in_a[i], in_b[i])


def pick(ref, rows, key):
    at, count = rows[key]
    return ref[pl.ds(at, count), :]


def put_both(out_a, out_b, rows, key, up, higher, lower):
    at, count = rows[key]
    out_a[pl.ds(at, count), :] = jnp.where(up, higher, lower)
    out_b[pl.ds(at, count), :] = jnp.where(up, lower, higher)


def pack_face_y(b, beta, shift, out_a, out_b):
    up = upward("gy", 1)
    for field, src in enumerate((b, beta, shift)):
        for x in range(16):
            n = FACE_Y[field, x][1]
            put_both(out_a, out_b, FACE_Y, (field, x), up, src[x, pl.ds(32 - n, n), :], src[x, pl.ds(0, n), :])


def y_sides(rows, key, in_a, in_b, up):
    a, b = pick(in_a, rows, key), pick(in_b, rows, key)
    return jnp.where(up, b, a), jnp.where(up, a, b)


def pack_pairs(pair, plane, start, count):
    even = lanes(count) % 2 == 0
    e = pair[plane, pl.ds(start, count, 4), :] + pair[plane, pl.ds(start + 1, count, 4), :]
    o = pair[plane, pl.ds(start + 2, count, 4), :] + pair[plane, pl.ds(start + 3, count, 4), :]
    return jnp.where(even, e + roll(e, -1), o + roll(o, 1)) * 0.125


def pair_residual(level, src, work, pair, first, planes):
    diag, held = work[5], {}

    def emit(i, lo, n, cur, e):
        r = e * diag[i, pl.ds(lo, n), :]
        if i % 2 == 0:
            held[0] = r
        else:
            pair[first + (i - 4) // 2, pl.ds(lo, n), :] = held[0] + r

    scaled_residual(level, src, planes, 0, work, emit)


def INNER(k):
    return range(5 + k, 19 - k)


def rest(k):
    return [i for i in range(k, 24 - k) if i not in INNER(k)]


def split_work(inner, outer, level):
    work = tuple(Split(i, o, 5, 18) for i, o in zip(inner[:9], outer[:9]))
    fields = [work[8]]
    for k in (1, 2, 3):
        fields.append(Split(inner[8 + k], outer[8 + k], INNER(k)[0], INNER(k)[-1]))
    step = StepSplit(inner[12], outer[12], INNER(1), level)
    return work, fields, step, Split(inner[13], outer[13], 3, 4)


def edge_rows(be, x, beta, ya_in, yb_in):
    (low, high), up = y_flags(), upward("gy", 1)
    lo, hi = y_sides(FACE_Y, (1, x), ya_in, yb_in, up)
    be[x + 5, 8:40, :] = beta[x] * 0.5
    be[x + 5, 7:8, :] = lo[8:9] * (0.5 * low)
    be[x + 5, 40:41, :] = hi[0:1] * (0.5 * high)


def inner_kernel(
    b, beta, shift, ya_in, yb_in,
    wx, wy, wym, wz, wzm, diag, inv, rhs_n, x0, x1, x2, x3, step, pair, packed, be, sums,
):
    for field, src in ((1, beta), (2, shift)):
        for m in range(8):
            at = 8 * field + m - 8
            sums[at] = src[2 * m] + src[2 * m + 1]
            packed[field - 1, m] = pack_pairs(sums, at, 0, 8)
    for x in range(16):
        edge_rows(be, x, beta, ya_in, yb_in)
    work = (wx, wy, wym, wz, wzm, diag, inv, rhs_n, x0)
    build(FINE, be, lambda i, at: b[i - 4], lambda i, at: shift[i - 4], work, INNER(0))
    sweeps(FINE, work, (x0, x1, x2, x3), step, INNER)
    pair_residual(FINE, x3, work, pair, 0, range(10, 14))


def outer_kernel(
    b, beta, shift, coarse, xa_in, xb_in, ya_in, yb_in, *refs,
):
    inner, refs = refs[:14], refs[14:]
    (x_out, packed, out_a, out_b, be, bb, ss), outer = refs[:7], refs[7:]
    near, up_x, up_y = x_flags(), upward("gx", 1), upward("gy", 1)
    own = (b, beta, shift)
    for x in [*range(-5, 2), *range(14, 21)]:
        if 0 <= x < 16:
            edge_rows(be, x, beta, ya_in, yb_in)
            continue
        p = fine_plane(1, x, own, xa_in, xb_in, up_x)
        be[x + 5, 8:40, :] = p * (0.5 * (near[-1] if x < 0 else near[1]))
        at = SECOND_Y[1, "fine", x][1]
        put_both(out_a, out_b, SECOND_Y, (1, "fine", x), up_y, p[32 - at:32], p[0:at])
    for field, dst in ((0, bb), (2, ss)):
        for x in [*range(-4, 0), *range(16, 20)]:
            p = fine_plane(field, x, own, xa_in, xb_in, up_x)
            dst[x + 4] = p
            at = SECOND_Y[field, "fine", x][1]
            put_both(out_a, out_b, SECOND_Y, (field, "fine", x), up_y, p[32 - at:32], p[0:at])
    work, fields, step, pair = split_work(inner, outer, FINE)

    def plane_of(src, halo):
        return lambda i, at: src[i - 4] if 4 <= i < 20 else halo[i]

    build(FINE, be, plane_of(b, bb), plane_of(shift, ss), work, rest(0))
    x = sweeps(FINE, work, fields, step, rest)
    pair_residual(FINE, x, work, pair, 0, [*range(4, 10), *range(14, 20)])
    for m in range(8):
        packed[m] = pack_pairs(pair, m, 0, 8)
        put_both(out_a, out_b, SECOND_Y, (0, "mid", m), up_y, packed[m, 3:7, :], packed[m, 1:5, :])
        for field in (1, 2):
            n = MID_Y[field]
            higher, lower = coarse[field - 1, m, 6 - n:6, :], coarse[field - 1, m, 2:2 + n, :]
            put_both(out_a, out_b, SECOND_Y, (field, "mid", m), up_y, higher, lower)
    for i in range(16):
        x_out[i] = x[i + 4, pl.ds(8, 32), :]


def strip_kernel(
    b, beta, shift, packed, ya_in, yb_in,
    wx, wy, wym, wz, wzm, diag, inv, rhs_n, x0, x1, x2, x3, step, pair, ext, be, bb, ss, sums,
):
    (low, high), up_y = y_flags(), upward("gy", 1)
    for x in range(16):
        lo, hi = y_sides(FACE_Y, (1, x), ya_in, yb_in, up_y)
        be[x + 5, 16:25, :] = beta[x, 0:9, :] * 0.5
        be[x + 5, 31:40, :] = beta[x, 23:32, :] * 0.5
        be[x + 5, 7:16, :] = lo * (0.5 * low)
        be[x + 5, 40:49, :] = hi * (0.5 * high)
    for field, src, dst in ((0, b, bb), (2, shift, ss)):
        for x in range(16):
            lo, hi = y_sides(FACE_Y, (field, x), ya_in, yb_in, up_y)
            dst[x + 4, 8:16, :] = src[x, 0:8, :]
            dst[x + 4, 24:32, :] = src[x, 24:32, :]
            dst[x + 4, 0:8, :] = lo
            dst[x + 4, 32:40, :] = hi
    work = (wx, wy, wym, wz, wzm, diag, inv, rhs_n, x0)
    build(STRIP, be, lambda i, at: bb[i, at, :], lambda i, at: ss[i, at, :], work, INNER(0))
    sweeps(STRIP, work, (x0, x1, x2, x3), step, INNER)
    pair_residual(STRIP, x3, work, pair, 0, range(10, 14))

    for m in range(8):
        sums[m] = (be[2 * m + 5] + be[2 * m + 6]) * 2.0
        sums[m + 8, 0:40, :] = ss[2 * m + 4] + ss[2 * m + 5]
        for field, plane, at in ((1, m, 8), (2, m + 8, 0)):
            dst = ext.at[field - 1, m]
            dst[4:6, :] = pack_pairs(sums, plane, at, 2)
            dst[6:14, :] = packed[field - 1, m]
            dst[14:16, :] = pack_pairs(sums, plane, at + 32, 2)


def edge_kernel(
    b, beta, shift, xa_in, xb_in, ya_in, yb_in, packed, ya2, yb2, *refs,
):
    inner, ext_c, refs = refs[:14], refs[14], refs[15:]
    (x_out, ext, near_a, near_b, far_a, far_b, be, bb, ss), outer = refs[:9], refs[9:]
    near, (low, high) = x_flags(), y_flags()
    up_x, up_y = upward("gx", 1), upward("gy", 1)
    own = (b, beta, shift)

    def sides(field, x):
        if 0 <= x < 16:
            return y_sides(FACE_Y, (field, x), ya_in, yb_in, up_y)
        return y_sides(SECOND_Y, (field, "fine", x), ya2, yb2, up_y)

    for x in [*range(-5, 2), *range(14, 21)]:
        p = fine_plane(1, x, own, xa_in, xb_in, up_x)
        lo, hi = sides(1, x)
        n = lo.shape[0]
        f = 0.5 if 0 <= x < 16 else 0.5 * (near[-1] if x < 0 else near[1])
        p = p * f
        be[x + 5, 16:25, :] = p[0:9]
        be[x + 5, 31:40, :] = p[23:32]
        be[x + 5, pl.ds(16 - n, n), :] = lo * (low * f)
        be[x + 5, pl.ds(40, n), :] = hi * (high * f)
    for field, dst in ((0, bb), (2, ss)):
        for x in [*range(-4, 1), *range(15, 20)]:
            p = fine_plane(field, x, own, xa_in, xb_in, up_x)
            lo, hi = sides(field, x)
            n = lo.shape[0]
            dst[x + 4, 8:16, :] = p[0:8]
            dst[x + 4, 24:32, :] = p[24:32]
            dst[x + 4, pl.ds(8 - n, n), :] = lo
            dst[x + 4, pl.ds(32, n), :] = hi
    work, fields, step, pair = split_work(inner, outer, STRIP)
    build(STRIP, be, lambda i, at: bb[i, at, :], lambda i, at: ss[i, at, :], work, rest(0))
    x = sweeps(STRIP, work, fields, step, rest)
    pair_residual(STRIP, x, work, pair, 0, [*range(4, 10), *range(14, 20)])
    for m in range(8):
        lo, hi = y_sides(SECOND_Y, (0, "mid", m), ya2, yb2, up_y)
        ext[0, m, 1:5, :] = lo
        ext[0, m, 5:7, :] = pack_pairs(pair, m, 4, 2)
        ext[0, m, 7:13, :] = packed[m, 1:7, :]
        ext[0, m, 13:15, :] = pack_pairs(pair, m, 28, 2)
        ext[0, m, 15:19, :] = hi
        for field in (1, 2):
            n = MID_Y[field]
            lo, hi = y_sides(SECOND_Y, (field, "mid", m), ya2, yb2, up_y)
            ext[field, m, 4 - n:4, :] = lo * low if field == 1 else lo
            ext[field, m, 4:16, :] = ext_c[field - 1, m, 4:16, :]
            ext[field, m, 16:16 + n, :] = hi * high if field == 1 else hi
    up2 = upward("gx", 2)
    for rows, up, a, c, first in ((NEAR_X, upward("gx", 1, 1), near_a, near_b, 1), (FAR_X, up2, far_a, far_b, 9)):
        for field, d in rows:
            n = side_rows(field, d)
            at = pl.ds(6 - n, 8 + 2 * n)
            higher, lower = ext[field, 8 - d + (first - 1), at, :], ext[field, d - first, at, :]
            put_both(a, c, rows, (field, d), up, higher, lower)
    for i in range(16):
        x_out[i, 0:4, :] = x[i + 4, pl.ds(16, 4), :]
        x_out[i, 4:8, :] = x[i + 4, pl.ds(36, 4), :]


def spread(dst, plane, start, a, b):
    n = a.shape[0]
    even = lanes(n) % 2 == 0
    dst[plane, pl.ds(start, n, 2), :] = jnp.where(even, a, roll(b, 1))
    dst[plane, pl.ds(start + 1, n, 2), :] = jnp.where(even, roll(a, -1), b)


def gather(field, d, ext, near, far=None):
    if d <= 0:
        n = side_rows(field, 0)
        at = pl.ds(6 - n, 8 + 2 * n)
        lower, higher = ext[field, -d, at, :], ext[field, 7 + d, at, :]
        return (lower * 0.125, higher * 0.125) if field == 1 else (lower, higher)
    hop, rows, (a, c) = (1, NEAR_X, near) if d <= 8 else (2, FAR_X, far)
    u = upward("gx", hop, 2 - hop)
    a, c = pick(a, rows, (field, d)), pick(c, rows, (field, d))
    lower, higher = jnp.where(u, c, a), jnp.where(u, a, c)
    if field == 1:
        flags = x_flags()
        return lower * (0.125 * flags[-hop]), higher * (0.125 * flags[hop])
    return lower, higher


def unpack_mid(field, planes, dst, first, reach, *messages):
    for i in planes:
        a, b = gather(field, reach - i, *messages)
        spread(dst, i, first - (a.shape[0] - 8), a, b)


def down_sample(pair, plane):
    low_pair = lanes(16) % 4 < 2
    s = pair[plane, pl.ds(4, 16, 2), :] + pair[plane, pl.ds(5, 16, 2), :]
    return (s + jnp.where(low_pair, roll(s, -2), roll(s, 2))) * 0.125


def pair_mid_residual(src, work, pair, planes):
    diag, held = work[5], {}

    def emit(i, lo, n, cur, e):
        r = e * diag[i, pl.ds(lo, n), :]
        if i % 2 == 0:
            held[0] = lo, n, r
        else:
            lo0, n0, r0 = held[0]
            at, end = max(lo, lo0), min(lo + n, lo0 + n0)
            total = r0[at - lo0:end - lo0] + r[at - lo:end - lo]
            pair[(i - 4) // 2, pl.ds(at, end - at), :] = total

    scaled_residual(MID, src, planes, 6, work, emit)


def MID_INNER(k):
    return range(3 + k, 14)


def mid_kernel(
    ext, near_a, near_b,
    wx, wy, wym, wz, wzm, diag, inv, rhs_n, x0, x1, x2, x3, step, pair,
    wx2, wy2, wym2, wz2, wzm2, diag2, inv2,
    be, bb, ss, be2, ss2, sums,
):
    messages = ext, (near_a, near_b)
    unpack_mid(1, range(3, 15), be, 20, 11, *messages)
    unpack_mid(0, range(3, 14), bb, 12, 10, *messages)
    unpack_mid(2, range(3, 14), ss, 12, 10, *messages)
    be[15, pl.ds(8, 40), :] = swap_lanes(be[14, pl.ds(8, 40), :])
    work = (wx, wy, wym, wz, wzm, diag, inv, rhs_n, x0)
    build(MID, be, lambda i, at: bb[i, at, :], lambda i, at: ss[i, at, :], work, MID_INNER(0))
    sweeps(MID, work, (x0, x1, x2, x3), step, MID_INNER)
    pair_mid_residual(x3, work, pair, range(8, 14))

    for m in range(6):
        sums[m] = be[2 * m + 3, pl.ds(8, 40), :] + be[2 * m + 4, pl.ds(8, 40), :]
    for m in range(5):
        sums[6 + m] = ss[2 * m + 4] + ss[2 * m + 5]
    for m in range(6):
        be2[m, 8:24, :] = down_sample(sums, m) * 0.25
    be2[6, 8:24, :] = swap_lanes(be2[5, 8:24, :])
    for m in range(5):
        ss2[m] = down_sample(sums, 6 + m)
    work2 = (wx2, wy2, wym2, wz2, wzm2, diag2, inv2, None, None)
    build(LOW, be2, None, lambda i, at: ss2[i, at, :], work2)


def coarse_kernel(
    x_fine, x_edge, ext, near_a, near_b, far_a, far_b,
    i_wx, i_wy, i_wym, i_wz, i_wzm, i_diag, i_inv, i_rhs_n, i_x0, i_x1, i_x2, i_x3, i_step, i_pair,
    wx2, wy2, wym2, wz2, wzm2, diag2, inv2,
    out, mid_out,
    be, bb, ss, wx, wy, wym, wz, wzm, diag, inv, rhs_n, x0, x1, x2, x3, step, pair,
    rhs_n2, xa2, xb2, step2, rep_mid, rep_fine, mids,
):
    messages = ext, (near_a, near_b), (far_a, far_b)
    unpack_mid(1, range(5), be, 20, 11, *messages)
    unpack_mid(0, range(3), bb, 12, 10, *messages)
    unpack_mid(2, range(3), ss, 12, 10, *messages)
    inner = (i_wx, i_wy, i_wym, i_wz, i_wzm, i_diag, i_inv, i_rhs_n, i_x0)
    outer = (wx, wy, wym, wz, wzm, diag, inv, rhs_n, x0)
    work = tuple(Split(i, o, 3, 14) for i, o in zip(inner, outer))
    fields = [work[8]] + [Split(i, o, 3 + k, 14) for k, i, o in ((1, i_x1, x1), (2, i_x2, x2), (3, i_x3, x3))]

    def rest(k):
        return range(k, 3 + k)

    build(MID, be, lambda i, at: bb[i, at, :], lambda i, at: ss[i, at, :], work, rest(0))
    x1 = sweeps(MID, work, fields, StepSplit(i_step, step, MID_INNER(1), MID), rest)
    pair = Split(i_pair, pair, 2, 4)
    pair_mid_residual(x1, work, pair, range(4, 8))
    for i in range(LOW.planes):
        lo, n = LOW.span(i, LOW.depth)
        begin(LOW, i, lo, n, lambda i, at: down_sample(pair, i), inv2[i], rhs_n2, xa2)
    work2 = (wx2, wy2, wym2, wz2, wzm2, diag2, inv2, rhs_n2, xa2)
    x2 = smooth(LOW, work2, xb2, step2)

    for m in range(2):
        low_x = x2[m + 3, pl.ds(12, 8), :]
        rep_mid[m, pl.ds(0, 8, 2), :] = low_x
        rep_mid[m, pl.ds(1, 8, 2), :] = low_x
    even = lanes(16) % 2 == 0
    for m in range(4):
        both = x1[m + 10, pl.ds(20, 16), :] + rep_mid[m // 2]
        for x, mid in (
            (m, jnp.where(even, both, roll(both, 1))),
            (7 - m, jnp.where(even, roll(both, -1), both)),
        ):
            mids[pl.ds(16 * x, 16), :] = mid
            rep_fine[x, pl.ds(0, 16, 2), :] = mid
            rep_fine[x, pl.ds(1, 16, 2), :] = mid
    for i in range(16):
        out[i, 4:28, :] = x_fine[i, 4:28, :] + rep_fine[i // 2, 4:28, :]
        out[i, 0:4, :] = x_edge[i, 0:4, :] + rep_fine[i // 2, 0:4, :]
        out[i, 28:32, :] = x_edge[i, 4:8, :] + rep_fine[i // 2, 28:32, :]
    row = lax.broadcasted_iota(jnp.int32, (128, 64), 0)
    col = lax.broadcasted_iota(jnp.int32, (128, 64), 1)
    even_lanes = jnp.where(row == 2 * col, 1.0, 0.0).astype(F32)
    compact = jnp.dot(mids[...], even_lanes, precision=lax.Precision.HIGHEST, preferred_element_type=F32)
    for m in range(8):
        mid_out[m] = compact[16 * m:16 * m + 16]


def vmem(*shape):
    return pltpu.VMEM(shape, F32)


def call(kernel, ins, outs, scratch=(), limit=24 * 2**20, space=pltpu.VMEM):
    return pl.pallas_call(
        kernel,
        out_shape=[jax.ShapeDtypeStruct(s, F32) for s in outs],
        in_specs=[pl.BlockSpec(memory_space=space)] * len(ins),
        out_specs=[pl.BlockSpec(memory_space=pltpu.VMEM)] * len(outs),
        scratch_shapes=list(scratch),
        compiler_params=pltpu.CompilerParams(vmem_limit_bytes=limit),
    )(*ins)


def work_shapes(planes, rows, pairs):
    flat, tall = (planes, rows, 128), (planes + 1, rows + 16, 128)
    return [flat] * 8 + [tall] * 4 + [flat, (pairs, rows, 128)]


def level_scratch(planes, rows):
    return [vmem(planes + 2, rows + 16, 128)] + [vmem(planes, rows, 128)] * 2


def work_scratch(planes, rows, pairs):
    return [vmem(*shape) for shape in work_shapes(planes, rows, pairs)]


def local(b, beta, shift):
    fields = (b, beta, shift)
    a, c = pack_fine_x(fields)
    xs = swaps(a, c, "gx", 1)
    a, c = call(pack_face_y, fields, [(FACE_Y_SIZE, 128)] * 2)
    ys = swaps(a, c, "gy", 1)
    *inner, packed_c = call(
        inner_kernel,
        (*fields, *ys),
        work_shapes(24, 32, 8) + [(2, 8, 8, 128)],
        [vmem(26, 48, 128), vmem(16, 32, 128)],
    )
    x_fine, packed, a, c = call(
        outer_kernel,
        (*fields, packed_c, *xs, *ys, *inner),
        [(16, 32, 128), (8, 8, 128)] + [(SECOND_Y_SIZE, 128)] * 2,
        level_scratch(24, 32) + work_scratch(24, 32, 8),
    )
    second = swaps(a, c, "gy", 1)
    *inner, ext_c = call(
        strip_kernel,
        (*fields, packed_c, *ys),
        work_shapes(24, 40, 8) + [(2, 8, 24, 128)],
        level_scratch(24, 40) + [vmem(16, 56, 128)],
    )
    x_edge, ext, near_a, near_b, far_a, far_b = call(
        edge_kernel,
        (*fields, *xs, *ys, packed, *second, *inner, ext_c),
        [(16, 8, 128), (3, 8, 24, 128)] + [(NEAR_X_SIZE, 128)] * 2 + [(FAR_X_SIZE, 128)] * 2,
        level_scratch(24, 40) + work_scratch(24, 40, 8),
    )
    near = swaps(near_a, near_b, "gx", 1, 1)
    far = swaps(far_a, far_b, "gx", 2)
    small = (5, 16, 128)
    inner = call(
        mid_kernel,
        (ext, *near),
        work_shapes(14, 40, 5) + [small] * 7,
        level_scratch(14, 40) + [vmem(7, 32, 128), vmem(*small), vmem(11, 40, 128)],
    )
    return tuple(call(
        coarse_kernel,
        (x_fine, x_edge, ext, *near, *far, *inner),
        [(16, 32, 128), (8, 16, 64)],
        level_scratch(14, 40) + work_scratch(14, 40, 5)
        + [vmem(*small), vmem(6, 32, 128), vmem(6, 32, 128), vmem(*small)]
        + [vmem(2, 16, 128), vmem(8, 32, 128), vmem(128, 128)],
    ))


def solution(mesh):
    placed = P("gx", "gy", None)
    return jax.shard_map(
        local, mesh=mesh, in_specs=(placed,) * 3, out_specs=(placed, placed), check_vma=False
    )
```
